256 devices in a mesh: blk: 64 (over z, y, core), grp: 4 (over x).
Axes of the slice: x: 4, y: 4, z: 8, core: 2. Of those that a mesh axis runs over, the one named last changes fastest.
Arguments:
- source_points: bfloat16 [524288, 64], P(('blk', 'grp')), may hold values from -6 to 6
- target_points: bfloat16 [524288, 64], P('blk'), may hold values from -6 to 6
- source_logw: float32 [524288], P(('blk', 'grp')), may hold values from -1 to 1
- target_logw: float32 [524288], P('blk'), may hold values from -1 to 1
- source_feats: bfloat16 [524288, 128], P(('blk', 'grp')), may hold values from -4 to 4
- target_feats: bfloat16 [524288, 128], P('blk'), may hold values from -4 to 4
- pair_owner: int32 [2048, 7], P(('blk', 'grp')), may hold values from 0 to 63, all different within a row; in each aligned block of 8 rows (0 to 7, 8 to 15, ...) at most 2 rows name the same one
- pair_slot: int32 [2048, 7], P(('blk', 'grp')), may hold values from 0 to 31
Outputs:
- moved_source: bfloat16 [524288, 128], P(('blk', 'grp'))
- moved_target: bfloat16 [524288, 128], P(('blk', 'grp'))
The draws below stay inside these ranges and needn't reach their ends.
Inputs may be any that keep to these rules, and one draw needn't show every extreme that they name: `pair_owner`: each row names 7 different owners. Within the rows of one device no owner is named more than 2 times, a bound that some block reaches.
All inputs are finite; a program needn't handle non-finite values.
Results may differ from the reference program's by a relative error of at most 0.0057.
Values may be sent and summed in bfloat16 or wider, within the bound.
A program may use at most 128 MiB of HBM per device.

```python
import math
import jax
import jax.numpy as jnp
import numpy as np
from jax import lax

WIDTH = 64
FEATURES = 128
BLOCK = 256
NEIGHBOURS = 7
ROUNDS = 2
DEV_BLOCKS = 8
OWNER_BLOCKS = 32
BLOCKS = 2048
POINTS = 524288
CAPACITY = 2
N_BLK = 64


def draw_source_points(key, part):
    key = jax.random.fold_in(key, 11)
    first = jax.random.fold_in(key, 0)
    values = jax.random.normal(first, (POINTS, WIDTH), jnp.float32)
    return jnp.clip(values, -4.0, 4.0).astype(jnp.bfloat16)


def draw_target_points(key, part):
    key = jax.random.fold_in(key, 12)
    first = jax.random.fold_in(key, 0)
    values = jax.random.normal(first, (POINTS, WIDTH), jnp.float32)
    return jnp.clip(values, -4.0, 4.0).astype(jnp.bfloat16)


def place_ends(values, own_key, low, largest):
    extent = values.shape
    place = [jax.random.randint(jax.random.fold_in(own_key, axis), (), 0, extent[axis]) for axis in range(len(extent))]
    values = values.at[tuple(place)].set(low)
    longest = extent.index(max(extent))
    place[longest] = (place[longest] + 1) % extent[longest]
    return values.at[tuple(place)].set(largest)


def levels(key, dims, cuts, least, largest):
    def one(dim, blocks):
        draws = jax.random.uniform(jax.random.fold_in(jax.random.fold_in(key, 6), dim), (blocks,), jnp.float32, least / len(cuts), largest / len(cuts))
        return jnp.repeat(jnp.exp(draws), dims[dim] // blocks).reshape((-1,) + (1,) * (len(dims) - dim - 1))

    loudness = one(*cuts[0])
    for cut in cuts[1:]:
        loudness = loudness * one(*cut)
    return loudness


def assign_block(key, own, number, rows, number_of, top, bound, skew):
    order = jax.random.permutation(key, number_of)
    heavy_load, usual = load_shares(number_of, rows * top, bound, skew, True), load_shares(number_of, rows * top, bound, skew, False)
    places = jnp.arange(number_of)

    def named(tallies, offset_by):
        used = int((tallies > 0).sum())
        fixed = max(1, used // 4)
        shifted = fixed + (places - fixed + offset_by * (used - fixed)) % max(1, number_of - fixed)
        return jnp.zeros((number_of,), jnp.int32).at[order[jnp.where(places < fixed, places, shifted)]].set(jnp.asarray(tallies, jnp.int32))

    tallies = jnp.where(number % 4 == 0, named(heavy_load, number // 4), named(usual, number - number // 4 - 1))
    mixed = jax.random.permutation(jax.random.fold_in(own, 3), number_of)
    giver, receiver = mixed[0:number_of // 2 * 2:2], mixed[1:number_of // 2 * 2:2]
    slack = jnp.minimum(tallies[giver] - 1, bound - tallies[receiver]) // 2
    slack = jnp.where((giver == order[0]) | (receiver == order[0]) | (tallies[receiver] == 0), 0, jnp.maximum(slack, 0))
    shifted = jax.random.randint(jax.random.fold_in(own, 4), (number_of // 2,), 0, 1 << 20) % (slack + 1)
    tallies = tallies.at[giver].add(-shifted).at[receiver].add(shifted)
    labels = jnp.searchsorted(jnp.cumsum(tallies), jnp.arange(rows * top), side="right").astype(jnp.int32)
    table = labels.reshape(top, rows).T
    table = table[jax.random.permutation(jax.random.fold_in(own, 1), rows)]
    offset_by = jax.random.randint(jax.random.fold_in(own, 2), (rows, 1), 0, top)
    return jnp.take_along_axis(table, (jnp.arange(top)[None, :] + offset_by) % top, axis=1)


def load_shares(count, total, reach, slope, full):
    weights = [(1 << 20) // math.isqrt(rank ** slope) + 1 for rank in range(1, count + 1)]
    largest = reach if full else min(reach, max(-(-total // count), total * weights[0] // sum(weights)))
    least = 1 if total - largest >= count - 1 else 0
    given, rest = [largest] + [least] * (count - 1), total - largest - least * (count - 1)
    while rest > 0:
        candidates = [i for i in range(1, count) if given[i] < largest] or [i for i in range(1, count) if given[i] < reach]
        whole, budget = sum([weights[i] for i in candidates]), rest
        for i in candidates:
            more = min(reach - given[i], max(1, budget * weights[i] // whole), rest)
            given[i] = given[i] + more
            rest = rest - more
    return np.array(given)


def scatter_about(rng, shape, spread, bound, cuts=(), kind=jnp.bfloat16):
    array = spread * jax.random.normal(rng, shape, jnp.float32)
    if cuts:
        array = array * levels(rng, shape, cuts, -0.22, 0.18)
    return jnp.clip(array, -bound, bound).astype(kind)


def setup_inputs(seed: int = 0) -> dict:
    streams_of = jax.random.split(jax.random.key(seed), 9)
    source_points = draw_source_points(jax.random.fold_in(streams_of[8], 71), 0)
    target_points = draw_target_points(jax.random.fold_in(streams_of[8], 71), 0)
    source_logw = jnp.clip(jax.random.uniform(streams_of[2], (POINTS,), jnp.float32, -1.0, 1.0) * levels(streams_of[2], (POINTS,), ((0, 256),), -0.4, 0.0), -1.0, 1.0)
    target_logw = jnp.clip(jax.random.uniform(streams_of[3], (POINTS,), jnp.float32, -1.0, 1.0) * levels(streams_of[3], (POINTS,), ((0, 64),), -0.4, 0.0), -1.0, 1.0)
    source_feats = scatter_about(streams_of[4], (POINTS, FEATURES), 1.0, 4.0, ((0, 256),))
    target_feats = scatter_about(streams_of[5], (POINTS, FEATURES), 1.0, 4.0, ((0, 64),))
    pair_owner_keys = jax.random.split(jax.random.fold_in(streams_of[6], 1), BLOCKS // DEV_BLOCKS)
    pair_owner_turns = jax.random.permutation(jax.random.fold_in(streams_of[6], 3), BLOCKS // DEV_BLOCKS)
    pair_owner = jax.vmap(lambda own, number: assign_block(jax.random.fold_in(streams_of[6], 2), own, number, DEV_BLOCKS, N_BLK, NEIGHBOURS, CAPACITY, 1))(pair_owner_keys, pair_owner_turns).reshape((BLOCKS, NEIGHBOURS))
    pair_slot = place_ends(jax.random.randint(streams_of[7], (BLOCKS, NEIGHBOURS), 0, OWNER_BLOCKS), jax.random.fold_in(streams_of[7], 1), 0, OWNER_BLOCKS - 1).astype(jnp.int32)
    return dict(source_points=source_points, target_points=target_points, source_logw=source_logw, target_logw=target_logw, source_feats=source_feats, target_feats=target_feats, pair_owner=pair_owner, pair_slot=pair_slot)


smoothing = 0.05
lowest = -1e30


def block_cost(points, targets):
    points_f = points.astype(jnp.float32)
    targets_f = targets.astype(jnp.float32)
    inner = jnp.einsum("id,kjd->kij", points_f, targets_f, precision=lax.Precision.HIGHEST)
    left = jnp.sum(points_f * points_f, axis=1)
    right = jnp.sum(targets_f * targets_f, axis=2)
    return (left[None, :, None] + right[:, None, :] - 2.0 * inner) * (0.5 / WIDTH)


def grouped(function, arrays):
    shaped = tuple(a.reshape((a.shape[0] // 4, 4) + a.shape[1:]) for a in arrays)

    def apply(batch):
        return jax.vmap(function)(*batch)

    result = lax.map(apply, shaped)
    return jax.tree.map(lambda r: r.reshape((r.shape[0] * r.shape[1],) + r.shape[2:]), result)


def reference(source_points, target_points, source_logw, target_logw, source_feats, target_feats, pair_owner, pair_slot):
    own_index = jnp.arange(BLOCKS, dtype=jnp.int32)[:, None]
    targets_of = jnp.concatenate([own_index, (pair_owner * OWNER_BLOCKS + pair_slot).astype(jnp.int32)], axis=1)
    flat_targets = targets_of.reshape(-1)
    sources = source_points.reshape(BLOCKS, BLOCK, WIDTH)
    targets = target_points.reshape(BLOCKS, BLOCK, WIDTH)
    source_weights = source_logw.reshape(BLOCKS, BLOCK)
    target_weights = target_logw.reshape(BLOCKS, BLOCK)
    source_blocks_feats = source_feats.reshape(BLOCKS, BLOCK, FEATURES)
    target_blocks_feats = target_feats.reshape(BLOCKS, BLOCK, FEATURES)
    target_pot = jnp.zeros((BLOCKS, BLOCK), jnp.float32)
    source_pot = jnp.zeros((BLOCKS, BLOCK), jnp.float32)
    column_lse = jnp.zeros((BLOCKS, BLOCK), jnp.float32)
    for sweep in range(ROUNDS):
        def row_pass(points, weights, chosen):
            cost = block_cost(points, targets[chosen])
            scores = (target_pot[chosen][:, None, :] - cost) / smoothing
            peak = jnp.max(scores, axis=(0, 2))
            total = jnp.sum(jnp.exp(scores - peak[None, :, None]), axis=(0, 2))
            return smoothing * (weights - peak - jnp.log(total))

        source_pot = grouped(row_pass, (sources, source_weights, targets_of))

        def column_pass(points, chosen, potential_row):
            cost = block_cost(points, targets[chosen])
            scores = (potential_row[None, :, None] - cost) / smoothing
            peak = jnp.max(scores, axis=1)
            total = jnp.sum(jnp.exp(scores - peak[:, None, :]), axis=1)
            return peak, total

        peaks, totals = grouped(column_pass, (sources, targets_of, source_pot))
        flat_peaks = peaks.reshape(-1, BLOCK)
        flat_totals = totals.reshape(-1, BLOCK)
        upper = jnp.full((BLOCKS, BLOCK), lowest, jnp.float32).at[flat_targets].max(flat_peaks)
        summed = jnp.zeros((BLOCKS, BLOCK), jnp.float32).at[flat_targets].add(flat_totals * jnp.exp(flat_peaks - upper[flat_targets]))
        column_lse = upper + jnp.log(summed)
        target_pot = smoothing * (target_weights - column_lse)

    def carry_pass(moved, inputs):
        points, chosen, potential_row, own_feats = inputs
        cost = block_cost(points, targets[chosen])
        scores = (target_pot[chosen][:, None, :] - cost) / smoothing
        peak = jnp.max(scores, axis=(0, 2))
        expo = jnp.exp(scores - peak[None, :, None])
        denom = jnp.sum(expo, axis=(0, 2))
        weights = expo.astype(jnp.bfloat16).astype(jnp.float32)
        mixed = jnp.einsum("kij,kjf->if", weights, target_blocks_feats[chosen].astype(jnp.float32), precision=lax.Precision.HIGHEST)
        moved_row = (mixed / denom[:, None]).astype(jnp.bfloat16)
        column_weights = jnp.exp((potential_row[None, :, None] - cost) / smoothing - column_lse[chosen][:, None, :])
        column_weights = column_weights.astype(jnp.bfloat16).astype(jnp.float32)
        parts = jnp.einsum("kij,if->kjf", column_weights, own_feats.astype(jnp.float32), precision=lax.Precision.HIGHEST)
        parts = parts.astype(jnp.bfloat16).astype(jnp.float32)
        moved = moved.at[chosen].add(parts)
        return moved, moved_row

    start = jnp.zeros((BLOCKS, BLOCK, FEATURES), jnp.float32)
    moved, rows = lax.scan(carry_pass, start, (sources, targets_of, source_pot, source_blocks_feats))
    moved_source = rows.reshape(POINTS, FEATURES)
    moved_target = moved.reshape(POINTS, FEATURES).astype(jnp.bfloat16)
    return moved_source, moved_target
```

```python
import functools
import jax
import jax.numpy as jnp
from jax import lax
from jax.experimental import pallas as pl
from jax.experimental.pallas import tpu as pltpu
from jax.sharding import PartitionSpec as P

ROUNDS = 2
LOWEST = -1e30
CROSS = 0.3125
SQUARE = 0.15625
MESH = pl.DeviceIdType.MESH
MIB = 2**20
f32 = jnp.float32
bf16 = jnp.bfloat16


def params(cid=None, vmem=48):
    if cid is None:
        return pltpu.CompilerParams(vmem_limit_bytes=vmem * MIB)
    return pltpu.CompilerParams(
        collective_id=cid, has_side_effects=True, vmem_limit_bytes=vmem * MIB
    )


def nt(a, b):
    return lax.dot_general(a, b, (((1,), (1,)), ((), ())), preferred_element_type=f32)


def tn(a, b):
    return lax.dot_general(a, b, (((0,), (0,)), ((), ())), preferred_element_type=f32)


def nn(a, b):
    return jnp.dot(a, b, preferred_element_type=f32)


def greet(axes):
    bar = pltpu.get_barrier_semaphore()
    total = 0
    for name in axes:
        n = lax.axis_size(name)
        me = lax.axis_index(name)

        @pl.loop(1, n)
        def _(s):
            pl.semaphore_signal(
                bar, inc=1, device_id={name: lax.rem(me + s, n)}, device_id_type=MESH
            )

        total += n - 1
    pl.semaphore_wait(bar, total)


def send_all(src, dst, send, recv, axis):
    n = lax.axis_size(axis)
    me = lax.axis_index(axis)

    @pl.loop(1, n)
    def _(s):
        to = lax.rem(me + s, n)
        pltpu.make_async_remote_copy(
            src_ref=src(to),
            dst_ref=dst,
            send_sem=send,
            recv_sem=recv,
            device_id={axis: to},
            device_id_type=MESH,
        ).start()


def wait_all(whole, send, recv, axis):
    n = lax.axis_size(axis)
    part = whole.at[pl.ds(0, n - 1)]
    copy = pltpu.make_async_remote_copy(
        src_ref=part,
        dst_ref=part,
        send_sem=send,
        recv_sem=recv,
        device_id={axis: lax.rem(lax.axis_index(axis) + 1, n)},
        device_id_type=MESH,
    )
    copy.wait_send()
    copy.wait_recv()


def exchange_kernel(x_ref, o_ref, send, recv, own):
    me = lax.axis_index("blk")
    greet(["blk"])
    mine = pltpu.make_async_copy(x_ref.at[me], o_ref.at[me], own)
    mine.start()
    send_all(lambda to: x_ref.at[to], o_ref.at[me], send, recv, "blk")
    mine.wait()
    wait_all(o_ref, send, recv, "blk")


def exchange(x, cid):
    return pl.pallas_call(
        exchange_kernel,
        out_shape=jax.ShapeDtypeStruct(x.shape, x.dtype),
        in_specs=[pl.BlockSpec(memory_space=pltpu.VMEM)],
        out_specs=pl.BlockSpec(memory_space=pltpu.VMEM),
        scratch_shapes=[pltpu.SemaphoreType.DMA] * 3,
        compiler_params=params(cid),
    )(x)


def reshard_kernel(x_ref, o_ref, send, recv, own, send_x, recv_x):
    me = lax.axis_index("blk")
    plane = lax.axis_index("grp")
    greet(["blk", "grp"])
    mine = pltpu.make_async_copy(x_ref.at[me], o_ref.at[plane, me], own)
    mine.start()
    send_all(lambda to: x_ref.at[to], o_ref.at[plane, me], send, recv, "blk")
    mine.wait()
    wait_all(x_ref, send, recv, "blk")
    send_all(lambda to: o_ref.at[plane], o_ref.at[plane], send_x, recv_x, "grp")
    wait_all(o_ref, send_x, recv_x, "grp")


def reshard(x, cid):
    planes = lax.axis_size("grp")
    return pl.pallas_call(
        reshard_kernel,
        out_shape=jax.ShapeDtypeStruct((planes,) + x.shape, x.dtype),
        in_specs=[pl.BlockSpec(memory_space=pltpu.VMEM)],
        out_specs=pl.BlockSpec(memory_space=pltpu.VMEM),
        scratch_shapes=[pltpu.SemaphoreType.DMA] * 5,
        compiler_params=params(cid),
    )(x)


def spread_kernel(x_ref, o_ref, send, recv, own):
    plane = lax.axis_index("grp")
    greet(["grp"])
    mine = pltpu.make_async_copy(x_ref.at[plane], o_ref.at[plane], own)
    mine.start()
    send_all(lambda to: x_ref.at[to], o_ref.at[plane], send, recv, "grp")
    mine.wait()
    wait_all(o_ref, send, recv, "grp")


def spread(x, cid):
    return pl.pallas_call(
        spread_kernel,
        out_shape=jax.ShapeDtypeStruct(x.shape, x.dtype),
        in_specs=[pl.BlockSpec(memory_space=pltpu.VMEM)],
        out_specs=pl.BlockSpec(memory_space=pltpu.VMEM),
        scratch_shapes=[pltpu.SemaphoreType.DMA] * 3,
        compiler_params=params(cid),
    )(x)


def potentials_kernel(
    inv, asked, posn, c_ref, logw_ref, beta_ref, lse_ref,
    padded, out1, in1, own, upper, summed, outx, inx, both, out2, in2,
    send1, recv1, send2, recv2, send3, recv3,
):
    me = lax.axis_index("blk")
    plane = lax.axis_index("grp")
    owners = lax.axis_size("blk")
    pairs, block = c_ref.shape
    rows = pairs // 8
    greet(["blk", "grp"])
    padded[pl.ds(0, pairs), :] = c_ref[...]
    padded[pl.ds(pairs, 8), :] = jnp.full((8, block), LOWEST, f32)

    @pl.loop(0, owners)
    def _(s):
        to = lax.rem(me + s, owners)
        out1[to, 0:1, :] = padded[pl.ds(inv[2 * to], 1), :]
        out1[to, 1:2, :] = padded[pl.ds(inv[2 * to + 1], 1), :]

        @pl.when(s > 0)
        def _():
            pltpu.make_async_remote_copy(
                src_ref=out1.at[to],
                dst_ref=in1.at[me],
                send_sem=send1,
                recv_sem=recv1,
                device_id={"blk": to},
                device_id_type=MESH,
            ).start()

    in1[me] = out1[me]
    own[...] = jnp.full(own.shape, LOWEST, f32)
    for r in range(rows):
        own[pl.ds(plane * rows + r, 1), :] = padded[pl.ds(8 * r, 1), :]
    wait_all(in1, send1, recv1, "blk")
    index = lax.broadcasted_iota(jnp.int32, own.shape, 0)

    def highest(t, best):
        for c in range(2):
            row = in1[t, c : c + 1, :]
            best = jnp.maximum(best, jnp.where(index == asked[2 * t + c], row, LOWEST))
        return best

    upper[pl.ds(0, own.shape[0]), :] = lax.fori_loop(0, owners, highest, own[...])
    upper[pl.ds(own.shape[0], 8), :] = jnp.zeros((8, block), f32)

    def add(t, total):
        for c in range(2):
            slot = asked[2 * t + c]
            value = jnp.exp(in1[t, c : c + 1, :] - upper[pl.ds(slot, 1), :])
            total = total + jnp.where(index == slot, value, 0.0)
        return total

    top = upper[pl.ds(0, own.shape[0]), :]
    first = jnp.where(own[...] > 0.5 * LOWEST, jnp.exp(own[...] - top), 0.0)
    total = lax.fori_loop(0, owners, add, first)
    mine = jnp.where(total > 0.0, top + jnp.log(jnp.where(total > 0.0, total, 1.0)), LOWEST)
    outx[...] = mine
    inx[plane] = mine
    send_all(lambda to: outx, inx.at[plane], send2, recv2, "grp")
    wait_all(inx, send2, recv2, "grp")
    planes = inx.shape[0]
    top = inx[0]
    for p in range(1, planes):
        top = jnp.maximum(top, inx[p])
    total = jnp.exp(inx[0] - top)
    for p in range(1, planes):
        total = total + jnp.exp(inx[p] - top)
    lse = top + jnp.log(total)
    both[0, pl.ds(0, lse.shape[0]), :] = logw_ref[...] - lse
    both[1, pl.ds(0, lse.shape[0]), :] = lse
    both[:, pl.ds(lse.shape[0], 8), :] = jnp.zeros((2, 8, block), f32)

    @pl.loop(0, owners)
    def _(s):
        to = lax.rem(me + s, owners)
        for c in range(2):
            slot = asked[2 * to + c]
            out2[to, 2 * c : 2 * c + 1, :] = both[0, pl.ds(slot, 1), :]
            out2[to, 2 * c + 1 : 2 * c + 2, :] = both[1, pl.ds(slot, 1), :]

        @pl.when(s > 0)
        def _():
            pltpu.make_async_remote_copy(
                src_ref=out2.at[to],
                dst_ref=in2.at[me],
                send_sem=send3,
                recv_sem=recv3,
                device_id={"blk": to},
                device_id_type=MESH,
            ).start()

    in2[me] = out2[me]
    wait_all(in2, send3, recv3, "blk")
    for r in range(rows):
        beta_ref[8 * r : 8 * r + 1, :] = both[0, pl.ds(plane * rows + r, 1), :]
        lse_ref[8 * r : 8 * r + 1, :] = both[1, pl.ds(plane * rows + r, 1), :]
        for k in range(7):
            where = posn[7 * r + k]
            owner = where // 2
            rank = where % 2
            beta_ref[8 * r + k + 1 : 8 * r + k + 2, :] = in2[owner, pl.ds(2 * rank, 1), :]
            lse_ref[8 * r + k + 1 : 8 * r + k + 2, :] = in2[owner, pl.ds(2 * rank + 1, 1), :]


def potentials(inv, asked, posn, c, logw, cid):
    pairs, block = c.shape
    owners = lax.axis_size("blk")
    planes = lax.axis_size("grp")
    held = logw.shape[0]
    smem = pl.BlockSpec(memory_space=pltpu.SMEM)
    vmem = pl.BlockSpec(memory_space=pltpu.VMEM)
    return pl.pallas_call(
        potentials_kernel,
        out_shape=(jax.ShapeDtypeStruct((pairs, block), f32),) * 2,
        in_specs=[smem, smem, smem, vmem, vmem],
        out_specs=(vmem, vmem),
        scratch_shapes=[
            pltpu.VMEM((pairs + 8, block), f32),
            pltpu.VMEM((owners, 2, block), f32),
            pltpu.VMEM((owners, 2, block), f32),
            pltpu.VMEM((held, block), f32),
            pltpu.VMEM((held + 8, block), f32),
            pltpu.VMEM((held, block), f32),
            pltpu.VMEM((held, block), f32),
            pltpu.VMEM((planes, held, block), f32),
            pltpu.VMEM((2, held + 8, block), f32),
            pltpu.VMEM((owners, 4, block), f32),
            pltpu.VMEM((owners, 4, block), f32),
        ]
        + [pltpu.SemaphoreType.DMA] * 6,
        compiler_params=params(cid),
    )(inv, asked, posn, c, logw)


def pack_kernel(groups, ids_ref, table_ref, o_ref, halves):
    count, width = table_ref.shape

    @pl.when(pl.program_id(0) == 0)
    def _():
        for start in range(0, count, 512):
            piece = table_ref[pl.ds(start, 512), :].astype(f32).reshape(32, 2, 8, width)
            for h in range(2):
                halves[h, pl.ds(start // 2, 256), :] = (
                    piece[:, h].reshape(256, width).astype(bf16)
                )

    ids = ids_ref[:, 0:1]
    index = lax.broadcasted_iota(jnp.int32, (ids.shape[0], count // 2), 1)
    hot = (index == ids).astype(f32).astype(bf16)
    low = nn(hot, halves[0])
    high = nn(hot, halves[1])
    for d in range(groups):
        for k in range(7):
            at = (d * 7 + k) * 8
            both = jnp.concatenate([low[at : at + 8], high[at : at + 8]], axis=0)
            o_ref[d, :, k * width : (k + 1) * width] = both.astype(bf16)


def pack(ids, table, dests):
    width = table.shape[-1]
    flat = table.reshape(-1, width)
    groups = 4
    return pl.pallas_call(
        functools.partial(pack_kernel, groups),
        grid=(dests // groups,),
        out_shape=jax.ShapeDtypeStruct((dests, 16, 7 * width), bf16),
        in_specs=[
            pl.BlockSpec((groups * 56, 128), lambda i: (i, 0)),
            pl.BlockSpec(flat.shape, lambda i: (0, 0)),
        ],
        out_specs=pl.BlockSpec((groups, 16, 7 * width), lambda i: (i, 0, 0)),
        scratch_shapes=[pltpu.VMEM((2, flat.shape[0] // 2, width), bf16)],
        compiler_params=params(),
    )(ids, flat)


def gather_rows_kernel(width, x_ref, o_ref, wide):
    lanes = x_ref.shape[1]
    for c in range(lanes // 128):
        wide[c] = x_ref[:, c * 128 : (c + 1) * 128].astype(f32)
    for r in range(8):
        for h in range(2):
            for c in range(2):
                if width == 128:
                    got = wide[c, pl.ds(h * 8 + r, 64, stride=16), :]
                    o_ref[r, 0, (2 * h + c) * 64 : (2 * h + c + 1) * 64, :] = got.astype(bf16)
            if width == 64:
                got = wide[0, pl.ds(h * 8 + r, 64, stride=16), :].astype(bf16)
                o_ref[r, 0, 2 * h * 64 : (2 * h + 1) * 64, :] = got[:, 0:64]
                o_ref[r, 0, (2 * h + 1) * 64 : (2 * h + 2) * 64, :] = got[:, 64:128]


def gather_rows(x, width):
    flat = x.reshape(x.shape[0] * 16, 7 * 2 * width)
    return pl.pallas_call(
        functools.partial(gather_rows_kernel, width),
        grid=(7,),
        out_shape=jax.ShapeDtypeStruct((8, 7, 256, width), bf16),
        in_specs=[pl.BlockSpec((flat.shape[0], 2 * width), lambda k: (0, k))],
        out_specs=pl.BlockSpec((8, 1, 256, width), lambda k: (0, k, 0, 0)),
        scratch_shapes=[pltpu.VMEM((2 * width // 128, flat.shape[0], 128), f32)],
        compiler_params=params(),
    )(flat)


def scatter_rows_kernel(x_ref, o_ref, wide):
    for r in range(8):
        for h in range(2):
            for c in range(2):
                at = (2 * h + c) * 64
                wide[c, pl.ds(h * 8 + r, 64, stride=16), :] = x_ref[r, 0, at : at + 64, :].astype(f32)
    for c in range(2):
        o_ref[:, c * 128 : (c + 1) * 128] = wide[c].astype(bf16)


def scatter_rows(x):
    rows = 1024
    return pl.pallas_call(
        scatter_rows_kernel,
        grid=(7,),
        out_shape=jax.ShapeDtypeStruct((rows, 7 * 256), bf16),
        in_specs=[pl.BlockSpec((8, 1, 256, 128), lambda k: (0, k, 0, 0))],
        out_specs=pl.BlockSpec((rows, 256), lambda k: (0, k)),
        scratch_shapes=[pltpu.VMEM((2, rows, 128), f32)],
        compiler_params=params(),
    )(x).reshape(64, 16, 7 * 256)


def squares_row(t):
    wide = t.astype(f32)
    square = wide * wide
    high = square.astype(bf16)
    low = (square - high.astype(f32)).astype(bf16)
    ones = jnp.ones((8, t.shape[1]), bf16)
    return SQUARE * (nt(ones, high) + nt(ones, low))[0:1]


def row_scores(first, x, own_ref, far_ref, beta_ref, scores):
    top = None
    for k in range(8):
        t = own_ref[...] if k == 0 else far_ref[0, k - 1]
        bias = -squares_row(t) if first else beta_ref[k : k + 1, :]
        z = nt(x, t) * CROSS + bias
        scores[k] = z
        top = z if top is None else jnp.maximum(top, z)
    return jnp.max(top, axis=1, keepdims=True)


def round_kernel(first, *refs):
    if first:
        x_ref, own_ref, far_ref, logw_ref, c_ref, alpha_ref, scores = refs
        beta_ref = None
    else:
        x_ref, own_ref, far_ref, logw_ref, beta_ref, c_ref, alpha_ref, scores = refs
    x = x_ref[...]
    peak = row_scores(first, x, own_ref, far_ref, beta_ref, scores)
    total = None
    for k in range(8):
        e = jnp.exp(scores[k] - peak)
        total = e if total is None else total + e
    alpha = logw_ref[...] - peak - jnp.log(jnp.sum(total, axis=1, keepdims=True))
    alpha_ref[...] = alpha
    for k in range(8):
        t = own_ref[...] if k == 0 else far_ref[0, k - 1]
        v = nt(x, t) * CROSS + alpha
        top = jnp.max(v, axis=0, keepdims=True)
        c_ref[k : k + 1, :] = top + jnp.log(jnp.sum(jnp.exp(v - top), axis=0, keepdims=True))


def one_round(x, own, far, logw, beta):
    first = beta is None
    specs = [
        pl.BlockSpec((256, 64), lambda r: (r, 0)),
        pl.BlockSpec((256, 64), lambda r: (r, 0)),
        pl.BlockSpec((1, 7, 256, 64), lambda r: (r, 0, 0, 0)),
        pl.BlockSpec((256, 1), lambda r: (r, 0)),
    ]
    args = [x, own, far, logw]
    if not first:
        specs.append(pl.BlockSpec((8, 256), lambda r: (r, 0)))
        args.append(beta)
    return pl.pallas_call(
        functools.partial(round_kernel, first),
        grid=(8,),
        out_shape=(jax.ShapeDtypeStruct((64, 256), f32), jax.ShapeDtypeStruct((2048, 1), f32)),
        in_specs=specs,
        out_specs=(
            pl.BlockSpec((8, 256), lambda r: (r, 0)),
            pl.BlockSpec((256, 1), lambda r: (r, 0)),
        ),
        scratch_shapes=[pltpu.VMEM((8, 256, 256), f32)],
        compiler_params=params(),
    )(*args)


def transport_kernel(
    x_ref, own_ref, far_ref, beta_ref, lse_ref, alpha_ref, ownf_ref, farf_ref, srcf_ref,
    moved_ref, diag_ref, parts_ref, scores,
):
    x = x_ref[...]
    peak = row_scores(False, x, own_ref, far_ref, beta_ref, scores)
    total = None
    mixed = None
    for k in range(8):
        e = jnp.exp(scores[k] - peak)
        total = e if total is None else total + e
        feats = ownf_ref[...] if k == 0 else farf_ref[0, k - 1]
        term = nn(e.astype(bf16), feats)
        mixed = term if mixed is None else mixed + term
    moved_ref[...] = (mixed / jnp.sum(total, axis=1, keepdims=True)).astype(bf16)
    alpha = alpha_ref[...]
    srcf = srcf_ref[...]
    for k in range(8):
        t = own_ref[...] if k == 0 else far_ref[0, k - 1]
        w = jnp.exp(nt(x, t) * CROSS + alpha - lse_ref[k : k + 1, :]).astype(bf16)
        part = tn(w, srcf).astype(bf16)
        if k == 0:
            diag_ref[...] = part
        else:
            parts_ref[0, k - 1] = part


def transport(x, own, far, beta, lse, alpha, ownf, farf, srcf):
    def row(width):
        return pl.BlockSpec((256, width), lambda r: (r, 0))

    def four(width):
        return pl.BlockSpec((1, 7, 256, width), lambda r: (r, 0, 0, 0))

    small = pl.BlockSpec((8, 256), lambda r: (r, 0))
    return pl.pallas_call(
        transport_kernel,
        grid=(8,),
        out_shape=(
            jax.ShapeDtypeStruct((2048, 128), bf16),
            jax.ShapeDtypeStruct((2048, 128), bf16),
            jax.ShapeDtypeStruct((8, 7, 256, 128), bf16),
        ),
        in_specs=[row(64), row(64), four(64), small, small, row(1), row(128), four(128), row(128)],
        out_specs=(row(128), row(128), four(128)),
        scratch_shapes=[pltpu.VMEM((8, 256, 256), f32)],
        compiler_params=params(),
    )(x, own, far, beta, lse, alpha, ownf, farf, srcf)


def collect_kernel(ids_ref, got_ref, o_ref, total):
    k = pl.program_id(0)
    got = got_ref[...].astype(f32).reshape(64, 2, 8, 256)
    index = lax.broadcasted_iota(jnp.int32, (total.shape[1], 512), 0)
    hot = (index == ids_ref[0]).astype(f32).astype(bf16)
    for h in range(2):
        piece = got[:, h].reshape(512, 256).astype(bf16)
        term = nn(hot, piece)

        @pl.when(k == 0)
        def _():
            total[h] = term

        @pl.when(k > 0)
        def _():
            total[h] += term

    @pl.when(k == 6)
    def _():
        for h in range(2):
            o_ref[:, h * 256 : (h + 1) * 256] = total[h].astype(bf16)


def collect(ids, got):
    flat = got.reshape(1024, 7 * 256)
    return pl.pallas_call(
        collect_kernel,
        grid=(7,),
        out_shape=jax.ShapeDtypeStruct((2048, 512), bf16),
        in_specs=[
            pl.BlockSpec((1, 1, 512), lambda k: (k, 0, 0)),
            pl.BlockSpec((1024, 256), lambda k: (0, k)),
        ],
        out_specs=pl.BlockSpec((2048, 512), lambda k: (0, 0)),
        scratch_shapes=[pltpu.VMEM((2, 2048, 256), f32)],
        compiler_params=params(),
    )(ids, flat)


def shards(
    source_points, target_points, source_logw, target_logw,
    source_feats, target_feats, pair_owner, pair_slot,
):
    n = lax.axis_size("blk")
    plane = lax.axis_index("grp")
    me = lax.axis_index("blk")
    start = plane * 2048
    own_points = lax.dynamic_slice_in_dim(target_points, start, 2048, 0)
    own_feats = lax.dynamic_slice_in_dim(target_feats, start, 2048, 0)

    requests = (pair_owner * 32 + pair_slot).reshape(56)
    table = lax.all_gather(requests, "blk")
    owner_of = table // 32
    slot_of = table % 32
    ids = (slot_of // 8) * 512 + owner_of * 8 + slot_of % 8
    ids = ids.reshape(n, 8, 7).transpose(0, 2, 1)
    ids_column = jnp.broadcast_to(ids.reshape(n * 56, 1), (n * 56, 128))
    ids_row = ids.transpose(1, 0, 2).reshape(7, 1, n * 8)
    here = owner_of == me
    rank = jnp.cumsum(here.astype(jnp.int32), axis=1) - 1
    asked = jnp.stack(
        [jnp.min(jnp.where(here & (rank == c), slot_of, 32), axis=1) for c in range(2)], axis=1
    ).reshape(2 * n)
    owners = pair_owner.reshape(56)
    earlier = jnp.tril(jnp.ones((56, 56), bool), -1) & (owners[:, None] == owners[None, :])
    posn = owners * 2 + jnp.sum(earlier.astype(jnp.int32), axis=1)
    order = jnp.arange(56, dtype=jnp.int32)
    row_of = order + order // 7 + 1
    inv = jnp.min(
        jnp.where(posn[None, :] == jnp.arange(2 * n)[:, None], row_of[None, :], 64), axis=1
    )

    def stripes(own, width):
        out = own.reshape(8, 2, 2, 64, width).transpose(3, 1, 0, 2, 4)
        return out.reshape(64, 16, 2 * width)

    point_table = reshard(stripes(own_points, 64), 0)
    feat_table = reshard(stripes(own_feats, 128), 1)
    far_points = gather_rows(exchange(pack(ids_column, point_table, n), 2), 64)
    sent_feats = pack(ids_column, feat_table, n)
    got_feats = lax.all_to_all(sent_feats, "blk", split_axis=0, concat_axis=0, tiled=True)

    logw = source_logw.reshape(2048, 1)
    owned_logw = target_logw.reshape(32, 256)
    beta = None
    for _ in range(ROUNDS):
        c, alpha = one_round(source_points, own_points, far_points, logw, beta)
        beta, lse = potentials(inv, asked, posn, c, owned_logw, 3)
    far_feats = gather_rows(got_feats, 128)
    moved_source, diag, parts = transport(
        source_points, own_points, far_points, beta, lse, alpha, own_feats, far_feats, source_feats
    )
    got_parts = exchange(scatter_rows(parts), 4)
    sums = collect(ids_row, got_parts)
    planes = spread(sums.reshape(4, 512, 512), 5)
    summed = jnp.sum(planes.astype(f32), axis=0).astype(bf16)
    final = exchange(
        summed.reshape(64, 8, 2, 256).transpose(0, 2, 1, 3).reshape(64, 16, 256), 6
    )
    far_sum = final.reshape(64, 2, 8, 2, 128).transpose(2, 1, 3, 0, 4).reshape(2048, 128)
    moved_target = (far_sum.astype(f32) + diag.astype(f32)).astype(bf16)
    return moved_source, moved_target


def solution(mesh):
    return jax.shard_map(
        shards,
        mesh=mesh,
        in_specs=(
            P(("blk", "grp"), None),
            P("blk", None),
            P(("blk", "grp")),
            P("blk"),
            P(("blk", "grp"), None),
            P("blk", None),
            P(("blk", "grp"), None),
            P(("blk", "grp"), None),
        ),
        out_specs=(P(("blk", "grp"), None), P(("blk", "grp"), None)),
        check_vma=False,
    )
```

```python
import functools
import jax
import jax.numpy as jnp
from jax import lax
from jax.experimental import pallas as pl
from jax.experimental.pallas import tpu as pltpu
from jax.sharding import PartitionSpec as P

LOWEST = -1e30
CROSS = 0.3125
SQUARE = 0.15625
MESH = pl.DeviceIdType.MESH
MIB = 2**20
f32 = jnp.float32
bf16 = jnp.bfloat16


def params(cid=None, vmem=48):
    if cid is None:
        return pltpu.CompilerParams(vmem_limit_bytes=vmem * MIB)
    return pltpu.CompilerParams(
        collective_id=cid, has_side_effects=True, vmem_limit_bytes=vmem * MIB
    )


def nt(a, b):
    return lax.dot_general(a, b, (((1,), (1,)), ((), ())), preferred_element_type=f32)


def tn(a, b):
    return lax.dot_general(a, b, (((0,), (0,)), ((), ())), preferred_element_type=f32)


def nn(a, b):
    return jnp.dot(a, b, preferred_element_type=f32)


def greet(axes):
    bar = pltpu.get_barrier_semaphore()
    total = 0
    for name in axes:
        n = lax.axis_size(name)
        me = lax.axis_index(name)

        @pl.loop(1, n)
        def _(s):
            pl.semaphore_signal(
                bar, inc=1, device_id={name: lax.rem(me + s, n)}, device_id_type=MESH
            )

        total += n - 1
    pl.semaphore_wait(bar, total)


def send_all(src, dst, send, recv, axis):
    n = lax.axis_size(axis)
    me = lax.axis_index(axis)

    @pl.loop(1, n)
    def _(s):
        to = lax.rem(me + s, n)
        pltpu.make_async_remote_copy(
            src_ref=src(to),
            dst_ref=dst,
            send_sem=send,
            recv_sem=recv,
            device_id={axis: to},
            device_id_type=MESH,
        ).start()


def wait_all(whole, send, recv, axis):
    n = lax.axis_size(axis)
    part = whole.at[pl.ds(0, n - 1)]
    copy = pltpu.make_async_remote_copy(
        src_ref=part,
        dst_ref=part,
        send_sem=send,
        recv_sem=recv,
        device_id={axis: lax.rem(lax.axis_index(axis) + 1, n)},
        device_id_type=MESH,
    )
    copy.wait_send()
    copy.wait_recv()


def exchange_kernel(x_ref, o_ref, send, recv, own):
    me = lax.axis_index("blk")
    greet(["blk"])
    mine = pltpu.make_async_copy(x_ref.at[me], o_ref.at[me], own)
    mine.start()
    send_all(lambda to: x_ref.at[to], o_ref.at[me], send, recv, "blk")
    mine.wait()
    wait_all(o_ref, send, recv, "blk")


def exchange(x, cid):
    return pl.pallas_call(
        exchange_kernel,
        out_shape=jax.ShapeDtypeStruct(x.shape, x.dtype),
        in_specs=[pl.BlockSpec(memory_space=pltpu.VMEM)],
        out_specs=pl.BlockSpec(memory_space=pltpu.VMEM),
        scratch_shapes=[pltpu.SemaphoreType.DMA] * 3,
        compiler_params=params(cid),
    )(x)


def front_kernel(
    ids_ref, points_ref, feats_ref, far_ref, packed_ref, table_ref,
    ids_all, ids_wide, table_p, table_f, halves_p, halves_f, out_p, in_p, wide,
    send_i, recv_i, send_p, recv_p, send_f, recv_f, own, sendx_p, recvx_p, sendx_f, recvx_f,
    send_t, recv_t,
):
    n = lax.axis_size("blk")
    me = lax.axis_index("blk")
    plane = lax.axis_index("grp")
    greet(["blk", "grp"])

    def remote(src, dst, send, recv, to):
        pltpu.make_async_remote_copy(
            src_ref=src,
            dst_ref=dst,
            send_sem=send,
            recv_sem=recv,
            device_id={"blk": to},
            device_id_type=MESH,
        ).start()

    @pl.loop(1, n)
    def _(s):
        to = lax.rem(me + s, n)
        remote(points_ref.at[to], table_p.at[plane, me], send_p, recv_p, to)
        remote(ids_ref, ids_all.at[n - s], send_i, recv_i, to)

    @pl.loop(1, n)
    def _(s):
        to = lax.rem(me + s, n)
        remote(feats_ref.at[to], table_f.at[plane, me], send_f, recv_f, to)

    ids_all[0] = ids_ref[...]
    table_p[plane, me] = points_ref[me]
    table_f[plane, me] = feats_ref[me]
    wait_all(points_ref, send_p, recv_p, "blk")
    send_all(lambda to: table_p.at[plane], table_p.at[plane], sendx_p, recvx_p, "grp")
    wait_all(ids_all, send_i, recv_i, "blk")
    ids = ids_all[...].reshape(n, 128)
    table_ref[...] = ids
    turned = jnp.transpose(ids.astype(f32))
    for s in range(n):
        ids_wide[s] = jnp.broadcast_to(turned[0:56, s : s + 1], (56, 128))
    wait_all(feats_ref, send_f, recv_f, "blk")
    send_all(lambda to: table_f.at[plane], table_f.at[plane], sendx_f, recvx_f, "grp")

    def halve(table, halves):
        width = halves.shape[2]

        @pl.loop(0, 4)
        def _(p):
            for start in range(0, n, 16):
                piece = table[p, pl.ds(start, 16)].astype(f32)
                for h in range(2):
                    halves[h, pl.ds(p * (8 * n) + start * 8, 128), :] = (
                        piece[:, 8 * h : 8 * h + 8].reshape(128, width).astype(bf16)
                    )

    def pack(halves, out, then):
        width = halves.shape[2]

        @pl.loop(0, n // 4)
        def _(g):
            ids = ids_wide[pl.ds(4 * g, 4)].reshape(224, 128)[:, 0:1]
            index = lax.broadcasted_iota(jnp.int32, (224, halves.shape[1]), 1)
            hot = (index == ids.astype(jnp.int32)).astype(f32).astype(bf16)
            low = nn(hot, halves[0])
            high = nn(hot, halves[1])
            for d in range(4):
                for k in range(7):
                    at = (d * 7 + k) * 8
                    both = jnp.concatenate([low[at : at + 8], high[at : at + 8]], axis=0)
                    out[4 * g + d, :, k * width : (k + 1) * width] = both.astype(bf16)
                then(4 * g + d)

    def send_points(s):
        @pl.when(s > 0)
        def _():
            to = lax.rem(me + s, n)
            remote(out_p.at[s], in_p.at[me], send_t, recv_t, to)

    wait_all(table_p, sendx_p, recvx_p, "grp")
    halve(table_p, halves_p)
    pack(halves_p, out_p, send_points)
    in_p[me] = out_p[0]
    wait_all(table_f, sendx_f, recvx_f, "grp")
    halve(table_f, halves_f)
    pack(halves_f, packed_ref, lambda s: None)
    wait_all(in_p, send_t, recv_t, "blk")
    for k in range(7):
        wide[...] = in_p[:, :, 128 * k : 128 * (k + 1)].astype(f32).reshape(n * 16, 128)
        for r in range(8):
            for h in range(2):
                got = wide[pl.ds(h * 8 + r, n, stride=16), :].astype(bf16)
                far_ref[r, k, 2 * h * 64 : (2 * h + 1) * 64, :] = got[:, 0:64]
                far_ref[r, k, (2 * h + 1) * 64 : (2 * h + 2) * 64, :] = got[:, 64:128]


def front(ids, points, feats, cid):
    n = lax.axis_size("blk")
    vmem = pl.BlockSpec(memory_space=pltpu.VMEM)
    return pl.pallas_call(
        front_kernel,
        out_shape=(
            jax.ShapeDtypeStruct((8, 7, 256, 64), bf16),
            jax.ShapeDtypeStruct((n, 16, 7 * 256), bf16),
            jax.ShapeDtypeStruct((n, 128), jnp.int32),
        ),
        in_specs=[vmem] * 3,
        out_specs=(vmem,) * 3,
        scratch_shapes=[
            pltpu.VMEM((n, 1, 128), jnp.int32),
            pltpu.VMEM((n, 56, 128), f32),
            pltpu.VMEM((4, n, 16, 128), bf16),
            pltpu.VMEM((4, n, 16, 256), bf16),
            pltpu.VMEM((2, 32 * n, 128), bf16),
            pltpu.VMEM((2, 32 * n, 256), bf16),
            pltpu.VMEM((n, 16, 7 * 128), bf16),
            pltpu.VMEM((n, 16, 7 * 128), bf16),
            pltpu.VMEM((n * 16, 128), f32),
        ]
        + [pltpu.SemaphoreType.DMA] * 13,
        compiler_params=params(cid),
    )(ids, points, feats)


def spread_kernel(x_ref, o_ref, send, recv, own):
    plane = lax.axis_index("grp")
    greet(["grp"])
    mine = pltpu.make_async_copy(x_ref.at[plane], o_ref.at[plane], own)
    mine.start()
    send_all(lambda to: x_ref.at[to], o_ref.at[plane], send, recv, "grp")
    mine.wait()
    wait_all(o_ref, send, recv, "grp")


def spread(x, cid):
    return pl.pallas_call(
        spread_kernel,
        out_shape=jax.ShapeDtypeStruct(x.shape, x.dtype),
        in_specs=[pl.BlockSpec(memory_space=pltpu.VMEM)],
        out_specs=pl.BlockSpec(memory_space=pltpu.VMEM),
        scratch_shapes=[pltpu.SemaphoreType.DMA] * 3,
        compiler_params=params(cid),
    )(x)


def rounds_kernel(
    inv, asked, posn, x_ref, own_ref, far_ref, logw_ref, logwt_ref, packed_ref,
    beta_ref, lse_ref, alpha_ref, got_ref,
    scores, padded, out1, in1, own, upper, outx, inx, both, out2, in2,
    send1, recv1, send2, recv2, send3, recv3, send_f, recv_f,
):
    me = lax.axis_index("blk")
    plane = lax.axis_index("grp")
    n = lax.axis_size("blk")
    pairs, block = beta_ref.shape
    rows = pairs // 8
    held = own.shape[0]
    greet(["blk", "grp"])
    padded[pl.ds(pairs, 8), :] = jnp.full((8, block), LOWEST, f32)

    def remote(src, dst, send, recv, to):
        pltpu.make_async_remote_copy(
            src_ref=src,
            dst_ref=dst,
            send_sem=send,
            recv_sem=recv,
            device_id={"blk": to},
            device_id_type=MESH,
        ).start()

    def bulk(chunk):
        @pl.loop(0, n // 8)
        def _(j):
            s = 8 * j + chunk

            @pl.when(s > 0)
            def _():
                remote(packed_ref.at[s], got_ref.at[me], send_f, recv_f, lax.rem(me + s, n))

    def compute(first, chunks):
        @pl.loop(0, rows)
        def _(r):
            for i, chunk in enumerate(chunks):

                @pl.when(r == i * (rows // len(chunks)))
                def _():
                    bulk(chunk)

            at = pl.ds(pl.multiple_of(r * block, block), block)
            x = x_ref[at, :]
            top = None
            for k in range(8):
                t = own_ref[at, :] if k == 0 else far_ref[r, k - 1]
                bias = -squares_row(t) if first else beta_ref[pl.ds(8 * r + k, 1), :]
                z = nt(x, t) * CROSS + bias
                scores[k] = z
                top = z if top is None else jnp.maximum(top, z)
            peak = jnp.max(top, axis=1, keepdims=True)
            total = None
            for k in range(8):
                e = jnp.exp(scores[k] - peak)
                total = e if total is None else total + e
            alpha = logw_ref[at, :] - peak - jnp.log(jnp.sum(total, axis=1, keepdims=True))
            alpha_ref[at, :] = alpha
            for k in range(8):
                t = own_ref[at, :] if k == 0 else far_ref[r, k - 1]
                v = nt(x, t) * CROSS + alpha
                top = jnp.max(v, axis=0, keepdims=True)
                padded[pl.ds(8 * r + k, 1), :] = top + jnp.log(
                    jnp.sum(jnp.exp(v - top), axis=0, keepdims=True)
                )

    def potentials(turn, chunks):
        @pl.loop(0, n)
        def _(s):
            to = lax.rem(me + s, n)
            out1[to, 0:1, :] = padded[pl.ds(inv[2 * to], 1), :]
            out1[to, 1:2, :] = padded[pl.ds(inv[2 * to + 1], 1), :]

            @pl.when(s > 0)
            def _():
                remote(out1.at[to], in1.at[me], send1, recv1, to)

        bulk(chunks[0])
        in1[me] = out1[me]
        own[...] = jnp.full(own.shape, LOWEST, f32)
        for r in range(rows):
            own[pl.ds(plane * rows + r, 1), :] = padded[pl.ds(8 * r, 1), :]
        wait_all(in1, send1, recv1, "blk")
        index = lax.broadcasted_iota(jnp.int32, own.shape, 0)

        def highest(t, best):
            for c in range(2):
                row = in1[t, c : c + 1, :]
                best = jnp.maximum(best, jnp.where(index == asked[2 * t + c], row, LOWEST))
            return best

        upper[pl.ds(0, held), :] = lax.fori_loop(0, n, highest, own[...])
        upper[pl.ds(held, 8), :] = jnp.zeros((8, block), f32)

        def add(t, total):
            for c in range(2):
                slot = asked[2 * t + c]
                value = jnp.exp(in1[t, c : c + 1, :] - upper[pl.ds(slot, 1), :])
                total = total + jnp.where(index == slot, value, 0.0)
            return total

        top = upper[pl.ds(0, held), :]
        first = jnp.where(own[...] > 0.5 * LOWEST, jnp.exp(own[...] - top), 0.0)
        total = lax.fori_loop(0, n, add, first)
        mine = jnp.where(total > 0.0, top + jnp.log(jnp.where(total > 0.0, total, 1.0)), LOWEST)
        outx[...] = mine
        here = inx.at[turn]
        here[plane] = mine
        send_all(lambda to: outx, here.at[plane], send2.at[turn], recv2.at[turn], "grp")
        wait_all(here, send2.at[turn], recv2.at[turn], "grp")
        planes = inx.shape[1]
        top = inx[turn, 0]
        for p in range(1, planes):
            top = jnp.maximum(top, inx[turn, p])
        total = jnp.exp(inx[turn, 0] - top)
        for p in range(1, planes):
            total = total + jnp.exp(inx[turn, p] - top)
        lse = top + jnp.log(total)
        both[0, pl.ds(0, held), :] = logwt_ref[...] - lse
        both[1, pl.ds(0, held), :] = lse
        both[:, pl.ds(held, 8), :] = jnp.zeros((2, 8, block), f32)

        @pl.loop(0, n)
        def _(s):
            to = lax.rem(me + s, n)
            for c in range(2):
                slot = asked[2 * to + c]
                out2[to, 2 * c : 2 * c + 1, :] = both[0, pl.ds(slot, 1), :]
                out2[to, 2 * c + 1 : 2 * c + 2, :] = both[1, pl.ds(slot, 1), :]

            @pl.when(s > 0)
            def _():
                remote(out2.at[to], in2.at[me], send3, recv3, to)

        bulk(chunks[1])
        in2[me] = out2[me]
        wait_all(in2, send3, recv3, "blk")
        for r in range(rows):
            beta_ref[8 * r : 8 * r + 1, :] = both[0, pl.ds(plane * rows + r, 1), :]
            lse_ref[8 * r : 8 * r + 1, :] = both[1, pl.ds(plane * rows + r, 1), :]
            for k in range(7):
                where = posn[8 * k + r]
                owner = where // 2
                rank = where % 2
                row = 8 * r + k + 1
                beta_ref[row : row + 1, :] = in2[owner, pl.ds(2 * rank, 1), :]
                lse_ref[row : row + 1, :] = in2[owner, pl.ds(2 * rank + 1, 1), :]

    compute(True, [0, 1])
    potentials(0, [2, 3])
    compute(False, [4, 5])
    potentials(1, [6, 7])
    got_ref[me] = packed_ref[0]
    wait_all(got_ref, send_f, recv_f, "blk")


def rounds(inv, asked, posn, x, own, far, logw, logwt, packed, cid):
    n = lax.axis_size("blk")
    planes = lax.axis_size("grp")
    pairs, block = 64, 256
    held = logwt.shape[0]
    smem = pl.BlockSpec(memory_space=pltpu.SMEM)
    vmem = pl.BlockSpec(memory_space=pltpu.VMEM)
    return pl.pallas_call(
        rounds_kernel,
        out_shape=(
            jax.ShapeDtypeStruct((pairs, block), f32),
            jax.ShapeDtypeStruct((pairs, block), f32),
            jax.ShapeDtypeStruct((2048, 1), f32),
            jax.ShapeDtypeStruct(packed.shape, bf16),
        ),
        in_specs=[smem] * 3 + [vmem] * 6,
        out_specs=(vmem,) * 4,
        scratch_shapes=[
            pltpu.VMEM((8, block, block), f32),
            pltpu.VMEM((pairs + 8, block), f32),
            pltpu.VMEM((n, 2, block), f32),
            pltpu.VMEM((n, 2, block), f32),
            pltpu.VMEM((held, block), f32),
            pltpu.VMEM((held + 8, block), f32),
            pltpu.VMEM((held, block), f32),
            pltpu.VMEM((2, planes, held, block), f32),
            pltpu.VMEM((2, held + 8, block), f32),
            pltpu.VMEM((n, 4, block), f32),
            pltpu.VMEM((n, 4, block), f32),
        ]
        + [pltpu.SemaphoreType.DMA] * 2
        + [pltpu.SemaphoreType.DMA((2,))] * 2
        + [pltpu.SemaphoreType.DMA] * 4,
        compiler_params=params(cid, 56),
    )(inv, asked, posn, x, own, far, logw, logwt, packed)


def gather_rows_kernel(width, x_ref, o_ref, wide):
    lanes = x_ref.shape[1]
    for c in range(lanes // 128):
        wide[c] = x_ref[:, c * 128 : (c + 1) * 128].astype(f32)
    for r in range(8):
        for h in range(2):
            for c in range(2):
                if width == 128:
                    got = wide[c, pl.ds(h * 8 + r, 64, stride=16), :]
                    o_ref[r, 0, (2 * h + c) * 64 : (2 * h + c + 1) * 64, :] = got.astype(bf16)
            if width == 64:
                got = wide[0, pl.ds(h * 8 + r, 64, stride=16), :].astype(bf16)
                o_ref[r, 0, 2 * h * 64 : (2 * h + 1) * 64, :] = got[:, 0:64]
                o_ref[r, 0, (2 * h + 1) * 64 : (2 * h + 2) * 64, :] = got[:, 64:128]


def gather_rows(x, width):
    flat = x.reshape(x.shape[0] * 16, 7 * 2 * width)
    return pl.pallas_call(
        functools.partial(gather_rows_kernel, width),
        grid=(7,),
        out_shape=jax.ShapeDtypeStruct((8, 7, 256, width), bf16),
        in_specs=[pl.BlockSpec((flat.shape[0], 2 * width), lambda k: (0, k))],
        out_specs=pl.BlockSpec((8, 1, 256, width), lambda k: (0, k, 0, 0)),
        scratch_shapes=[pltpu.VMEM((2 * width // 128, flat.shape[0], 128), f32)],
        compiler_params=params(),
    )(flat)


def scatter_rows_kernel(x_ref, o_ref, wide):
    for r in range(8):
        for h in range(2):
            for c in range(2):
                at = (2 * h + c) * 64
                wide[c, pl.ds(h * 8 + r, 64, stride=16), :] = x_ref[r, 0, at : at + 64, :].astype(f32)
    for c in range(2):
        o_ref[:, c * 128 : (c + 1) * 128] = wide[c].astype(bf16)


def scatter_rows(x):
    rows = 1024
    return pl.pallas_call(
        scatter_rows_kernel,
        grid=(7,),
        out_shape=jax.ShapeDtypeStruct((rows, 7 * 256), bf16),
        in_specs=[pl.BlockSpec((8, 1, 256, 128), lambda k: (0, k, 0, 0))],
        out_specs=pl.BlockSpec((rows, 256), lambda k: (0, k)),
        scratch_shapes=[pltpu.VMEM((2, rows, 128), f32)],
        compiler_params=params(),
    )(x).reshape(64, 16, 7 * 256)


def squares_row(t):
    wide = t.astype(f32)
    square = wide * wide
    high = square.astype(bf16)
    low = (square - high.astype(f32)).astype(bf16)
    ones = jnp.ones((8, t.shape[1]), bf16)
    return SQUARE * (nt(ones, high) + nt(ones, low))[0:1]


def row_scores(x, own_ref, far_ref, beta_ref, scores):
    top = None
    for k in range(8):
        t = own_ref[...] if k == 0 else far_ref[0, k - 1]
        z = nt(x, t) * CROSS + beta_ref[k : k + 1, :]
        scores[k] = z
        top = z if top is None else jnp.maximum(top, z)
    return jnp.max(top, axis=1, keepdims=True)


def transport_kernel(
    x_ref, own_ref, far_ref, beta_ref, lse_ref, alpha_ref, ownf_ref, farf_ref, srcf_ref,
    moved_ref, diag_ref, parts_ref, scores,
):
    x = x_ref[...]
    peak = row_scores(x, own_ref, far_ref, beta_ref, scores)
    total = None
    mixed = None
    for k in range(8):
        e = jnp.exp(scores[k] - peak)
        total = e if total is None else total + e
        feats = ownf_ref[...] if k == 0 else farf_ref[0, k - 1]
        term = nn(e.astype(bf16), feats)
        mixed = term if mixed is None else mixed + term
    moved_ref[...] = (mixed / jnp.sum(total, axis=1, keepdims=True)).astype(bf16)
    alpha = alpha_ref[...]
    srcf = srcf_ref[...]
    for k in range(8):
        t = own_ref[...] if k == 0 else far_ref[0, k - 1]
        w = jnp.exp(nt(x, t) * CROSS + alpha - lse_ref[k : k + 1, :]).astype(bf16)
        part = tn(w, srcf).astype(bf16)
        if k == 0:
            diag_ref[...] = part
        else:
            parts_ref[0, k - 1] = part


def transport(x, own, far, beta, lse, alpha, ownf, farf, srcf):
    def row(width):
        return pl.BlockSpec((256, width), lambda r: (r, 0))

    def four(width):
        return pl.BlockSpec((1, 7, 256, width), lambda r: (r, 0, 0, 0))

    small = pl.BlockSpec((8, 256), lambda r: (r, 0))
    return pl.pallas_call(
        transport_kernel,
        grid=(8,),
        out_shape=(
            jax.ShapeDtypeStruct((2048, 128), bf16),
            jax.ShapeDtypeStruct((2048, 128), bf16),
            jax.ShapeDtypeStruct((8, 7, 256, 128), bf16),
        ),
        in_specs=[row(64), row(64), four(64), small, small, row(1), row(128), four(128), row(128)],
        out_specs=(row(128), row(128), four(128)),
        scratch_shapes=[pltpu.VMEM((8, 256, 256), f32)],
        compiler_params=params(),
    )(x, own, far, beta, lse, alpha, ownf, farf, srcf)


def collect_kernel(ids_ref, got_ref, o_ref, total):
    k = pl.program_id(0)
    got = got_ref[...].astype(f32).reshape(64, 2, 8, 256)
    index = lax.broadcasted_iota(jnp.int32, (total.shape[1], 512), 0)
    hot = (index == ids_ref[0]).astype(f32).astype(bf16)
    for h in range(2):
        piece = got[:, h].reshape(512, 256).astype(bf16)
        term = nn(hot, piece)

        @pl.when(k == 0)
        def _():
            total[h] = term

        @pl.when(k > 0)
        def _():
            total[h] += term

    @pl.when(k == 6)
    def _():
        for h in range(2):
            o_ref[:, h * 256 : (h + 1) * 256] = total[h].astype(bf16)


def collect(ids, got):
    flat = got.reshape(1024, 7 * 256)
    return pl.pallas_call(
        collect_kernel,
        grid=(7,),
        out_shape=jax.ShapeDtypeStruct((2048, 512), bf16),
        in_specs=[
            pl.BlockSpec((1, 1, 512), lambda k: (k, 0, 0)),
            pl.BlockSpec((1024, 256), lambda k: (0, k)),
        ],
        out_specs=pl.BlockSpec((2048, 512), lambda k: (0, 0)),
        scratch_shapes=[pltpu.VMEM((2, 2048, 256), f32)],
        compiler_params=params(),
    )(ids, flat)


def shards(
    source_points, target_points, source_logw, target_logw,
    source_feats, target_feats, pair_owner, pair_slot,
):
    n = lax.axis_size("blk")
    plane = lax.axis_index("grp")
    me = lax.axis_index("blk")
    start = plane * 2048
    own_points = lax.dynamic_slice_in_dim(target_points, start, 2048, 0)
    own_feats = lax.dynamic_slice_in_dim(target_feats, start, 2048, 0)

    def stripes(own, width):
        out = own.reshape(8, 2, 2, 64, width).transpose(3, 1, 0, 2, 4)
        return out.reshape(64, 16, 2 * width)

    wanted = (pair_slot // 8) * 512 + pair_owner * 8 + pair_slot % 8
    ids = jnp.pad(wanted.T.reshape(1, 56), ((0, 0), (0, 72)))
    far_points, packed, near = front(
        ids, stripes(own_points, 64), stripes(own_feats, 128), 0
    )
    spin = lax.rem(jnp.arange(n) - me + n, n)
    table = near[spin][:, :56]
    ids_row = table.reshape(n, 7, 8).transpose(1, 0, 2).reshape(7, 1, n * 8)
    owner_of = (table // 8) % 64
    slot_of = (table // 512) * 8 + table % 8
    here = owner_of == me
    rank = jnp.cumsum(here.astype(jnp.int32), axis=1) - 1
    asked = jnp.stack(
        [jnp.min(jnp.where(here & (rank == c), slot_of, 32), axis=1) for c in range(2)], axis=1
    ).reshape(2 * n)
    owners = pair_owner.T.reshape(56)
    earlier = jnp.tril(jnp.ones((56, 56), bool), -1) & (owners[:, None] == owners[None, :])
    posn = owners * 2 + jnp.sum(earlier.astype(jnp.int32), axis=1)
    order = jnp.arange(56, dtype=jnp.int32)
    row_of = (order % 8) * 8 + order // 8 + 1
    inv = jnp.min(
        jnp.where(posn[None, :] == jnp.arange(2 * n)[:, None], row_of[None, :], 64), axis=1
    )

    logw = source_logw.reshape(2048, 1)
    owned_logw = target_logw.reshape(32, 256)
    beta, lse, alpha, got_feats = rounds(
        inv, asked, posn, source_points, own_points, far_points, logw, owned_logw, packed, 3
    )
    far_feats = gather_rows(got_feats, 128)
    moved_source, diag, parts = transport(
        source_points, own_points, far_points, beta, lse, alpha, own_feats, far_feats, source_feats
    )
    got_parts = exchange(scatter_rows(parts), 4)
    sums = collect(ids_row, got_parts)
    planes = spread(sums.reshape(4, 512, 512), 5)
    summed = jnp.sum(planes.astype(f32), axis=0).astype(bf16)
    final = exchange(
        summed.reshape(64, 8, 2, 256).transpose(0, 2, 1, 3).reshape(64, 16, 256), 6
    )
    far_sum = final.reshape(64, 2, 8, 2, 128).transpose(2, 1, 3, 0, 4).reshape(2048, 128)
    moved_target = (far_sum.astype(f32) + diag.astype(f32)).astype(bf16)
    return moved_source, moved_target


def solution(mesh):
    return jax.shard_map(
        shards,
        mesh=mesh,
        in_specs=(
            P(("blk", "grp"), None),
            P("blk", None),
            P(("blk", "grp")),
            P("blk"),
            P(("blk", "grp"), None),
            P("blk", None),
            P(("blk", "grp"), None),
            P(("blk", "grp"), None),
        ),
        out_specs=(P(("blk", "grp"), None), P(("blk", "grp"), None)),
        check_vma=False,
    )
```

```python
import functools
import jax
import jax.numpy as jnp
from jax import lax
from jax.experimental import pallas as pl
from jax.experimental.pallas import tpu as pltpu
from jax.sharding import PartitionSpec as P

LOWEST = -1e30
CROSS = 0.3125
SQUARE = 0.15625
MESH = pl.DeviceIdType.MESH
MIB = 2**20
f32 = jnp.float32
bf16 = jnp.bfloat16


def params(cid=None, vmem=48):
    if cid is None:
        return pltpu.CompilerParams(vmem_limit_bytes=vmem * MIB)
    return pltpu.CompilerParams(
        collective_id=cid, has_side_effects=True, vmem_limit_bytes=vmem * MIB
    )


def nt(a, b):
    return lax.dot_general(a, b, (((1,), (1,)), ((), ())), preferred_element_type=f32)


def tn(a, b):
    return lax.dot_general(a, b, (((0,), (0,)), ((), ())), preferred_element_type=f32)


def nn(a, b):
    return jnp.dot(a, b, preferred_element_type=f32)


def greet(axes):
    bar = pltpu.get_barrier_semaphore()
    total = 0
    for name in axes:
        n = lax.axis_size(name)
        me = lax.axis_index(name)

        @pl.loop(1, n)
        def _(s):
            pl.semaphore_signal(
                bar, inc=1, device_id={name: lax.rem(me + s, n)}, device_id_type=MESH
            )

        total += n - 1
    pl.semaphore_wait(bar, total)


def send_all(src, dst, send, recv, axis):
    n = lax.axis_size(axis)
    me = lax.axis_index(axis)

    @pl.loop(1, n)
    def _(s):
        to = lax.rem(me + s, n)
        pltpu.make_async_remote_copy(
            src_ref=src(to),
            dst_ref=dst,
            send_sem=send,
            recv_sem=recv,
            device_id={axis: to},
            device_id_type=MESH,
        ).start()


def wait_all(whole, send, recv, axis):
    n = lax.axis_size(axis)
    part = whole.at[pl.ds(0, n - 1)]
    copy = pltpu.make_async_remote_copy(
        src_ref=part,
        dst_ref=part,
        send_sem=send,
        recv_sem=recv,
        device_id={axis: lax.rem(lax.axis_index(axis) + 1, n)},
        device_id_type=MESH,
    )
    copy.wait_send()
    copy.wait_recv()


def front_kernel(
    ids_ref, points_ref, feats_ref, far_ref, packed_ref, table_ref,
    ids_all, ids_wide, table_p, table_f, halves_p, halves_f, out_p, in_p, wide,
    send_i, recv_i, send_p, recv_p, send_f, recv_f, own, sendx_p, recvx_p, sendx_f, recvx_f,
    send_t, recv_t,
):
    n = lax.axis_size("blk")
    me = lax.axis_index("blk")
    plane = lax.axis_index("grp")
    greet(["blk", "grp"])

    def remote(src, dst, send, recv, to):
        pltpu.make_async_remote_copy(
            src_ref=src,
            dst_ref=dst,
            send_sem=send,
            recv_sem=recv,
            device_id={"blk": to},
            device_id_type=MESH,
        ).start()

    @pl.loop(1, n)
    def _(s):
        to = lax.rem(me + s, n)
        remote(points_ref.at[to], table_p.at[plane, me], send_p, recv_p, to)
        remote(ids_ref, ids_all.at[n - s], send_i, recv_i, to)

    @pl.loop(1, n)
    def _(s):
        to = lax.rem(me + s, n)
        remote(feats_ref.at[to], table_f.at[plane, me], send_f, recv_f, to)

    ids_all[0] = ids_ref[...]
    table_p[plane, me] = points_ref[me]
    table_f[plane, me] = feats_ref[me]
    wait_all(points_ref, send_p, recv_p, "blk")
    send_all(lambda to: table_p.at[plane], table_p.at[plane], sendx_p, recvx_p, "grp")
    wait_all(ids_all, send_i, recv_i, "blk")
    ids = ids_all[...].reshape(n, 128)
    table_ref[...] = ids
    turned = jnp.transpose(ids.astype(f32))
    for s in range(n):
        ids_wide[s] = jnp.broadcast_to(turned[0:56, s : s + 1], (56, 128))
    wait_all(feats_ref, send_f, recv_f, "blk")
    send_all(lambda to: table_f.at[plane], table_f.at[plane], sendx_f, recvx_f, "grp")

    def halve(table, halves):
        width = halves.shape[2]

        @pl.loop(0, 4)
        def _(p):
            for start in range(0, n, 16):
                piece = table[p, pl.ds(start, 16)].astype(f32)
                for h in range(2):
                    halves[h, pl.ds(p * (8 * n) + start * 8, 128), :] = (
                        piece[:, 8 * h : 8 * h + 8].reshape(128, width).astype(bf16)
                    )

    def pack(halves, out, then):
        width = halves.shape[2]

        @pl.loop(0, n // 4)
        def _(g):
            ids = ids_wide[pl.ds(4 * g, 4)].reshape(224, 128)[:, 0:1]
            index = lax.broadcasted_iota(jnp.int32, (224, halves.shape[1]), 1)
            hot = (index == ids.astype(jnp.int32)).astype(f32).astype(bf16)
            low = nn(hot, halves[0])
            high = nn(hot, halves[1])
            for d in range(4):
                for k in range(7):
                    at = (d * 7 + k) * 8
                    both = jnp.concatenate([low[at : at + 8], high[at : at + 8]], axis=0)
                    out[4 * g + d, :, k * width : (k + 1) * width] = both.astype(bf16)
                then(4 * g + d)

    def send_points(s):
        @pl.when(s > 0)
        def _():
            to = lax.rem(me + s, n)
            remote(out_p.at[s], in_p.at[me], send_t, recv_t, to)

    wait_all(table_p, sendx_p, recvx_p, "grp")
    halve(table_p, halves_p)
    pack(halves_p, out_p, send_points)
    in_p[me] = out_p[0]
    wait_all(table_f, sendx_f, recvx_f, "grp")
    halve(table_f, halves_f)
    pack(halves_f, packed_ref, lambda s: None)
    wait_all(in_p, send_t, recv_t, "blk")
    for k in range(7):
        wide[...] = in_p[:, :, 128 * k : 128 * (k + 1)].astype(f32).reshape(n * 16, 128)
        for r in range(8):
            for h in range(2):
                got = wide[pl.ds(h * 8 + r, n, stride=16), :].astype(bf16)
                far_ref[r, k, 2 * h * 64 : (2 * h + 1) * 64, :] = got[:, 0:64]
                far_ref[r, k, (2 * h + 1) * 64 : (2 * h + 2) * 64, :] = got[:, 64:128]


def front(ids, points, feats, cid):
    n = lax.axis_size("blk")
    vmem = pl.BlockSpec(memory_space=pltpu.VMEM)
    return pl.pallas_call(
        front_kernel,
        out_shape=(
            jax.ShapeDtypeStruct((8, 7, 256, 64), bf16),
            jax.ShapeDtypeStruct((n, 16, 7 * 256), bf16),
            jax.ShapeDtypeStruct((n, 128), jnp.int32),
        ),
        in_specs=[vmem] * 3,
        out_specs=(vmem,) * 3,
        scratch_shapes=[
            pltpu.VMEM((n, 1, 128), jnp.int32),
            pltpu.VMEM((n, 56, 128), f32),
            pltpu.VMEM((4, n, 16, 128), bf16),
            pltpu.VMEM((4, n, 16, 256), bf16),
            pltpu.VMEM((2, 32 * n, 128), bf16),
            pltpu.VMEM((2, 32 * n, 256), bf16),
            pltpu.VMEM((n, 16, 7 * 128), bf16),
            pltpu.VMEM((n, 16, 7 * 128), bf16),
            pltpu.VMEM((n * 16, 128), f32),
        ]
        + [pltpu.SemaphoreType.DMA] * 13,
        compiler_params=params(cid),
    )(ids, points, feats)


def rounds_kernel(
    inv, asked, posn, x_ref, own_ref, far_ref, logw_ref, logwt_ref, packed_ref,
    beta_ref, lse_ref, alpha_ref, got_ref,
    scores, padded, out1, in1, own, upper, outx, inx, both, out2, in2,
    send1, recv1, send2, recv2, send3, recv3, send_f, recv_f,
):
    me = lax.axis_index("blk")
    plane = lax.axis_index("grp")
    n = lax.axis_size("blk")
    pairs, block = beta_ref.shape
    rows = pairs // 8
    held = own.shape[0]
    greet(["blk", "grp"])
    padded[pl.ds(pairs, 8), :] = jnp.full((8, block), LOWEST, f32)

    def remote(src, dst, send, recv, to):
        pltpu.make_async_remote_copy(
            src_ref=src,
            dst_ref=dst,
            send_sem=send,
            recv_sem=recv,
            device_id={"blk": to},
            device_id_type=MESH,
        ).start()

    def bulk(chunk):
        @pl.loop(0, n // 8)
        def _(j):
            s = 8 * j + chunk

            @pl.when(s > 0)
            def _():
                remote(packed_ref.at[s], got_ref.at[me], send_f, recv_f, lax.rem(me + s, n))

    def compute(first, chunks):
        @pl.loop(0, rows)
        def _(r):
            for i, chunk in enumerate(chunks):

                @pl.when(r == i * (rows // len(chunks)))
                def _():
                    bulk(chunk)

            at = pl.ds(pl.multiple_of(r * block, block), block)
            x = x_ref[at, :]
            top = None
            for k in range(8):
                t = own_ref[at, :] if k == 0 else far_ref[r, k - 1]
                bias = -squares_row(t) if first else beta_ref[pl.ds(8 * r + k, 1), :]
                z = nt(x, t) * CROSS + bias
                scores[k] = z
                top = z if top is None else jnp.maximum(top, z)
            peak = jnp.max(top, axis=1, keepdims=True)
            total = None
            for k in range(8):
                e = jnp.exp(scores[k] - peak)
                total = e if total is None else total + e
            alpha = logw_ref[at, :] - peak - jnp.log(jnp.sum(total, axis=1, keepdims=True))
            alpha_ref[at, :] = alpha
            for k in range(8):
                t = own_ref[at, :] if k == 0 else far_ref[r, k - 1]
                v = nt(x, t) * CROSS + alpha
                top = jnp.max(v, axis=0, keepdims=True)
                padded[pl.ds(8 * r + k, 1), :] = top + jnp.log(
                    jnp.sum(jnp.exp(v - top), axis=0, keepdims=True)
                )

    def potentials(turn, chunks):
        @pl.loop(0, n)
        def _(s):
            to = lax.rem(me + s, n)
            out1[to, 0:1, :] = padded[pl.ds(inv[2 * to], 1), :]
            out1[to, 1:2, :] = padded[pl.ds(inv[2 * to + 1], 1), :]

            @pl.when(s > 0)
            def _():
                remote(out1.at[to], in1.at[me], send1, recv1, to)

        bulk(chunks[0])
        in1[me] = out1[me]
        own[...] = jnp.full(own.shape, LOWEST, f32)
        for r in range(rows):
            own[pl.ds(plane * rows + r, 1), :] = padded[pl.ds(8 * r, 1), :]
        wait_all(in1, send1, recv1, "blk")
        index = lax.broadcasted_iota(jnp.int32, own.shape, 0)

        def highest(t, best):
            for c in range(2):
                row = in1[t, c : c + 1, :]
                best = jnp.maximum(best, jnp.where(index == asked[2 * t + c], row, LOWEST))
            return best

        upper[pl.ds(0, held), :] = lax.fori_loop(0, n, highest, own[...])
        upper[pl.ds(held, 8), :] = jnp.zeros((8, block), f32)

        def add(t, total):
            for c in range(2):
                slot = asked[2 * t + c]
                value = jnp.exp(in1[t, c : c + 1, :] - upper[pl.ds(slot, 1), :])
                total = total + jnp.where(index == slot, value, 0.0)
            return total

        top = upper[pl.ds(0, held), :]
        first = jnp.where(own[...] > 0.5 * LOWEST, jnp.exp(own[...] - top), 0.0)
        total = lax.fori_loop(0, n, add, first)
        mine = jnp.where(total > 0.0, top + jnp.log(jnp.where(total > 0.0, total, 1.0)), LOWEST)
        outx[...] = mine
        here = inx.at[turn]
        here[plane] = mine
        send_all(lambda to: outx, here.at[plane], send2.at[turn], recv2.at[turn], "grp")
        wait_all(here, send2.at[turn], recv2.at[turn], "grp")
        planes = inx.shape[1]
        top = inx[turn, 0]
        for p in range(1, planes):
            top = jnp.maximum(top, inx[turn, p])
        total = jnp.exp(inx[turn, 0] - top)
        for p in range(1, planes):
            total = total + jnp.exp(inx[turn, p] - top)
        lse = top + jnp.log(total)
        both[0, pl.ds(0, held), :] = logwt_ref[...] - lse
        both[1, pl.ds(0, held), :] = lse
        both[:, pl.ds(held, 8), :] = jnp.zeros((2, 8, block), f32)

        @pl.loop(0, n)
        def _(s):
            to = lax.rem(me + s, n)
            for c in range(2):
                slot = asked[2 * to + c]
                out2[to, 2 * c : 2 * c + 1, :] = both[0, pl.ds(slot, 1), :]
                out2[to, 2 * c + 1 : 2 * c + 2, :] = both[1, pl.ds(slot, 1), :]

            @pl.when(s > 0)
            def _():
                remote(out2.at[to], in2.at[me], send3, recv3, to)

        bulk(chunks[1])
        in2[me] = out2[me]
        wait_all(in2, send3, recv3, "blk")
        for r in range(rows):
            beta_ref[8 * r : 8 * r + 1, :] = both[0, pl.ds(plane * rows + r, 1), :]
            lse_ref[8 * r : 8 * r + 1, :] = both[1, pl.ds(plane * rows + r, 1), :]
            for k in range(7):
                where = posn[8 * k + r]
                owner = where // 2
                rank = where % 2
                row = 8 * r + k + 1
                beta_ref[row : row + 1, :] = in2[owner, pl.ds(2 * rank, 1), :]
                lse_ref[row : row + 1, :] = in2[owner, pl.ds(2 * rank + 1, 1), :]

    compute(True, [0, 1])
    potentials(0, [2, 3])
    compute(False, [4, 5])
    potentials(1, [6, 7])
    got_ref[me] = packed_ref[0]
    wait_all(got_ref, send_f, recv_f, "blk")


def rounds(inv, asked, posn, x, own, far, logw, logwt, packed, cid):
    n = lax.axis_size("blk")
    planes = lax.axis_size("grp")
    pairs, block = 64, 256
    held = logwt.shape[0]
    smem = pl.BlockSpec(memory_space=pltpu.SMEM)
    vmem = pl.BlockSpec(memory_space=pltpu.VMEM)
    return pl.pallas_call(
        rounds_kernel,
        out_shape=(
            jax.ShapeDtypeStruct((pairs, block), f32),
            jax.ShapeDtypeStruct((pairs, block), f32),
            jax.ShapeDtypeStruct((2048, 1), f32),
            jax.ShapeDtypeStruct(packed.shape, bf16),
        ),
        in_specs=[smem] * 3 + [vmem] * 6,
        out_specs=(vmem,) * 4,
        scratch_shapes=[
            pltpu.VMEM((8, block, block), f32),
            pltpu.VMEM((pairs + 8, block), f32),
            pltpu.VMEM((n, 2, block), f32),
            pltpu.VMEM((n, 2, block), f32),
            pltpu.VMEM((held, block), f32),
            pltpu.VMEM((held + 8, block), f32),
            pltpu.VMEM((held, block), f32),
            pltpu.VMEM((2, planes, held, block), f32),
            pltpu.VMEM((2, held + 8, block), f32),
            pltpu.VMEM((n, 4, block), f32),
            pltpu.VMEM((n, 4, block), f32),
        ]
        + [pltpu.SemaphoreType.DMA] * 2
        + [pltpu.SemaphoreType.DMA((2,))] * 2
        + [pltpu.SemaphoreType.DMA] * 4,
        compiler_params=params(cid, 56),
    )(inv, asked, posn, x, own, far, logw, logwt, packed)


def squares_row(t):
    wide = t.astype(f32)
    square = wide * wide
    high = square.astype(bf16)
    low = (square - high.astype(f32)).astype(bf16)
    ones = jnp.ones((8, t.shape[1]), bf16)
    return SQUARE * (nt(ones, high) + nt(ones, low))[0:1]


def back_kernel(
    ids_ref, x_ref, own_ref, far_ref, beta_ref, lse_ref, alpha_ref, ownf_ref, gotf_ref, srcf_ref,
    moved_ref, out_ref,
    scores, farf, wide, diag, out_h, in_h, pieces, total, out_x, in_x, out_f, in_f,
    send_m, recv_m, send_x, recv_x, send_f, recv_f,
):
    n = lax.axis_size("blk")
    me = lax.axis_index("blk")
    plane = lax.axis_index("grp")
    greet(["blk", "grp"])

    def remote(src, dst, send, recv, to):
        pltpu.make_async_remote_copy(
            src_ref=src,
            dst_ref=dst,
            send_sem=send,
            recv_sem=recv,
            device_id={"blk": to},
            device_id_type=MESH,
        ).start()

    def parts(h):
        @pl.loop(0, 8)
        def _(r):
            at = pl.ds(pl.multiple_of(r * 256, 256), 256)
            x = x_ref[at, :]
            alpha = alpha_ref[at, :]
            srcf = srcf_ref[at, :]
            half = pl.ds(pl.multiple_of(r * 256 + 128 * h, 128), 128)
            for k in range(8):
                t = own_ref[half, :] if k == 0 else far_ref[r, k - 1, 128 * h : 128 * h + 128, :]
                shift = lse_ref[pl.ds(8 * r + k, 1), :][:, 128 * h : 128 * h + 128]
                w = jnp.exp(nt(x, t) * CROSS + alpha - shift).astype(bf16)
                part = tn(w, srcf).astype(bf16).astype(f32)
                if k == 0:
                    diag[half, :] = part
                else:
                    for c in range(2):
                        wide[k - 1, pl.ds(c * 8 + r, n, stride=16), :] = part[64 * c : 64 * c + 64]

        for k in range(7):
            out_h[h, :, :, 128 * k : 128 * (k + 1)] = wide[k].reshape(n, 16, 128).astype(bf16)
        for chunk in range(8):

            @pl.loop(0, n // 8)
            def _(j):
                s = 8 * j + chunk

                @pl.when(s > 0)
                def _():
                    to = lax.rem(me + s, n)
                    remote(
                        out_h.at[h, to], in_h.at[h, me], send_m.at[h], recv_m.at[h, chunk // 2], to
                    )

        in_h[h, me] = out_h[h, me]

    def rows():
        for k in range(7):
            for c in range(2):
                lanes = 128 * (2 * k + c)
                buffer = (2 * k + c) % 7
                wide[buffer] = gotf_ref[:, :, lanes : lanes + 128].astype(f32).reshape(16 * n, 128)
                for r in range(8):
                    for h in range(2):
                        got = wide[buffer, pl.ds(h * 8 + r, n, stride=16), :]
                        farf[r, k, 64 * (2 * h + c) : 64 * (2 * h + c + 1), :] = got.astype(bf16)

        @pl.loop(0, 8)
        def _(r):
            at = pl.ds(pl.multiple_of(r * 256, 256), 256)
            x = x_ref[at, :]
            top = None
            for k in range(8):
                t = own_ref[at, :] if k == 0 else far_ref[r, k - 1]
                z = nt(x, t) * CROSS + beta_ref[pl.ds(8 * r + k, 1), :]
                scores[k] = z
                top = z if top is None else jnp.maximum(top, z)
            peak = jnp.max(top, axis=1, keepdims=True)
            weight = None
            mixed = None
            for k in range(8):
                e = jnp.exp(scores[k] - peak)
                weight = e if weight is None else weight + e
                feats = ownf_ref[at, :] if k == 0 else farf[r, k - 1]
                term = nn(e.astype(bf16), feats)
                mixed = term if mixed is None else mixed + term
            moved_ref[at, :] = (mixed / jnp.sum(weight, axis=1, keepdims=True)).astype(bf16)

    def collect(h, group):
        first = 1 if group == 0 else 0
        got = in_h.at[h, pl.ds(0, 16 - first)]
        pltpu.make_async_remote_copy(
            src_ref=got,
            dst_ref=got,
            send_sem=send_m.at[h],
            recv_sem=recv_m.at[h, group],
            device_id={"blk": lax.rem(me + 1, n)},
            device_id_type=MESH,
        ).wait_recv()

        @pl.loop(0, 8)
        def _(pair):
            chunk = 2 * group + pair // 4
            j = lax.rem(2 * pair, 8)
            one = in_h[h, lax.rem(me - 8 * j - chunk + 2 * n, n)].astype(f32)
            two = in_h[h, lax.rem(me - 8 * j - 8 - chunk + 2 * n, n)].astype(f32)
            for k in range(7):
                for c in range(2):
                    lanes = slice(128 * k, 128 * (k + 1))
                    both = jnp.concatenate(
                        [one[8 * c : 8 * c + 8, lanes], two[8 * c : 8 * c + 8, lanes]], axis=0
                    )
                    at = pl.ds(pl.multiple_of(128 * k + 16 * pair, 16), 16)
                    pieces[at, 128 * c : 128 * (c + 1)] = both.astype(bf16)

        @pl.loop(0, 8)
        def _(m):
            at = pl.ds(pl.multiple_of(256 * m, 256), 256)
            index = lax.broadcasted_iota(jnp.int32, (256, 896), 0) + 256 * m
            hot = (index == ids_ref[group]).astype(f32).astype(bf16)
            term = nn(hot, pieces[...])
            if group == 0:
                total[at, :] = term
            else:
                total[at, :] += term

    def spread(h):
        planes = out_x.shape[1]
        for p in range(planes):
            out_x[h, p] = total[512 * p : 512 * (p + 1), :].astype(bf16)
        in_x[h, plane] = out_x[h, plane]
        send_all(
            lambda to: out_x.at[h, to], in_x.at[h, plane], send_x.at[h], recv_x.at[h], "grp"
        )

    def finish(h):
        wait_all(in_x.at[h], send_x.at[h], recv_x.at[h], "grp")
        planes = in_x.shape[1]
        whole = in_x[h, 0].astype(f32)
        for p in range(1, planes):
            whole = whole + in_x[h, p].astype(f32)
        both = jnp.concatenate(
            [whole[:, 128 * c : 128 * (c + 1)].reshape(n, 8, 128) for c in range(2)], axis=1
        )
        out_f[h] = both.astype(bf16)

        @pl.loop(1, n)
        def _(s):
            to = lax.rem(me + s, n)
            remote(out_f.at[h, to], in_f.at[h, me], send_f.at[h], recv_f.at[h], to)

        in_f[h, me] = out_f[h, me]

    def deliver(h):
        wait_all(in_f.at[h], send_f.at[h], recv_f.at[h], "blk")
        wide[h] = in_f[h].astype(f32).reshape(16 * n, 128)
        for s in range(8):
            for c in range(2):
                at = 256 * s + 64 * (2 * h + c)
                got = wide[h, pl.ds(c * 8 + s, n, stride=16), :]
                out_ref[at : at + 64, :] = (got + diag[at : at + 64, :]).astype(bf16)

    parts(0)
    parts(1)
    rows()
    for group in range(4):
        collect(0, group)
    spread(0)
    collect(1, 0)
    collect(1, 1)
    finish(0)
    collect(1, 2)
    collect(1, 3)
    spread(1)
    finish(1)
    deliver(0)
    deliver(1)
    for h in range(2):
        sent = out_h.at[h, pl.ds(0, n - 1)]
        pltpu.make_async_remote_copy(
            src_ref=sent,
            dst_ref=sent,
            send_sem=send_m.at[h],
            recv_sem=recv_m.at[h, 0],
            device_id={"blk": lax.rem(me + 1, n)},
            device_id_type=MESH,
        ).wait_send()


def back(ids, x, own, far, beta, lse, alpha, ownf, gotf, srcf, cid):
    n = lax.axis_size("blk")
    planes = lax.axis_size("grp")
    vmem = pl.BlockSpec(memory_space=pltpu.VMEM)
    return pl.pallas_call(
        back_kernel,
        out_shape=(
            jax.ShapeDtypeStruct((2048, 128), bf16),
            jax.ShapeDtypeStruct((2048, 128), bf16),
        ),
        in_specs=[vmem] * 10,
        out_specs=(vmem,) * 2,
        scratch_shapes=[
            pltpu.VMEM((8, 256, 256), f32),
            pltpu.VMEM((8, 7, 256, 128), bf16),
            pltpu.VMEM((7, 16 * n, 128), f32),
            pltpu.VMEM((2048, 128), f32),
            pltpu.VMEM((2, n, 16, 896), bf16),
            pltpu.VMEM((2, n, 16, 896), bf16),
            pltpu.VMEM((896, 256), bf16),
            pltpu.VMEM((2048, 256), f32),
            pltpu.VMEM((2, planes, 512, 256), bf16),
            pltpu.VMEM((2, planes, 512, 256), bf16),
            pltpu.VMEM((2, n, 16, 128), bf16),
            pltpu.VMEM((2, n, 16, 128), bf16),
            pltpu.SemaphoreType.DMA((2,)),
            pltpu.SemaphoreType.DMA((2, 4)),
        ]
        + [pltpu.SemaphoreType.DMA((2,))] * 4,
        compiler_params=params(cid, 60),
    )(ids, x, own, far, beta, lse, alpha, ownf, gotf, srcf)


def shards(
    source_points, target_points, source_logw, target_logw,
    source_feats, target_feats, pair_owner, pair_slot,
):
    n = lax.axis_size("blk")
    plane = lax.axis_index("grp")
    me = lax.axis_index("blk")
    start = plane * 2048
    own_points = lax.dynamic_slice_in_dim(target_points, start, 2048, 0)
    own_feats = lax.dynamic_slice_in_dim(target_feats, start, 2048, 0)

    def stripes(own, width):
        out = own.reshape(8, 2, 2, 64, width).transpose(3, 1, 0, 2, 4)
        return out.reshape(64, 16, 2 * width)

    wanted = (pair_slot // 8) * 512 + pair_owner * 8 + pair_slot % 8
    ids = jnp.pad(wanted.T.reshape(1, 56), ((0, 0), (0, 72)))
    far_points, packed, near = front(
        ids, stripes(own_points, 64), stripes(own_feats, 128), 0
    )
    spin = lax.rem(jnp.arange(n) - me + n, n)
    table = near[spin][:, :56]
    message = jnp.arange(n)
    away = 8 * (message % 8) + message // 8
    ids_row = near[(n - away) % n][:, :56].reshape(4, 16, 7, 8).transpose(0, 2, 1, 3)
    ids_row = ids_row.reshape(4, 1, 896)
    owner_of = (table // 8) % 64
    slot_of = (table // 512) * 8 + table % 8
    here = owner_of == me
    rank = jnp.cumsum(here.astype(jnp.int32), axis=1) - 1
    asked = jnp.stack(
        [jnp.min(jnp.where(here & (rank == c), slot_of, 32), axis=1) for c in range(2)], axis=1
    ).reshape(2 * n)
    owners = pair_owner.T.reshape(56)
    earlier = jnp.tril(jnp.ones((56, 56), bool), -1) & (owners[:, None] == owners[None, :])
    posn = owners * 2 + jnp.sum(earlier.astype(jnp.int32), axis=1)
    order = jnp.arange(56, dtype=jnp.int32)
    row_of = (order % 8) * 8 + order // 8 + 1
    inv = jnp.min(
        jnp.where(posn[None, :] == jnp.arange(2 * n)[:, None], row_of[None, :], 64), axis=1
    )

    logw = source_logw.reshape(2048, 1)
    owned_logw = target_logw.reshape(32, 256)
    beta, lse, alpha, got_feats = rounds(
        inv, asked, posn, source_points, own_points, far_points, logw, owned_logw, packed, 3
    )
    moved_source, moved_target = back(
        ids_row, source_points, own_points, far_points, beta, lse, alpha,
        own_feats, got_feats, source_feats, 4,
    )
    return moved_source, moved_target


def solution(mesh):
    return jax.shard_map(
        shards,
        mesh=mesh,
        in_specs=(
            P(("blk", "grp"), None),
            P("blk", None),
            P(("blk", "grp")),
            P("blk"),
            P(("blk", "grp"), None),
            P("blk", None),
            P(("blk", "grp"), None),
            P(("blk", "grp"), None),
        ),
        out_specs=(P(("blk", "grp"), None), P(("blk", "grp"), None)),
        check_vma=False,
    )
```

```python
import functools
import jax
import jax.numpy as jnp
from jax import lax
from jax.experimental import pallas as pl
from jax.experimental.pallas import tpu as pltpu
from jax.sharding import PartitionSpec as P

LOWEST = -1e30
CROSS = 0.3125
SQUARE = 0.15625
MESH = pl.DeviceIdType.MESH
MIB = 2**20
f32 = jnp.float32
bf16 = jnp.bfloat16


def params(cid=None, vmem=48):
    if cid is None:
        return pltpu.CompilerParams(vmem_limit_bytes=vmem * MIB)
    return pltpu.CompilerParams(
        collective_id=cid, has_side_effects=True, vmem_limit_bytes=vmem * MIB
    )


def nt(a, b):
    return lax.dot_general(a, b, (((1,), (1,)), ((), ())), preferred_element_type=f32)


def tn(a, b):
    return lax.dot_general(a, b, (((0,), (0,)), ((), ())), preferred_element_type=f32)


def nn(a, b):
    return jnp.dot(a, b, preferred_element_type=f32)


def greet_signal(axes):
    bar = pltpu.get_barrier_semaphore()
    for name in axes:
        n = lax.axis_size(name)
        me = lax.axis_index(name)

        @pl.loop(1, n)
        def _(s):
            pl.semaphore_signal(
                bar, inc=1, device_id={name: lax.rem(me + s, n)}, device_id_type=MESH
            )


def greet_wait(axes):
    total = sum(lax.axis_size(name) - 1 for name in axes)
    pl.semaphore_wait(pltpu.get_barrier_semaphore(), total)


def remote(src, dst, send, recv, axis, to):
    return pltpu.make_async_remote_copy(
        src_ref=src,
        dst_ref=dst,
        send_sem=send,
        recv_sem=recv,
        device_id={axis: to},
        device_id_type=MESH,
    )


def send_all(src, dst, send, recv, axis):
    n = lax.axis_size(axis)
    me = lax.axis_index(axis)

    @pl.loop(1, n)
    def _(s):
        to = lax.rem(me + s, n)
        remote(src(to), dst, send, recv, axis, to).start()


def messages(ref, count, send, recv, axis):
    part = ref.at[pl.ds(0, count)]
    n = lax.axis_size(axis)
    return remote(part, part, send, recv, axis, lax.rem(lax.axis_index(axis) + 1, n))


def wait_all(ref, send, recv, axis):
    every = messages(ref, lax.axis_size(axis) - 1, send, recv, axis)
    every.wait_send()
    every.wait_recv()


def away(m):
    return 8 * lax.rem(m, 8) + m // 8


def message(s):
    return 8 * lax.rem(s, 8) + s // 8


def squares_row(t):
    wide = t.astype(f32)
    square = wide * wide
    high = square.astype(bf16)
    low = (square - high.astype(f32)).astype(bf16)
    ones = jnp.ones((8, t.shape[1]), bf16)
    return SQUARE * (nt(ones, high) + nt(ones, low))[0:1]


def whole_kernel(
    inv, posn, msg_ref, x_hbm, ownp_hbm, logw_ref, logwt_ref, srcf_hbm, tfeats_hbm,
    moved_ref, out_ref,
    x_ref, own_ref, srcf_ref, ownf_ref, stripe_p, stripe_f, logw_col, alpha_ref,
    ids_all, ids_wide, ids_lane, asked, table_p, table_f, halves_p, halves_f, out_p, in_p,
    far_ref, packed_ref, got_ref, scores, beta_ref, lse_ref,
    padded, out1, in1, own, upper, outx, inx, both, out2, in2,
    farf, wide, diag, out_h, in_h, pieces, total, out_x, in_x, out_f, in_f,
    local, send_i, recv_i, send_p, recv_p, send_t, recv_t, send_f, recv_f,
    send1, recv1, send3, recv3, send_s, recv_s,
    sendx_p, recvx_p, sendx_f, recvx_f, send2, recv2,
    send_m, recv_m, send_x, recv_x, send_o, recv_o,
):
    n = lax.axis_size("blk")
    me = lax.axis_index("blk")
    plane = lax.axis_index("grp")
    pairs, block = beta_ref.shape
    rows = pairs // 8
    held = own.shape[0]
    planes = table_p.shape[0]
    mine = pl.ds(pl.multiple_of(plane * 2048, 2048), 2048)
    copies = [
        pltpu.make_async_copy(src, dst, local.at[i])
        for i, (src, dst) in enumerate(
            [
                (ownp_hbm, own_ref),
                (tfeats_hbm.at[mine], ownf_ref),
                (x_hbm, x_ref),
                (srcf_hbm, srcf_ref),
            ]
        )
    ]
    for copy in copies:
        copy.start()
    greet_signal(["blk", "grp"])

    copies[0].wait()
    for s in range(8):
        for h in range(2):
            at = 256 * s + 128 * h
            pair = [own_ref[at + 64 * c : at + 64 * c + 64, :].astype(f32) for c in range(2)]
            wide[0, pl.ds(h * 8 + s, n, stride=16), :] = jnp.concatenate(pair, axis=1)
    stripe_p[...] = wide[0].reshape(n, 16, 128).astype(bf16)
    copies[1].wait()
    for c in range(2):
        for s in range(8):
            for h in range(2):
                at = 256 * s + 128 * h + 64 * c
                wide[1 + c, pl.ds(h * 8 + s, n, stride=16), :] = ownf_ref[at : at + 64, :].astype(f32)
        stripe_f[:, :, 128 * c : 128 * c + 128] = wide[1 + c].reshape(n, 16, 128).astype(bf16)
    greet_wait(["blk", "grp"])

    @pl.loop(1, n)
    def _(s):
        to = lax.rem(me + s, n)
        remote(stripe_p.at[to], table_p.at[plane, me], send_p, recv_p, "blk", to).start()
        remote(msg_ref.at[to], ids_all.at[message(s)], send_i, recv_i, "blk", to).start()

    @pl.loop(1, n)
    def _(s):
        to = lax.rem(me + s, n)
        remote(stripe_f.at[to], table_f.at[plane, me], send_s, recv_s, "blk", to).start()

    ids_all[0] = msg_ref[me]
    table_p[plane, me] = stripe_p[me]
    table_f[plane, me] = stripe_f[me]
    turned = jnp.transpose(logw_ref[...])
    for r in range(rows):
        logw_col[block * r : block * (r + 1), :] = turned[:, r : r + 1]
    padded[pl.ds(pairs, 8), :] = jnp.full((8, block), LOWEST, f32)
    copies[2].wait()
    copies[3].wait()
    wait_all(stripe_p, send_p, recv_p, "blk")
    send_all(lambda to: table_p.at[plane], table_p.at[plane], sendx_p, recvx_p, "grp")
    wait_all(ids_all, send_i, recv_i, "blk")
    scalars = pltpu.make_async_copy(ids_all, asked, local.at[0])
    scalars.start()
    ids = ids_all[...].reshape(n, 128).astype(f32)
    turned = jnp.transpose(ids)
    for m in range(n):
        ids_wide[m] = jnp.broadcast_to(turned[0:56, m : m + 1], (56, 128))
    spot = lax.broadcasted_iota(jnp.int32, (16, 128), 1) // 8
    row = lax.broadcasted_iota(jnp.int32, (16, 128), 0)
    for group in range(4):
        some = ids[16 * group : 16 * group + 16]
        for k in range(7):
            moved = pltpu.roll(some, (128 - 8 * k) % 128, 1)
            moved = pltpu.roll(moved, 0, 1, stride=8, stride_axis=0)
            ids_lane[group, :, 128 * k : 128 * k + 128] = jnp.sum(
                jnp.where(spot == row, moved, 0.0), axis=0, keepdims=True
            ).astype(jnp.int32)
    scalars.wait()
    wait_all(stripe_f, send_s, recv_s, "blk")
    send_all(lambda to: table_f.at[plane], table_f.at[plane], sendx_f, recvx_f, "grp")

    def halve(table, halves):
        width = halves.shape[2]

        @pl.loop(0, planes)
        def _(p):
            for start in range(0, n, 16):
                piece = table[p, pl.ds(start, 16)].astype(f32)
                for h in range(2):
                    at = pl.ds(p * (8 * n) + start * 8, 128)
                    halves[h, at, :] = piece[:, 8 * h : 8 * h + 8].reshape(128, width).astype(bf16)

    def pack(halves, out, then):
        width = halves.shape[2]

        @pl.loop(0, n // 4)
        def _(g):
            ids = ids_wide[pl.ds(4 * g, 4)].reshape(224, 128)[:, 0:1]
            index = lax.broadcasted_iota(jnp.int32, (224, halves.shape[1]), 1)
            hot = (index == ids.astype(jnp.int32)).astype(f32).astype(bf16)
            low = nn(hot, halves[0])
            high = nn(hot, halves[1])
            for d in range(4):
                for k in range(7):
                    at = (d * 7 + k) * 8
                    two = jnp.concatenate([low[at : at + 8], high[at : at + 8]], axis=0)
                    out[4 * g + d, :, k * width : (k + 1) * width] = two.astype(bf16)
                then(4 * g + d)

    def send_points(m):
        @pl.when(m > 0)
        def _():
            to = lax.rem(me + n - away(m), n)
            remote(out_p.at[m], in_p.at[me], send_t, recv_t, "blk", to).start()

    wait_all(table_p, sendx_p, recvx_p, "grp")
    halve(table_p, halves_p)
    pack(halves_p, out_p, send_points)
    in_p[me] = out_p[0]
    wait_all(table_f, sendx_f, recvx_f, "grp")
    halve(table_f, halves_f)
    pack(halves_f, packed_ref, lambda m: None)
    got_ref[me] = packed_ref[0]
    wait_all(in_p, send_t, recv_t, "blk")
    for k in range(7):
        wide[k] = in_p[:, :, 128 * k : 128 * (k + 1)].astype(f32).reshape(n * 16, 128)
        for r in range(8):
            for h in range(2):
                got = wide[k, pl.ds(h * 8 + r, n, stride=16), :].astype(bf16)
                far_ref[r, k, 2 * h * 64 : (2 * h + 1) * 64, :] = got[:, 0:64]
                far_ref[r, k, (2 * h + 1) * 64 : (2 * h + 2) * 64, :] = got[:, 64:128]

    def bulk(chunk):
        @pl.loop(0, n // 8)
        def _(j):
            m = 8 * chunk + j

            @pl.when(m > 0)
            def _():
                to = lax.rem(me + n - away(m), n)
                remote(packed_ref.at[m], got_ref.at[me], send_f, recv_f, "blk", to).start()

    def compute(first, chunks):
        @pl.loop(0, rows)
        def _(r):
            for i, chunk in enumerate(chunks):

                @pl.when(r == i * (rows // len(chunks)))
                def _():
                    bulk(chunk)

            at = pl.ds(pl.multiple_of(r * block, block), block)
            x = x_ref[at, :]
            top = None
            for k in range(8):
                t = own_ref[at, :] if k == 0 else far_ref[r, k - 1]
                bias = -squares_row(t) if first else beta_ref[pl.ds(8 * r + k, 1), :]
                z = nt(x, t) * CROSS + bias
                scores[k] = z
                top = z if top is None else jnp.maximum(top, z)
            peak = jnp.max(top, axis=1, keepdims=True)
            weight = None
            for k in range(8):
                e = jnp.exp(scores[k] - peak)
                weight = e if weight is None else weight + e
            alpha = logw_col[at, :] - peak - jnp.log(jnp.sum(weight, axis=1, keepdims=True))
            alpha_ref[at, :] = alpha
            for k in range(8):
                t = own_ref[at, :] if k == 0 else far_ref[r, k - 1]
                v = nt(x, t) * CROSS + alpha
                top = jnp.max(v, axis=0, keepdims=True)
                padded[pl.ds(8 * r + k, 1), :] = top + jnp.log(
                    jnp.sum(jnp.exp(v - top), axis=0, keepdims=True)
                )

    def potentials(turn, chunks):
        @pl.loop(0, n)
        def _(s):
            to = lax.rem(me + s, n)
            out1[to, 0:1, :] = padded[pl.ds(inv[2 * to], 1), :]
            out1[to, 1:2, :] = padded[pl.ds(inv[2 * to + 1], 1), :]

            @pl.when(s > 0)
            def _():
                remote(out1.at[to], in1.at[message(s)], send1, recv1, "blk", to).start()

        for chunk in chunks[0]:
            bulk(chunk)
        in1[0] = out1[me]
        own[...] = jnp.full(own.shape, LOWEST, f32)
        for r in range(rows):
            own[pl.ds(plane * rows + r, 1), :] = padded[pl.ds(8 * r, 1), :]
        wait_all(in1, send1, recv1, "blk")
        index = lax.broadcasted_iota(jnp.int32, own.shape, 0)

        def highest(m, best):
            for c in range(2):
                value = in1[m, c : c + 1, :]
                best = jnp.maximum(best, jnp.where(index == asked[m, 0, 56 + c], value, LOWEST))
            return best

        upper[pl.ds(0, held), :] = lax.fori_loop(0, n, highest, own[...])
        upper[pl.ds(held, 8), :] = jnp.zeros((8, block), f32)

        def add(m, so_far):
            for c in range(2):
                slot = asked[m, 0, 56 + c]
                value = jnp.exp(in1[m, c : c + 1, :] - upper[pl.ds(slot, 1), :])
                so_far = so_far + jnp.where(index == slot, value, 0.0)
            return so_far

        top = upper[pl.ds(0, held), :]
        first = jnp.where(own[...] > 0.5 * LOWEST, jnp.exp(own[...] - top), 0.0)
        summed = lax.fori_loop(0, n, add, first)
        part = jnp.where(summed > 0.0, top + jnp.log(jnp.where(summed > 0.0, summed, 1.0)), LOWEST)
        outx[...] = part
        here = inx.at[turn]
        here[plane] = part
        send_all(lambda to: outx, here.at[plane], send2.at[turn], recv2.at[turn], "grp")
        wait_all(here, send2.at[turn], recv2.at[turn], "grp")
        top = inx[turn, 0]
        for p in range(1, planes):
            top = jnp.maximum(top, inx[turn, p])
        summed = jnp.exp(inx[turn, 0] - top)
        for p in range(1, planes):
            summed = summed + jnp.exp(inx[turn, p] - top)
        lse = top + jnp.log(summed)
        both[0, pl.ds(0, held), :] = logwt_ref[...] - lse
        both[1, pl.ds(0, held), :] = lse
        both[:, pl.ds(held, 8), :] = jnp.zeros((2, 8, block), f32)

        @pl.loop(0, n)
        def _(m):
            for c in range(2):
                slot = asked[m, 0, 56 + c]
                out2[m, 2 * c : 2 * c + 1, :] = both[0, pl.ds(slot, 1), :]
                out2[m, 2 * c + 1 : 2 * c + 2, :] = both[1, pl.ds(slot, 1), :]

            @pl.when(m > 0)
            def _():
                to = lax.rem(me + n - away(m), n)
                remote(out2.at[m], in2.at[me], send3, recv3, "blk", to).start()

        for chunk in chunks[1]:
            bulk(chunk)
        in2[me] = out2[0]
        wait_all(in2, send3, recv3, "blk")
        for r in range(rows):
            beta_ref[8 * r : 8 * r + 1, :] = both[0, pl.ds(plane * rows + r, 1), :]
            lse_ref[8 * r : 8 * r + 1, :] = both[1, pl.ds(plane * rows + r, 1), :]
            for k in range(7):
                where = posn[8 * k + r]
                owner = where // 2
                rank = where % 2
                row = 8 * r + k + 1
                beta_ref[row : row + 1, :] = in2[owner, pl.ds(2 * rank, 1), :]
                lse_ref[row : row + 1, :] = in2[owner, pl.ds(2 * rank + 1, 1), :]

    compute(True, [0, 1])
    potentials(0, [[2], [3]])
    compute(False, [4, 5])
    potentials(1, [[6], [7]])

    def parts(h):
        @pl.loop(0, rows)
        def _(r):
            at = pl.ds(pl.multiple_of(r * block, block), block)
            x = x_ref[at, :]
            alpha = alpha_ref[at, :]
            srcf = srcf_ref[at, :]
            half = pl.ds(pl.multiple_of(r * 256 + 128 * h, 128), 128)
            for k in range(8):
                t = own_ref[half, :] if k == 0 else far_ref[r, k - 1, 128 * h : 128 * h + 128, :]
                shift = lse_ref[pl.ds(8 * r + k, 1), :][:, 128 * h : 128 * h + 128]
                w = jnp.exp(nt(x, t) * CROSS + alpha - shift).astype(bf16)
                part = tn(w, srcf).astype(bf16).astype(f32)
                if k == 0:
                    diag[half, :] = part
                else:
                    for c in range(2):
                        wide[k - 1, pl.ds(c * 8 + r, n, stride=16), :] = part[64 * c : 64 * c + 64]

        for k in range(7):
            out_h[h, :, :, 128 * k : 128 * (k + 1)] = wide[k].reshape(n, 16, 128).astype(bf16)
        for chunk in range(8):

            @pl.loop(0, n // 8)
            def _(j):
                s = 8 * j + chunk

                @pl.when(s > 0)
                def _():
                    to = lax.rem(me + s, n)
                    remote(
                        out_h.at[h, to],
                        in_h.at[h, 8 * chunk + j],
                        send_m.at[h],
                        recv_m.at[h, chunk // 2],
                        "blk",
                        to,
                    ).start()

        in_h[h, 0] = out_h[h, me]

    def move_rows():
        wait_all(got_ref, send_f, recv_f, "blk")
        for k in range(7):
            for c in range(2):
                lanes = 128 * (2 * k + c)
                buffer = (2 * k + c) % 7
                wide[buffer] = got_ref[:, :, lanes : lanes + 128].astype(f32).reshape(16 * n, 128)
                for r in range(8):
                    for h in range(2):
                        got = wide[buffer, pl.ds(h * 8 + r, n, stride=16), :]
                        farf[r, k, 64 * (2 * h + c) : 64 * (2 * h + c + 1), :] = got.astype(bf16)

        @pl.loop(0, rows)
        def _(r):
            at = pl.ds(pl.multiple_of(r * block, block), block)
            x = x_ref[at, :]
            top = None
            for k in range(8):
                t = own_ref[at, :] if k == 0 else far_ref[r, k - 1]
                z = nt(x, t) * CROSS + beta_ref[pl.ds(8 * r + k, 1), :]
                scores[k] = z
                top = z if top is None else jnp.maximum(top, z)
            peak = jnp.max(top, axis=1, keepdims=True)
            weight = None
            mixed = None
            for k in range(8):
                e = jnp.exp(scores[k] - peak)
                weight = e if weight is None else weight + e
                feats = ownf_ref[at, :] if k == 0 else farf[r, k - 1]
                term = nn(e.astype(bf16), feats)
                mixed = term if mixed is None else mixed + term
            moved_ref[at, :] = (mixed / jnp.sum(weight, axis=1, keepdims=True)).astype(bf16)

    def collect(h, group):
        count = 16 - (1 if group == 0 else 0)
        messages(in_h.at[h], count, send_m.at[h], recv_m.at[h, group], "blk").wait_recv()

        @pl.loop(0, 8)
        def _(pair):
            one = in_h[h, 16 * group + 2 * pair].astype(f32)
            two = in_h[h, 16 * group + 2 * pair + 1].astype(f32)
            for k in range(7):
                for c in range(2):
                    lanes = slice(128 * k, 128 * (k + 1))
                    joined = jnp.concatenate(
                        [one[8 * c : 8 * c + 8, lanes], two[8 * c : 8 * c + 8, lanes]], axis=0
                    )
                    at = pl.ds(pl.multiple_of(128 * k + 16 * pair, 16), 16)
                    pieces[at, 128 * c : 128 * (c + 1)] = joined.astype(bf16)

        @pl.loop(0, 8)
        def _(i):
            at = pl.ds(pl.multiple_of(256 * i, 256), 256)
            index = lax.broadcasted_iota(jnp.int32, (256, 896), 0) + 256 * i
            hot = (index == ids_lane[group]).astype(f32).astype(bf16)
            term = nn(hot, pieces[...])
            if group == 0:
                total[at, :] = term
            else:
                total[at, :] += term

    def spread(h):
        for p in range(planes):
            out_x[h, p] = total[512 * p : 512 * (p + 1), :].astype(bf16)
        in_x[h, plane] = out_x[h, plane]
        send_all(
            lambda to: out_x.at[h, to], in_x.at[h, plane], send_x.at[h], recv_x.at[h], "grp"
        )

    def finish(h):
        wait_all(in_x.at[h], send_x.at[h], recv_x.at[h], "grp")
        added = in_x[h, 0].astype(f32)
        for p in range(1, planes):
            added = added + in_x[h, p].astype(f32)
        joined = jnp.concatenate(
            [added[:, 128 * c : 128 * (c + 1)].reshape(n, 8, 128) for c in range(2)], axis=1
        )
        out_f[h] = joined.astype(bf16)
        send_all(lambda to: out_f.at[h, to], in_f.at[h, me], send_o.at[h], recv_o.at[h], "blk")
        in_f[h, me] = out_f[h, me]

    def deliver(h):
        wait_all(in_f.at[h], send_o.at[h], recv_o.at[h], "blk")
        wide[h] = in_f[h].astype(f32).reshape(16 * n, 128)
        for s in range(8):
            for c in range(2):
                at = 256 * s + 64 * (2 * h + c)
                got = wide[h, pl.ds(c * 8 + s, n, stride=16), :]
                out_ref[at : at + 64, :] = (got + diag[at : at + 64, :]).astype(bf16)

    parts(0)
    parts(1)
    move_rows()
    for group in range(4):
        collect(0, group)
    spread(0)
    collect(1, 0)
    collect(1, 1)
    finish(0)
    collect(1, 2)
    collect(1, 3)
    spread(1)
    finish(1)
    deliver(0)
    deliver(1)
    for h in range(2):
        messages(out_h.at[h], n - 1, send_m.at[h], recv_m.at[h, 0], "blk").wait_send()


def whole(inv, posn, msg, x, ownp, logw, logwt, srcf, tfeats, cid):
    n = lax.axis_size("blk")
    planes = lax.axis_size("grp")
    pairs, block = 64, 256
    held = logwt.shape[0]
    smem = pl.BlockSpec(memory_space=pltpu.SMEM)
    vmem = pl.BlockSpec(memory_space=pltpu.VMEM)
    hbm = pl.BlockSpec(memory_space=pl.ANY)
    scratch = [
        ((2048, 64), bf16),
        ((2048, 64), bf16),
        ((2048, 128), bf16),
        ((2048, 128), bf16),
        ((n, 16, 128), bf16),
        ((n, 16, 256), bf16),
        ((2048, 1), f32),
        ((2048, 1), f32),
        ((n, 1, 128), jnp.int32),
        ((n, 56, 128), f32),
        ((4, 1, 896), jnp.int32),
        None,
        ((planes, n, 16, 128), bf16),
        ((planes, n, 16, 256), bf16),
        ((2, planes * 8 * n, 128), bf16),
        ((2, planes * 8 * n, 256), bf16),
        ((n, 16, 7 * 128), bf16),
        ((n, 16, 7 * 128), bf16),
        ((8, 7, 256, 64), bf16),
        ((n, 16, 7 * 256), bf16),
        ((n, 16, 7 * 256), bf16),
        ((8, block, block), f32),
        ((pairs, block), f32),
        ((pairs, block), f32),
        ((pairs + 8, block), f32),
        ((n, 2, block), f32),
        ((n, 2, block), f32),
        ((held, block), f32),
        ((held + 8, block), f32),
        ((held, block), f32),
        ((2, planes, held, block), f32),
        ((2, held + 8, block), f32),
        ((n, 4, block), f32),
        ((n, 4, block), f32),
        ((8, 7, 256, 128), bf16),
        ((7, 16 * n, 128), f32),
        ((2048, 128), f32),
        ((2, n, 16, 896), bf16),
        ((2, n, 16, 896), bf16),
        ((896, 256), bf16),
        ((planes * 8 * n, 256), f32),
        ((2, planes, 8 * n, 256), bf16),
        ((2, planes, 8 * n, 256), bf16),
        ((2, n, 16, 128), bf16),
        ((2, n, 16, 128), bf16),
    ]
    dma = pltpu.SemaphoreType.DMA
    return pl.pallas_call(
        whole_kernel,
        out_shape=(
            jax.ShapeDtypeStruct((2048, 128), bf16),
            jax.ShapeDtypeStruct((2048, 128), bf16),
        ),
        in_specs=[smem, smem, vmem, hbm, hbm, vmem, vmem, hbm, hbm],
        out_specs=(vmem,) * 2,
        scratch_shapes=[
            pltpu.SMEM((n, 1, 128), jnp.int32) if item is None else pltpu.VMEM(*item)
            for item in scratch
        ]
        + [dma((4,))]
        + [dma] * 14
        + [dma] * 4
        + [dma((2,))] * 2
        + [dma((2,)), dma((2, 4))]
        + [dma((2,))] * 4,
        compiler_params=params(cid, 62),
    )(inv, posn, msg, x, ownp, logw, logwt, srcf, tfeats)


def shards(
    source_points, target_points, source_logw, target_logw,
    source_feats, target_feats, pair_owner, pair_slot,
):
    n = lax.axis_size("blk")
    plane = lax.axis_index("grp")
    own_points = lax.dynamic_slice_in_dim(target_points, plane * 2048, 2048, 0)
    owners = pair_owner.T.reshape(56)
    slots = pair_slot.T.reshape(56)
    ids = (slots // 8) * (8 * n) + owners * 8 + slots % 8
    earlier = jnp.tril(jnp.ones((56, 56), bool), -1) & (owners[:, None] == owners[None, :])
    posn = owners * 2 + jnp.sum(earlier.astype(jnp.int32), axis=1)
    order = jnp.arange(56, dtype=jnp.int32)
    row_of = (order % 8) * 8 + order // 8 + 1
    at = posn[None, :] == jnp.arange(2 * n, dtype=jnp.int32)[:, None]
    inv = jnp.min(jnp.where(at, row_of[None, :], 64), axis=1)
    asked = jnp.min(jnp.where(at, slots[None, :], 32), axis=1).reshape(n, 2)
    msg = jnp.concatenate(
        [jnp.broadcast_to(ids[None], (n, 56)), asked, jnp.zeros((n, 70), jnp.int32)], axis=1
    ).reshape(n, 1, 128)
    return whole(
        inv, posn, msg, source_points, own_points, source_logw.reshape(8, 256),
        target_logw.reshape(32, 256), source_feats, target_feats, 0,
    )


def solution(mesh):
    return jax.shard_map(
        shards,
        mesh=mesh,
        in_specs=(
            P(("blk", "grp"), None),
            P("blk", None),
            P(("blk", "grp")),
            P("blk"),
            P(("blk", "grp"), None),
            P("blk", None),
            P(("blk", "grp"), None),
            P(("blk", "grp"), None),
        ),
        out_specs=(P(("blk", "grp"), None), P(("blk", "grp"), None)),
        check_vma=False,
    )
```

```python
import functools
import jax
import jax.numpy as jnp
from jax import lax
from jax.experimental import pallas as pl
from jax.experimental.pallas import tpu as pltpu
from jax.sharding import PartitionSpec as P

LOWEST = -1e30
CROSS = 0.3125
SQUARE = 0.15625
MESH = pl.DeviceIdType.MESH
MIB = 2**20
SCHEDULE = ((3, 10, 6), (3, 10, 6))
f32 = jnp.float32
bf16 = jnp.bfloat16


def params(cid=None, vmem=48):
    if cid is None:
        return pltpu.CompilerParams(vmem_limit_bytes=vmem * MIB)
    return pltpu.CompilerParams(
        collective_id=cid, has_side_effects=True, vmem_limit_bytes=vmem * MIB
    )


def nt(a, b):
    return lax.dot_general(a, b, (((1,), (1,)), ((), ())), preferred_element_type=f32)


def tn(a, b):
    return lax.dot_general(a, b, (((0,), (0,)), ((), ())), preferred_element_type=f32)


def nn(a, b):
    return jnp.dot(a, b, preferred_element_type=f32)


def greet_signal(axes):
    bar = pltpu.get_barrier_semaphore()
    for name in axes:
        n = lax.axis_size(name)
        me = lax.axis_index(name)

        @pl.loop(1, n)
        def _(s):
            pl.semaphore_signal(
                bar, inc=1, device_id={name: lax.rem(me + s, n)}, device_id_type=MESH
            )


def greet_wait(axes):
    total = sum(lax.axis_size(name) - 1 for name in axes)
    pl.semaphore_wait(pltpu.get_barrier_semaphore(), total)


def remote(src, dst, send, recv, axis, to):
    return pltpu.make_async_remote_copy(
        src_ref=src,
        dst_ref=dst,
        send_sem=send,
        recv_sem=recv,
        device_id={axis: to},
        device_id_type=MESH,
    )


def send_all(src, dst, send, recv, axis):
    n = lax.axis_size(axis)
    me = lax.axis_index(axis)

    @pl.loop(1, n)
    def _(s):
        to = lax.rem(me + s, n)
        remote(src(to), dst, send, recv, axis, to).start()


def messages(ref, count, send, recv, axis):
    part = ref.at[pl.ds(0, count)]
    n = lax.axis_size(axis)
    return remote(part, part, send, recv, axis, lax.rem(lax.axis_index(axis) + 1, n))


def wait_all(ref, send, recv, axis):
    every = messages(ref, lax.axis_size(axis) - 1, send, recv, axis)
    every.wait_send()
    every.wait_recv()


def away(m):
    place = lax.rem(m, 8)
    return 8 * (2 * lax.rem(place, 4) + place // 4) + m // 8


def holder(m, me):
    z, yc = me // 8, lax.rem(me, 8)
    return 8 * lax.rem(z + 8 + along(m, yc), 8) + lax.rem(yc + m // 4, 8)


def sender(m, me):
    z, yc = me // 8, lax.rem(lax.rem(me, 8) + 8 - m // 4, 8)
    return 8 * lax.rem(z + 8 - along(m, yc), 8) + yc


def along(m, yc):
    turn = lax.rem(m, 4)
    two = (turn // 2) * (1 - turn // 3)
    return turn - 4 * (turn // 3) - 4 * two * lax.rem(yc, 2)


def stripe(device):
    return 8 * lax.rem(device // 8, 4) + lax.rem(device, 8)


def message(s):
    z = s // 8
    return 8 * lax.rem(s, 8) + z // 2 + 4 * lax.rem(z, 2)


def squares_row(t):
    wide = t.astype(f32)
    square = wide * wide
    high = square.astype(bf16)
    low = (square - high.astype(f32)).astype(bf16)
    ones = jnp.ones((8, t.shape[1]), bf16)
    return SQUARE * (nt(ones, high) + nt(ones, low))[0:1]


def whole_kernel(
    inv, posn, msg_ref, x_hbm, ownp_hbm, logw_ref, logwt_ref, srcf_hbm, tfeats_hbm,
    moved_ref, out_ref,
    turned_x, turned_own, logwt, x_ref, own_ref, srcf_ref, ownf_ref, stripe_p, stripe_f, logw_col, alpha_ref,
    ids_all, ids_sel, ids_wide, ids_lane, asked, table_p, table_f, halves_p, halves_f, out_p, in_p,
    far_ref, packed_ref, got_ref, scores, beta_ref, lse_ref,
    padded, out1, in1, own, upper, outx, inx, both, out2, in2,
    farf, wide, diag, out_h, in_h, pieces, total, out_x, in_x, out_f, in_f,
    local, send_i, recv_i, send_p, recv_p, send_t, recv_t, send_f, recv_f,
    send1, recv1, send3, recv3, send_s, recv_s,
    sendx_p, recvx_p, sendx_f, recvx_f, send2, recv2,
    send_m, recv_m, send_x, recv_x, send_o, recv_o,
):
    n = lax.axis_size("blk")
    me = lax.axis_index("blk")
    plane = lax.axis_index("grp")
    pairs, block = beta_ref.shape
    rows = pairs // 8
    held = own.shape[0]
    planes = table_p.shape[0]
    mine = pl.ds(pl.multiple_of(plane * 2048, 2048), 2048)
    copies = [
        pltpu.make_async_copy(src, dst, local.at[i])
        for i, (src, dst) in enumerate(
            [
                (ownp_hbm.at[:, mine], turned_own),
                (tfeats_hbm.at[mine], ownf_ref),
                (x_hbm, turned_x),
                (srcf_hbm, srcf_ref),
            ]
        )
    ]
    for copy in copies:
        copy.start()
    greet_signal(["blk", "grp"])

    copies[0].wait()
    for i in range(0, 2048, 256):
        own_ref[i : i + 256, :] = jnp.transpose(turned_own[:, i : i + 256].astype(f32)).astype(bf16)
    for s in range(8):
        for h in range(2):
            at = 256 * s + 128 * h
            pair = [own_ref[at + 64 * c : at + 64 * c + 64, :].astype(f32) for c in range(2)]
            wide[0, pl.ds(h * 8 + s, n, stride=16), :] = jnp.concatenate(pair, axis=1)
    stripe_p[...] = wide[0].reshape(n, 16, 128).astype(bf16)
    copies[1].wait()
    for c in range(2):
        for s in range(8):
            for h in range(2):
                at = 256 * s + 128 * h + 64 * c
                wide[1 + c, pl.ds(h * 8 + s, n, stride=16), :] = ownf_ref[at : at + 64, :].astype(f32)
        stripe_f[:, :, 128 * c : 128 * c + 128] = wide[1 + c].reshape(n, 16, 128).astype(bf16)
    greet_wait(["blk", "grp"])

    @pl.loop(1, n)
    def _(s):
        to = lax.rem(me + s, n)
        remote(stripe_p.at[to], table_p.at[plane, me], send_p, recv_p, "blk", to).start()
        remote(msg_ref.at[to], ids_all.at[message(s)], send_i, recv_i, "blk", to).start()

    @pl.loop(1, n)
    def _(s):
        to = lax.rem(me + s, n)
        remote(stripe_f.at[to], table_f.at[plane, me], send_s, recv_s, "blk", to).start()

    ids_all[0] = msg_ref[me]
    table_p[plane, me] = stripe_p[me]
    table_f[plane, me] = stripe_f[me]
    turned = jnp.transpose(logw_ref[...])
    for i in range(16):
        logw_col[128 * i : 128 * (i + 1), :] = turned[:, i : i + 1]
    for i in range(2):
        logwt[:, 128 * i : 128 * (i + 1)] = logwt_ref[pl.ds(i, held, stride=2), :]
    padded[pl.ds(pairs, 8), :] = jnp.full((8, block), LOWEST, f32)
    copies[2].wait()
    for i in range(0, 2048, 256):
        x_ref[i : i + 256, :] = jnp.transpose(turned_x[:, i : i + 256].astype(f32)).astype(bf16)
    copies[3].wait()
    wait_all(stripe_p, send_p, recv_p, "blk")
    send_all(lambda to: table_p.at[plane], table_p.at[plane], sendx_p, recvx_p, "grp")
    wait_all(ids_all, send_i, recv_i, "blk")
    scalars = pltpu.make_async_copy(ids_all, asked, local.at[0])
    scalars.start()
    ids = ids_all[...].reshape(n, 128).astype(f32)
    turned = jnp.transpose(ids)
    for m in range(n):
        ids_wide[m] = jnp.broadcast_to(turned[0:56, m : m + 1], (56, 128))
    spot = lax.broadcasted_iota(jnp.int32, (16, 128), 1) // 8
    row = lax.broadcasted_iota(jnp.int32, (16, 128), 0)

    @pl.loop(0, n // 2)
    def _(m):
        ids_sel[m] = ids_all[message(lax.rem(me + n - sender(m, me), n))]

    for group in range(2):
        some = ids_sel[16 * group : 16 * group + 16].reshape(16, 128).astype(f32)
        for k in range(7):
            moved = pltpu.roll(some, (128 - 8 * k) % 128, 1)
            moved = pltpu.roll(moved, 0, 1, stride=8, stride_axis=0)
            ids_lane[group, :, 128 * k : 128 * k + 128] = jnp.sum(
                jnp.where(spot == row, moved, 0.0), axis=0, keepdims=True
            ).astype(jnp.int32)
    scalars.wait()
    wait_all(stripe_f, send_s, recv_s, "blk")
    send_all(lambda to: table_f.at[plane], table_f.at[plane], sendx_f, recvx_f, "grp")

    def halve(table, halves):
        width = halves.shape[2]

        @pl.loop(0, planes)
        def _(p):
            for start in range(0, n, 16):
                piece = table[p, pl.ds(start, 16)].astype(f32)
                for h in range(2):
                    at = pl.ds(p * (8 * n) + start * 8, 128)
                    halves[h, at, :] = piece[:, 8 * h : 8 * h + 8].reshape(128, width).astype(bf16)

    def pack(halves, out, then):
        width = halves.shape[2]

        @pl.loop(0, n // 4)
        def _(g):
            ids = ids_wide[pl.ds(4 * g, 4)].reshape(224, 128)[:, 0:1]
            index = lax.broadcasted_iota(jnp.int32, (224, halves.shape[1]), 1)
            hot = (index == ids.astype(jnp.int32)).astype(f32).astype(bf16)
            low = nn(hot, halves[0])
            high = nn(hot, halves[1])
            for d in range(4):
                for k in range(7):
                    at = (d * 7 + k) * 8
                    two = jnp.concatenate([low[at : at + 8], high[at : at + 8]], axis=0)
                    out[4 * g + d, :, k * width : (k + 1) * width] = two.astype(bf16)
                then(4 * g + d)

    def send_points(m):
        @pl.when(m > 0)
        def _():
            to = lax.rem(me + n - away(m), n)
            remote(out_p.at[m], in_p.at[me], send_t, recv_t, "blk", to).start()

    wait_all(table_p, sendx_p, recvx_p, "grp")
    halve(table_p, halves_p)
    pack(halves_p, out_p, send_points)
    in_p[me] = out_p[0]
    wait_all(table_f, sendx_f, recvx_f, "grp")
    halve(table_f, halves_f)
    pack(halves_f, packed_ref, lambda m: None)
    got_ref[me] = packed_ref[0]
    wait_all(in_p, send_t, recv_t, "blk")
    for k in range(7):
        wide[k] = in_p[:, :, 128 * k : 128 * (k + 1)].astype(f32).reshape(n * 16, 128)
        for r in range(8):
            for h in range(2):
                got = wide[k, pl.ds(h * 8 + r, n, stride=16), :].astype(bf16)
                far_ref[r, k, 2 * h * 64 : (2 * h + 1) * 64, :] = got[:, 0:64]
                far_ref[r, k, (2 * h + 1) * 64 : (2 * h + 2) * 64, :] = got[:, 64:128]

    def bulk(first, count):
        @pl.loop(0, count)
        def _(j):
            m = first + j

            @pl.when(m > 0)
            def _():
                to = lax.rem(me + n - away(m), n)
                remote(packed_ref.at[m], got_ref.at[me], send_f, recv_f, "blk", to).start()

    def compute(first, start, count):
        @pl.loop(0, rows)
        def _(r):
            @pl.when(lax.rem(r, 2) == 0)
            def _():
                bulk(start + (r // 2) * count, count)

            at = pl.ds(pl.multiple_of(r * block, block), block)
            x = x_ref[at, :]
            top = None
            for k in range(8):
                t = own_ref[at, :] if k == 0 else far_ref[r, k - 1]
                bias = -squares_row(t) if first else beta_ref[pl.ds(8 * r + k, 1), :]
                z = nt(x, t) * CROSS + bias
                scores[k] = z
                top = z if top is None else jnp.maximum(top, z)
            peak = jnp.max(top, axis=1, keepdims=True)
            weight = None
            for k in range(8):
                e = jnp.exp(scores[k] - peak)
                weight = e if weight is None else weight + e
            alpha = logw_col[at, :] - peak - jnp.log(jnp.sum(weight, axis=1, keepdims=True))
            alpha_ref[at, :] = alpha
            for k in range(8):
                t = own_ref[at, :] if k == 0 else far_ref[r, k - 1]
                v = nt(x, t) * CROSS + alpha
                top = jnp.max(v, axis=0, keepdims=True)
                padded[pl.ds(8 * r + k, 1), :] = top + jnp.log(
                    jnp.sum(jnp.exp(v - top), axis=0, keepdims=True)
                )

    def potentials(turn, start, counts):
        @pl.loop(0, n)
        def _(s):
            to = lax.rem(me + s, n)
            out1[to, 0:1, :] = padded[pl.ds(inv[2 * to], 1), :]
            out1[to, 1:2, :] = padded[pl.ds(inv[2 * to + 1], 1), :]

            @pl.when(s > 0)
            def _():
                remote(out1.at[to], in1.at[message(s)], send1, recv1, "blk", to).start()

        bulk(start, counts[0])
        in1[0] = out1[me]
        own[...] = jnp.full(own.shape, LOWEST, f32)
        for r in range(rows):
            own[pl.ds(plane * rows + r, 1), :] = padded[pl.ds(8 * r, 1), :]
        wait_all(in1, send1, recv1, "blk")
        index = lax.broadcasted_iota(jnp.int32, own.shape, 0)

        def highest(m, best):
            for c in range(2):
                value = in1[m, c : c + 1, :]
                best = jnp.maximum(best, jnp.where(index == asked[m, 0, 56 + c], value, LOWEST))
            return best

        upper[pl.ds(0, held), :] = lax.fori_loop(0, n, highest, own[...])
        upper[pl.ds(held, 8), :] = jnp.zeros((8, block), f32)

        def add(m, so_far):
            for c in range(2):
                slot = asked[m, 0, 56 + c]
                value = jnp.exp(in1[m, c : c + 1, :] - upper[pl.ds(slot, 1), :])
                so_far = so_far + jnp.where(index == slot, value, 0.0)
            return so_far

        top = upper[pl.ds(0, held), :]
        first = jnp.where(own[...] > 0.5 * LOWEST, jnp.exp(own[...] - top), 0.0)
        summed = lax.fori_loop(0, n, add, first)
        part = jnp.where(summed > 0.0, top + jnp.log(jnp.where(summed > 0.0, summed, 1.0)), LOWEST)
        outx[...] = part
        here = inx.at[turn]
        here[plane] = part
        send_all(lambda to: outx, here.at[plane], send2.at[turn], recv2.at[turn], "grp")
        wait_all(here, send2.at[turn], recv2.at[turn], "grp")
        top = inx[turn, 0]
        for p in range(1, planes):
            top = jnp.maximum(top, inx[turn, p])
        summed = jnp.exp(inx[turn, 0] - top)
        for p in range(1, planes):
            summed = summed + jnp.exp(inx[turn, p] - top)
        lse = top + jnp.log(summed)
        both[0, pl.ds(0, held), :] = logwt[...] - lse
        both[1, pl.ds(0, held), :] = lse
        both[:, pl.ds(held, 8), :] = jnp.zeros((2, 8, block), f32)

        @pl.loop(0, n)
        def _(m):
            for c in range(2):
                slot = asked[m, 0, 56 + c]
                out2[m, 2 * c : 2 * c + 1, :] = both[0, pl.ds(slot, 1), :]
                out2[m, 2 * c + 1 : 2 * c + 2, :] = both[1, pl.ds(slot, 1), :]

            @pl.when(m > 0)
            def _():
                to = lax.rem(me + n - away(m), n)
                remote(out2.at[m], in2.at[me], send3, recv3, "blk", to).start()

        bulk(start + counts[0], counts[1])
        in2[me] = out2[0]
        wait_all(in2, send3, recv3, "blk")
        for r in range(rows):
            beta_ref[8 * r : 8 * r + 1, :] = both[0, pl.ds(plane * rows + r, 1), :]
            lse_ref[8 * r : 8 * r + 1, :] = both[1, pl.ds(plane * rows + r, 1), :]
            for k in range(7):
                where = posn[8 * k + r]
                owner = where // 2
                rank = where % 2
                row = 8 * r + k + 1
                beta_ref[row : row + 1, :] = in2[owner, pl.ds(2 * rank, 1), :]
                lse_ref[row : row + 1, :] = in2[owner, pl.ds(2 * rank + 1, 1), :]

    sent = 0
    for turn in range(2):
        per_two, after_ask, after_answer = SCHEDULE[turn]
        compute(turn == 0, sent, per_two)
        sent += 4 * per_two
        potentials(turn, sent, (after_ask, after_answer))
        sent += after_ask + after_answer
    bulk(sent, n - sent)

    few = n // 2

    def parts(h):
        @pl.loop(0, rows)
        def _(r):
            at = pl.ds(pl.multiple_of(r * block, block), block)
            x = x_ref[at, :]
            alpha = alpha_ref[at, :]
            srcf = srcf_ref[at, :]
            half = pl.ds(pl.multiple_of(r * 256 + 128 * h, 128), 128)
            for k in range(8):
                t = own_ref[half, :] if k == 0 else far_ref[r, k - 1, 128 * h : 128 * h + 128, :]
                shift = lse_ref[pl.ds(8 * r + k, 1), :][:, 128 * h : 128 * h + 128]
                w = jnp.exp(nt(x, t) * CROSS + alpha - shift).astype(bf16)
                part = tn(w, srcf).astype(bf16).astype(f32)
                if k == 0:
                    diag[half, :] = part
                else:
                    for d in range(2):
                        for c in range(2):
                            at = 64 * d + 32 * c
                            to = pl.ds(512 * d + 8 * c + r, few, stride=16)
                            wide[k - 1, to, :] = part[at : at + 32]

        for k in range(7):
            for d in range(2):
                lanes = 128 * (7 * d + k)
                value = wide[k, 512 * d : 512 * (d + 1), :].reshape(few, 16, 128)
                out_h[h, :, :, lanes : lanes + 128] = value.astype(bf16)
        @pl.loop(1, few)
        def _(m):
            to = holder(m, me)
            remote(
                out_h.at[h, stripe(to)],
                in_h.at[h, m],
                send_m.at[h],
                recv_m.at[h, m // 16],
                "blk",
                to,
            ).start()

        in_h[h, 0] = out_h[h, stripe(me)]

    def move_rows():
        wait_all(got_ref, send_f, recv_f, "blk")
        for k in range(7):
            for c in range(2):
                lanes = 128 * (2 * k + c)
                buffer = (2 * k + c) % 7
                wide[buffer] = got_ref[:, :, lanes : lanes + 128].astype(f32).reshape(16 * n, 128)
                for r in range(8):
                    for h in range(2):
                        got = wide[buffer, pl.ds(h * 8 + r, n, stride=16), :]
                        farf[r, k, 64 * (2 * h + c) : 64 * (2 * h + c + 1), :] = got.astype(bf16)

        @pl.loop(0, rows)
        def _(r):
            at = pl.ds(pl.multiple_of(r * block, block), block)
            x = x_ref[at, :]
            top = None
            for k in range(8):
                t = own_ref[at, :] if k == 0 else far_ref[r, k - 1]
                z = nt(x, t) * CROSS + beta_ref[pl.ds(8 * r + k, 1), :]
                scores[k] = z
                top = z if top is None else jnp.maximum(top, z)
            peak = jnp.max(top, axis=1, keepdims=True)
            weight = None
            mixed = None
            for k in range(8):
                e = jnp.exp(scores[k] - peak)
                weight = e if weight is None else weight + e
                feats = ownf_ref[at, :] if k == 0 else farf[r, k - 1]
                term = nn(e.astype(bf16), feats)
                mixed = term if mixed is None else mixed + term
            moved_ref[at, :] = (mixed / jnp.sum(weight, axis=1, keepdims=True)).astype(bf16)

    def collect(h, group):
        count = 16 - (1 if group == 0 else 0)
        messages(in_h.at[h], count, send_m.at[h], recv_m.at[h, group], "blk").wait_recv()

        @pl.loop(0, 8)
        def _(pair):
            one = in_h[h, 16 * group + 2 * pair].astype(f32)
            two = in_h[h, 16 * group + 2 * pair + 1].astype(f32)
            for k in range(7):
                for d in range(2):
                    for c in range(2):
                        lanes = slice(128 * (7 * d + k), 128 * (7 * d + k + 1))
                        joined = jnp.concatenate(
                            [one[8 * c : 8 * c + 8, lanes], two[8 * c : 8 * c + 8, lanes]], axis=0
                        )
                        at = pl.ds(pl.multiple_of(128 * k + 16 * pair, 16), 16)
                        pieces[at, 128 * (2 * d + c) : 128 * (2 * d + c + 1)] = joined.astype(bf16)

        @pl.loop(0, 8)
        def _(i):
            at = pl.ds(pl.multiple_of(256 * i, 256), 256)
            index = lax.broadcasted_iota(jnp.int32, (256, 896), 0) + 256 * i
            hot = (index == ids_lane[group]).astype(f32).astype(bf16)
            term = nn(hot, pieces[...])
            if group == 0:
                total[at, :] = term
            else:
                total[at, :] += term

    def spread(h):
        for p in range(planes):
            out_x[p] = total[512 * p : 512 * (p + 1), :].astype(bf16)
        in_x[h, plane] = out_x[plane]
        send_all(lambda to: out_x.at[to], in_x.at[h, plane], send_x.at[h], recv_x.at[h], "grp")

    def finish(h):
        wait_all(in_x.at[h], send_x.at[h], recv_x.at[h], "grp")
        added = in_x[h, 0].astype(f32)
        for p in range(1, planes):
            added = added + in_x[h, p].astype(f32)
        for d in range(2):
            joined = jnp.concatenate(
                [
                    added[:, 128 * (2 * d + c) : 128 * (2 * d + c + 1)].reshape(n, 8, 128)
                    for c in range(2)
                ],
                axis=1,
            )
            out_f[h, :, :, 128 * d : 128 * (d + 1)] = joined.astype(bf16)
        send_all(lambda to: out_f.at[h, to], in_f.at[h, me], send_o.at[h], recv_o.at[h], "blk")
        in_f[h, me] = out_f[h, me]

    def deliver(h):
        wait_all(in_f.at[h], send_o.at[h], recv_o.at[h], "blk")
        for d in range(2):
            lanes = slice(128 * d, 128 * (d + 1))
            added = in_f[h, 0:few, :, lanes].astype(f32) + in_f[h, few:n, :, lanes].astype(f32)
            wide[h, 512 * d : 512 * (d + 1), :] = added.reshape(16 * few, 128)
            for s in range(8):
                for c in range(2):
                    at = 256 * s + 128 * h + 64 * d + 32 * c
                    got = wide[h, pl.ds(512 * d + 8 * c + s, few, stride=16), :]
                    out_ref[at : at + 32, :] = (got + diag[at : at + 32, :]).astype(bf16)

    parts(0)
    parts(1)
    move_rows()
    collect(0, 0)
    collect(0, 1)
    spread(0)
    collect(1, 0)
    collect(1, 1)
    finish(0)
    spread(1)
    finish(1)
    deliver(0)
    deliver(1)
    for h in range(2):
        messages(out_h.at[h], few - 1, send_m.at[h], recv_m.at[h, 0], "blk").wait_send()


def whole(inv, posn, msg, x, ownp, logw, logwt, srcf, tfeats, cid):
    n = lax.axis_size("blk")
    planes = lax.axis_size("grp")
    pairs, block = 64, 256
    held = 32
    smem = pl.BlockSpec(memory_space=pltpu.SMEM)
    vmem = pl.BlockSpec(memory_space=pltpu.VMEM)
    hbm = pl.BlockSpec(memory_space=pl.ANY)
    scratch = [
        ((64, 2048), bf16),
        ((64, 2048), bf16),
        ((held, block), f32),
        ((2048, 64), bf16),
        ((2048, 64), bf16),
        ((2048, 128), bf16),
        ((2048, 128), bf16),
        ((n, 16, 128), bf16),
        ((n, 16, 256), bf16),
        ((2048, 1), f32),
        ((2048, 1), f32),
        ((n, 1, 128), jnp.int32),
        ((n // 2, 1, 128), jnp.int32),
        ((n, 56, 128), f32),
        ((2, 1, 896), jnp.int32),
        None,
        ((planes, n, 16, 128), bf16),
        ((planes, n, 16, 256), bf16),
        ((2, planes * 8 * n, 128), bf16),
        ((2, planes * 8 * n, 256), bf16),
        ((n, 16, 7 * 128), bf16),
        ((n, 16, 7 * 128), bf16),
        ((8, 7, 256, 64), bf16),
        ((n, 16, 7 * 256), bf16),
        ((n, 16, 7 * 256), bf16),
        ((8, block, block), f32),
        ((pairs, block), f32),
        ((pairs, block), f32),
        ((pairs + 8, block), f32),
        ((n, 2, block), f32),
        ((n, 2, block), f32),
        ((held, block), f32),
        ((held + 8, block), f32),
        ((held, block), f32),
        ((2, planes, held, block), f32),
        ((2, held + 8, block), f32),
        ((n, 4, block), f32),
        ((n, 4, block), f32),
        ((8, 7, 256, 128), bf16),
        ((7, 16 * n, 128), f32),
        ((2048, 128), f32),
        ((2, n // 2, 16, 1792), bf16),
        ((2, n // 2, 16, 1792), bf16),
        ((896, 512), bf16),
        ((planes * 8 * n, 512), f32),
        ((planes, 8 * n, 512), bf16),
        ((2, planes, 8 * n, 512), bf16),
        ((2, n, 16, 256), bf16),
        ((2, n, 16, 256), bf16),
    ]
    dma = pltpu.SemaphoreType.DMA
    return pl.pallas_call(
        whole_kernel,
        out_shape=(
            jax.ShapeDtypeStruct((2048, 128), bf16),
            jax.ShapeDtypeStruct((2048, 128), bf16),
        ),
        in_specs=[smem, smem, vmem, hbm, hbm, vmem, vmem, hbm, hbm],
        out_specs=(vmem,) * 2,
        scratch_shapes=[
            pltpu.SMEM((n, 1, 128), jnp.int32) if item is None else pltpu.VMEM(*item)
            for item in scratch
        ]
        + [dma((4,))]
        + [dma] * 14
        + [dma] * 4
        + [dma((2,))] * 2
        + [dma((2,)), dma((2, 2))]
        + [dma((2,))] * 4,
        compiler_params=params(cid, 62),
    )(inv, posn, msg, x, ownp, logw, logwt, srcf, tfeats)


def shards(
    source_points, target_points, source_logw, target_logw,
    source_feats, target_feats, pair_owner, pair_slot,
):
    n = lax.axis_size("blk")
    owners = pair_owner.T.reshape(56)
    slots = pair_slot.T.reshape(56)
    ids = (slots // 8) * (8 * n) + owners * 8 + slots % 8
    earlier = jnp.tril(jnp.ones((56, 56), bool), -1) & (owners[:, None] == owners[None, :])
    posn = owners * 2 + jnp.sum(earlier.astype(jnp.int32), axis=1)
    order = jnp.arange(56, dtype=jnp.int32)
    row_of = (order % 8) * 8 + order // 8 + 1
    at = posn[None, :] == jnp.arange(2 * n, dtype=jnp.int32)[:, None]
    inv = jnp.min(jnp.where(at, row_of[None, :], 64), axis=1)
    asked = jnp.min(jnp.where(at, slots[None, :], 32), axis=1).reshape(n, 2)
    msg = jnp.concatenate(
        [jnp.broadcast_to(ids[None], (n, 56)), asked, jnp.zeros((n, 70), jnp.int32)], axis=1
    ).reshape(n, 1, 128)
    return whole(
        inv, posn, msg, source_points.T, target_points.T, source_logw.reshape(16, 128),
        target_logw.reshape(64, 128), source_feats, target_feats, 0,
    )


def solution(mesh):
    return jax.shard_map(
        shards,
        mesh=mesh,
        in_specs=(
            P(("blk", "grp"), None),
            P("blk", None),
            P(("blk", "grp")),
            P("blk"),
            P(("blk", "grp"), None),
            P("blk", None),
            P(("blk", "grp"), None),
            P(("blk", "grp"), None),
        ),
        out_specs=(P(("blk", "grp"), None), P(("blk", "grp"), None)),
        check_vma=False,
    )
```

```python
import functools
import jax
import jax.numpy as jnp
from jax import lax
from jax.experimental import pallas as pl
from jax.experimental.pallas import tpu as pltpu
from jax.sharding import PartitionSpec as P

LOWEST = -1e30
CROSS = 0.3125
SQUARE = 0.15625
MESH = pl.DeviceIdType.MESH
MIB = 2**20
SCHEDULE = ((3, 10, 8), (3, 10, 8))
f32 = jnp.float32
bf16 = jnp.bfloat16


def params(cid=None, vmem=48):
    if cid is None:
        return pltpu.CompilerParams(vmem_limit_bytes=vmem * MIB)
    return pltpu.CompilerParams(
        collective_id=cid, has_side_effects=True, vmem_limit_bytes=vmem * MIB
    )


def nt(a, b):
    return lax.dot_general(a, b, (((1,), (1,)), ((), ())), preferred_element_type=f32)


def tn(a, b):
    return lax.dot_general(a, b, (((0,), (0,)), ((), ())), preferred_element_type=f32)


def nn(a, b):
    return jnp.dot(a, b, preferred_element_type=f32)


def greet_signal(axes):
    bar = pltpu.get_barrier_semaphore()
    for name in axes:
        n = lax.axis_size(name)
        me = lax.axis_index(name)

        @pl.loop(1, n)
        def _(s):
            pl.semaphore_signal(
                bar, inc=1, device_id={name: lax.rem(me + s, n)}, device_id_type=MESH
            )


def greet_wait(axes):
    total = sum(lax.axis_size(name) - 1 for name in axes)
    pl.semaphore_wait(pltpu.get_barrier_semaphore(), total)


def remote(src, dst, send, recv, axis, to):
    return pltpu.make_async_remote_copy(
        src_ref=src,
        dst_ref=dst,
        send_sem=send,
        recv_sem=recv,
        device_id={axis: to},
        device_id_type=MESH,
    )


def send_all(src, dst, send, recv, axis):
    n = lax.axis_size(axis)
    me = lax.axis_index(axis)

    @pl.loop(1, n)
    def _(s):
        to = lax.rem(me + s, n)
        remote(src(to), dst, send, recv, axis, to).start()


def messages(ref, count, send, recv, axis):
    part = ref.at[pl.ds(0, count)]
    n = lax.axis_size(axis)
    return remote(part, part, send, recv, axis, lax.rem(lax.axis_index(axis) + 1, n))


def wait_all(ref, send, recv, axis):
    every = messages(ref, lax.axis_size(axis) - 1, send, recv, axis)
    every.wait_send()
    every.wait_recv()


def away(m):
    place = lax.rem(m, 8)
    return 8 * (2 * lax.rem(place, 4) + place // 4) + m // 8


def holder(m, me):
    z, yc = me // 8, lax.rem(me, 8)
    return 8 * lax.rem(z + 8 + along(m, yc), 8) + lax.rem(yc + m // 4, 8)


def sender(m, me):
    z, yc = me // 8, lax.rem(lax.rem(me, 8) + 8 - m // 4, 8)
    return 8 * lax.rem(z + 8 - along(m, yc), 8) + yc


def along(m, yc):
    turn = lax.rem(m, 4)
    two = (turn // 2) * (1 - turn // 3)
    return turn - 4 * (turn // 3) - 4 * two * lax.rem(yc, 2)


def stripe(device):
    return 8 * lax.rem(device // 8, 4) + lax.rem(device, 8)


def message(s):
    z = s // 8
    return 8 * lax.rem(s, 8) + z // 2 + 4 * lax.rem(z, 2)


def squares_row(t):
    wide = t.astype(f32)
    square = wide * wide
    high = square.astype(bf16)
    low = (square - high.astype(f32)).astype(bf16)
    ones = jnp.ones((8, t.shape[1]), bf16)
    return SQUARE * (nt(ones, high) + nt(ones, low))[0:1]


def whole_kernel(
    inv, posn, msg_ref, x_hbm, ownp_hbm, logw_ref, logwt_ref, srcf_hbm, tfeats_hbm,
    moved_ref, out_ref,
    turned_x, turned_own, logwt, x_ref, own_ref, srcf_ref, ownf_ref, stripe_p, stripe_f, logw_col, alpha_ref,
    ids_all, ids_sel, ids_wide, ids_lane, asked, table_p, table_f, halves_p, halves_f, out_p, in_p,
    far_ref, packed_ref, got_ref, scores, beta_ref, lse_ref,
    padded, out1, in1, own, upper, outx, inx, both, out2, in2,
    farf, wide, diag, out_h, in_h, pieces, total, out_x, in_x, out_f, in_f,
    local, send_i, recv_i, send_p, recv_p, send_t, recv_t, send_f, recv_f,
    send1, recv1, send3, recv3, send_s, recv_s,
    sendx_p, recvx_p, sendx_f, recvx_f, send2, recv2,
    send_m, recv_m, send_x, recv_x, send_o, recv_o,
):
    n = lax.axis_size("blk")
    me = lax.axis_index("blk")
    plane = lax.axis_index("grp")
    pairs, block = beta_ref.shape
    rows = pairs // 8
    held = own.shape[0]
    planes = table_p.shape[0]
    mine = pl.ds(pl.multiple_of(plane * 2048, 2048), 2048)
    copies = [
        pltpu.make_async_copy(src, dst, local.at[i])
        for i, (src, dst) in enumerate(
            [
                (ownp_hbm.at[:, mine], turned_own),
                (tfeats_hbm.at[mine], ownf_ref),
                (x_hbm, turned_x),
                (srcf_hbm, srcf_ref),
            ]
        )
    ]
    for copy in copies:
        copy.start()
    greet_signal(["blk", "grp"])

    copies[0].wait()
    for i in range(0, 2048, 256):
        own_ref[i : i + 256, :] = jnp.transpose(turned_own[:, i : i + 256].astype(f32)).astype(bf16)
    for s in range(8):
        for h in range(2):
            at = 256 * s + 128 * h
            pair = [own_ref[at + 64 * c : at + 64 * c + 64, :].astype(f32) for c in range(2)]
            wide[0, pl.ds(h * 8 + s, n, stride=16), :] = jnp.concatenate(pair, axis=1)
    stripe_p[...] = wide[0].reshape(n, 16, 128).astype(bf16)
    copies[1].wait()
    for c in range(2):
        for s in range(8):
            for h in range(2):
                at = 256 * s + 128 * h + 64 * c
                wide[1 + c, pl.ds(h * 8 + s, n, stride=16), :] = ownf_ref[at : at + 64, :].astype(f32)
        stripe_f[:, :, 128 * c : 128 * c + 128] = wide[1 + c].reshape(n, 16, 128).astype(bf16)
    greet_wait(["blk", "grp"])

    @pl.loop(1, n)
    def _(s):
        to = lax.rem(me + s, n)
        remote(stripe_p.at[to], table_p.at[plane, me], send_p, recv_p, "blk", to).start()
        remote(msg_ref.at[to], ids_all.at[message(s)], send_i, recv_i, "blk", to).start()

    @pl.loop(1, n)
    def _(s):
        to = lax.rem(me + s, n)
        remote(stripe_f.at[to], table_f.at[plane, me], send_s, recv_s, "blk", to).start()

    ids_all[0] = msg_ref[me]
    table_p[plane, me] = stripe_p[me]
    table_f[plane, me] = stripe_f[me]
    turned = jnp.transpose(logw_ref[...])
    for i in range(16):
        logw_col[128 * i : 128 * (i + 1), :] = turned[:, i : i + 1]
    for i in range(2):
        logwt[:, 128 * i : 128 * (i + 1)] = logwt_ref[pl.ds(i, held, stride=2), :]
    padded[pl.ds(pairs, 8), :] = jnp.full((8, block), LOWEST, f32)
    copies[2].wait()
    for i in range(0, 2048, 256):
        x_ref[i : i + 256, :] = jnp.transpose(turned_x[:, i : i + 256].astype(f32)).astype(bf16)
    copies[3].wait()
    wait_all(stripe_p, send_p, recv_p, "blk")
    send_all(lambda to: table_p.at[plane], table_p.at[plane], sendx_p, recvx_p, "grp")
    wait_all(ids_all, send_i, recv_i, "blk")
    scalars = pltpu.make_async_copy(ids_all, asked, local.at[0])
    scalars.start()
    ids = ids_all[...].reshape(n, 128).astype(f32)
    turned = jnp.transpose(ids)
    for m in range(n):
        ids_wide[m] = jnp.broadcast_to(turned[0:56, m : m + 1], (56, 128))
    spot = lax.broadcasted_iota(jnp.int32, (16, 128), 1) // 8
    row = lax.broadcasted_iota(jnp.int32, (16, 128), 0)

    @pl.loop(0, n // 2)
    def _(m):
        ids_sel[m] = ids_all[message(lax.rem(me + n - sender(m, me), n))]

    for group in range(2):
        some = ids_sel[16 * group : 16 * group + 16].reshape(16, 128).astype(f32)
        for k in range(7):
            moved = pltpu.roll(some, (128 - 8 * k) % 128, 1)
            moved = pltpu.roll(moved, 0, 1, stride=8, stride_axis=0)
            ids_lane[group, :, 128 * k : 128 * k + 128] = jnp.sum(
                jnp.where(spot == row, moved, 0.0), axis=0, keepdims=True
            ).astype(jnp.int32)
    scalars.wait()
    wait_all(stripe_f, send_s, recv_s, "blk")
    send_all(lambda to: table_f.at[plane], table_f.at[plane], sendx_f, recvx_f, "grp")

    def halve(table, halves):
        width = halves.shape[2]

        @pl.loop(0, planes)
        def _(p):
            for start in range(0, n, 16):
                piece = table[p, pl.ds(start, 16)].astype(f32)
                for h in range(2):
                    at = pl.ds(p * (8 * n) + start * 8, 128)
                    halves[h, at, :] = piece[:, 8 * h : 8 * h + 8].reshape(128, width).astype(bf16)

    def pack(halves, out, then):
        width = halves.shape[2]

        @pl.loop(0, n // 4)
        def _(g):
            ids = ids_wide[pl.ds(4 * g, 4)].reshape(224, 128)[:, 0:1]
            index = lax.broadcasted_iota(jnp.int32, (224, halves.shape[1]), 1)
            hot = (index == ids.astype(jnp.int32)).astype(f32).astype(bf16)
            low = nn(hot, halves[0])
            high = nn(hot, halves[1])
            for d in range(4):
                for k in range(7):
                    at = (d * 7 + k) * 8
                    two = jnp.concatenate([low[at : at + 8], high[at : at + 8]], axis=0)
                    out[4 * g + d, :, k * width : (k + 1) * width] = two.astype(bf16)
                then(4 * g + d)

    def send_points(m):
        @pl.when(m > 0)
        def _():
            to = lax.rem(me + n - away(m), n)
            remote(out_p.at[m], in_p.at[me], send_t, recv_t, "blk", to).start()

    wait_all(table_p, sendx_p, recvx_p, "grp")
    halve(table_p, halves_p)
    pack(halves_p, out_p, send_points)
    in_p[me] = out_p[0]
    wait_all(table_f, sendx_f, recvx_f, "grp")
    halve(table_f, halves_f)
    pack(halves_f, packed_ref, lambda m: None)
    got_ref[me] = packed_ref[0]
    wait_all(in_p, send_t, recv_t, "blk")
    for k in range(7):
        wide[k] = in_p[:, :, 128 * k : 128 * (k + 1)].astype(f32).reshape(n * 16, 128)
        for r in range(8):
            for h in range(2):
                got = wide[k, pl.ds(h * 8 + r, n, stride=16), :].astype(bf16)
                far_ref[r, k, 2 * h * 64 : (2 * h + 1) * 64, :] = got[:, 0:64]
                far_ref[r, k, (2 * h + 1) * 64 : (2 * h + 2) * 64, :] = got[:, 64:128]

    def bulk(first, count):
        @pl.loop(0, count)
        def _(j):
            m = first + j

            @pl.when(m > 0)
            def _():
                to = lax.rem(me + n - away(m), n)
                remote(packed_ref.at[m], got_ref.at[me], send_f, recv_f, "blk", to).start()

    def compute(first, start, count):
        @pl.loop(0, rows)
        def _(r):
            @pl.when(lax.rem(r, 2) == 0)
            def _():
                bulk(start + (r // 2) * count, count)

            at = pl.ds(pl.multiple_of(r * block, block), block)
            x = x_ref[at, :]
            top = None
            for k in range(8):
                t = own_ref[at, :] if k == 0 else far_ref[r, k - 1]
                bias = -squares_row(t) if first else beta_ref[pl.ds(8 * r + k, 1), :]
                z = nt(x, t) * CROSS + bias
                scores[k] = z
                top = z if top is None else jnp.maximum(top, z)
            peak = jnp.max(top, axis=1, keepdims=True)
            weight = None
            for k in range(8):
                e = jnp.exp(scores[k] - peak)
                weight = e if weight is None else weight + e
            alpha = logw_col[at, :] - peak - jnp.log(jnp.sum(weight, axis=1, keepdims=True))
            alpha_ref[at, :] = alpha
            for k in range(8):
                t = own_ref[at, :] if k == 0 else far_ref[r, k - 1]
                v = nt(x, t) * CROSS + alpha
                top = jnp.max(v, axis=0, keepdims=True)
                padded[pl.ds(8 * r + k, 1), :] = top + jnp.log(
                    jnp.sum(jnp.exp(v - top), axis=0, keepdims=True)
                )

    def potentials(turn, start, counts):
        @pl.loop(0, n)
        def _(s):
            to = lax.rem(me + s, n)
            out1[to, 0:1, :] = padded[pl.ds(inv[2 * to], 1), :]
            out1[to, 1:2, :] = padded[pl.ds(inv[2 * to + 1], 1), :]

            @pl.when(s > 0)
            def _():
                remote(out1.at[to], in1.at[message(s)], send1, recv1, "blk", to).start()

        bulk(start, counts[0])
        in1[0] = out1[me]
        own[...] = jnp.full(own.shape, LOWEST, f32)
        for r in range(rows):
            own[pl.ds(plane * rows + r, 1), :] = padded[pl.ds(8 * r, 1), :]
        wait_all(in1, send1, recv1, "blk")
        index = lax.broadcasted_iota(jnp.int32, own.shape, 0)

        def highest(m, best):
            for c in range(2):
                value = in1[m, c : c + 1, :]
                best = jnp.maximum(best, jnp.where(index == asked[m, 0, 56 + c], value, LOWEST))
            return best

        upper[pl.ds(0, held), :] = lax.fori_loop(0, n, highest, own[...])
        upper[pl.ds(held, 8), :] = jnp.zeros((8, block), f32)

        def add(m, so_far):
            for c in range(2):
                slot = asked[m, 0, 56 + c]
                value = jnp.exp(in1[m, c : c + 1, :] - upper[pl.ds(slot, 1), :])
                so_far = so_far + jnp.where(index == slot, value, 0.0)
            return so_far

        top = upper[pl.ds(0, held), :]
        first = jnp.where(own[...] > 0.5 * LOWEST, jnp.exp(own[...] - top), 0.0)
        summed = lax.fori_loop(0, n, add, first)
        part = jnp.where(summed > 0.0, top + jnp.log(jnp.where(summed > 0.0, summed, 1.0)), LOWEST)
        outx[...] = part
        here = inx.at[turn]
        here[plane] = part
        send_all(lambda to: outx, here.at[plane], send2.at[turn], recv2.at[turn], "grp")
        wait_all(here, send2.at[turn], recv2.at[turn], "grp")
        top = inx[turn, 0]
        for p in range(1, planes):
            top = jnp.maximum(top, inx[turn, p])
        summed = jnp.exp(inx[turn, 0] - top)
        for p in range(1, planes):
            summed = summed + jnp.exp(inx[turn, p] - top)
        lse = top + jnp.log(summed)
        both[0, pl.ds(0, held), :] = logwt[...] - lse
        both[1, pl.ds(0, held), :] = lse
        both[:, pl.ds(held, 8), :] = jnp.zeros((2, 8, block), f32)

        @pl.loop(0, n)
        def _(m):
            for c in range(2):
                slot = asked[m, 0, 56 + c]
                out2[m, 2 * c : 2 * c + 1, :] = both[0, pl.ds(slot, 1), :]
                out2[m, 2 * c + 1 : 2 * c + 2, :] = both[1, pl.ds(slot, 1), :]

            @pl.when(m > 0)
            def _():
                to = lax.rem(me + n - away(m), n)
                remote(out2.at[m], in2.at[me], send3, recv3, "blk", to).start()

        bulk(start + counts[0], counts[1])
        in2[me] = out2[0]
        wait_all(in2, send3, recv3, "blk")
        for r in range(rows):
            beta_ref[8 * r : 8 * r + 1, :] = both[0, pl.ds(plane * rows + r, 1), :]
            lse_ref[8 * r : 8 * r + 1, :] = both[1, pl.ds(plane * rows + r, 1), :]
            for k in range(7):
                where = posn[8 * k + r]
                owner = where // 2
                rank = where % 2
                row = 8 * r + k + 1
                beta_ref[row : row + 1, :] = in2[owner, pl.ds(2 * rank, 1), :]
                lse_ref[row : row + 1, :] = in2[owner, pl.ds(2 * rank + 1, 1), :]

    sent = 0
    for turn in range(2):
        per_two, after_ask, after_answer = SCHEDULE[turn]
        compute(turn == 0, sent, per_two)
        sent += 4 * per_two
        potentials(turn, sent, (after_ask, after_answer))
        sent += after_ask + after_answer

    few = n // 2

    def parts(h):
        @pl.loop(0, rows)
        def _(r):
            at = pl.ds(pl.multiple_of(r * block, block), block)
            x = x_ref[at, :]
            alpha = alpha_ref[at, :]
            srcf = srcf_ref[at, :]
            half = pl.ds(pl.multiple_of(r * 256 + 128 * h, 128), 128)
            for k in range(8):
                t = own_ref[half, :] if k == 0 else far_ref[r, k - 1, 128 * h : 128 * h + 128, :]
                shift = lse_ref[pl.ds(8 * r + k, 1), :][:, 128 * h : 128 * h + 128]
                w = jnp.exp(nt(x, t) * CROSS + alpha - shift).astype(bf16)
                part = tn(w, srcf).astype(bf16).astype(f32)
                if k == 0:
                    diag[half, :] = part
                else:
                    for d in range(2):
                        for c in range(2):
                            at = 64 * d + 32 * c
                            to = pl.ds(512 * d + 8 * c + r, few, stride=16)
                            wide[k - 1, to, :] = part[at : at + 32]

        for k in range(7):
            for d in range(2):
                lanes = 128 * k
                value = wide[k, 512 * d : 512 * (d + 1), :].reshape(few, 16, 128)
                out_h[2 * h + d, :, :, lanes : lanes + 128] = value.astype(bf16)
        for q in (2 * h, 2 * h + 1):

            @pl.loop(1, few)
            def _(m):
                to = holder(m, me)
                remote(
                    out_h.at[q, stripe(to)],
                    in_h.at[q, m],
                    send_m.at[q],
                    recv_m.at[q, m // 16],
                    "blk",
                    to,
                ).start()

            in_h[q, 0] = out_h[q, stripe(me)]

    def move_rows():
        wait_all(got_ref, send_f, recv_f, "blk")
        for k in range(7):
            for c in range(2):
                lanes = 128 * (2 * k + c)
                buffer = (2 * k + c) % 7
                wide[buffer] = got_ref[:, :, lanes : lanes + 128].astype(f32).reshape(16 * n, 128)
                for r in range(8):
                    for h in range(2):
                        got = wide[buffer, pl.ds(h * 8 + r, n, stride=16), :]
                        farf[r, k, 64 * (2 * h + c) : 64 * (2 * h + c + 1), :] = got.astype(bf16)

        @pl.loop(0, rows)
        def _(r):
            at = pl.ds(pl.multiple_of(r * block, block), block)
            x = x_ref[at, :]
            top = None
            for k in range(8):
                t = own_ref[at, :] if k == 0 else far_ref[r, k - 1]
                z = nt(x, t) * CROSS + beta_ref[pl.ds(8 * r + k, 1), :]
                scores[k] = z
                top = z if top is None else jnp.maximum(top, z)
            peak = jnp.max(top, axis=1, keepdims=True)
            weight = None
            mixed = None
            for k in range(8):
                e = jnp.exp(scores[k] - peak)
                weight = e if weight is None else weight + e
                feats = ownf_ref[at, :] if k == 0 else farf[r, k - 1]
                term = nn(e.astype(bf16), feats)
                mixed = term if mixed is None else mixed + term
            moved_ref[at, :] = (mixed / jnp.sum(weight, axis=1, keepdims=True)).astype(bf16)

    def collect(q):
        for group in range(2):
            count = 16 - (1 if group == 0 else 0)
            messages(in_h.at[q], count, send_m.at[q], recv_m.at[q, group], "blk").wait_recv()

            @pl.loop(0, 8)
            def _(pair):
                one = in_h[q, 16 * group + 2 * pair].astype(f32)
                two = in_h[q, 16 * group + 2 * pair + 1].astype(f32)
                for k in range(7):
                    for c in range(2):
                        lanes = slice(128 * k, 128 * (k + 1))
                        joined = jnp.concatenate(
                            [one[8 * c : 8 * c + 8, lanes], two[8 * c : 8 * c + 8, lanes]], axis=0
                        )
                        at = pl.ds(pl.multiple_of(128 * k + 16 * pair, 16), 16)
                        pieces[at, 128 * c : 128 * (c + 1)] = joined.astype(bf16)

            @pl.loop(0, 8)
            def _(i):
                at = pl.ds(pl.multiple_of(256 * i, 256), 256)
                index = lax.broadcasted_iota(jnp.int32, (256, 896), 0) + 256 * i
                hot = (index == ids_lane[group]).astype(f32).astype(bf16)
                term = nn(hot, pieces[...])
                if group == 0:
                    total[at, :] = term
                else:
                    total[at, :] += term

    def spread(q):
        out = out_x.at[q % 2]
        for p in range(planes):
            out[p] = total[512 * p : 512 * (p + 1), :].astype(bf16)
        in_x[q, plane] = out[plane]
        send_all(lambda to: out.at[to], in_x.at[q, plane], send_x.at[q], recv_x.at[q], "grp")

    def finish(q):
        wait_all(in_x.at[q], send_x.at[q], recv_x.at[q], "grp")
        added = in_x[q, 0].astype(f32)
        for p in range(1, planes):
            added = added + in_x[q, p].astype(f32)
        joined = jnp.concatenate(
            [added[:, 128 * c : 128 * (c + 1)].reshape(n, 8, 128) for c in range(2)], axis=1
        )
        out_f[q] = joined.astype(bf16)
        send_all(lambda to: out_f.at[q, to], in_f.at[q, me], send_o.at[q], recv_o.at[q], "blk")
        in_f[q, me] = out_f[q, me]

    def deliver(q):
        wait_all(in_f.at[q], send_o.at[q], recv_o.at[q], "blk")
        added = in_f[q, 0:few].astype(f32) + in_f[q, few:n].astype(f32)
        wide[q, 0:512, :] = added.reshape(16 * few, 128)
        for s in range(8):
            for c in range(2):
                at = 256 * s + 64 * q + 32 * c
                got = wide[q, pl.ds(8 * c + s, few, stride=16), :]
                out_ref[at : at + 32, :] = (got + diag[at : at + 32, :]).astype(bf16)

    parts(0)
    parts(1)
    bulk(sent, n - sent)
    collect(0)
    spread(0)
    collect(1)
    spread(1)
    finish(0)
    collect(2)
    spread(2)
    finish(1)
    collect(3)
    spread(3)
    move_rows()
    finish(2)
    finish(3)
    for q in range(4):
        deliver(q)
    for q in range(4):
        messages(out_h.at[q], few - 1, send_m.at[q], recv_m.at[q, 0], "blk").wait_send()


def whole(inv, posn, msg, x, ownp, logw, logwt, srcf, tfeats, cid):
    n = lax.axis_size("blk")
    planes = lax.axis_size("grp")
    pairs, block = 64, 256
    held = 32
    smem = pl.BlockSpec(memory_space=pltpu.SMEM)
    vmem = pl.BlockSpec(memory_space=pltpu.VMEM)
    hbm = pl.BlockSpec(memory_space=pl.ANY)
    scratch = [
        ((64, 2048), bf16),
        ((64, 2048), bf16),
        ((held, block), f32),
        ((2048, 64), bf16),
        ((2048, 64), bf16),
        ((2048, 128), bf16),
        ((2048, 128), bf16),
        ((n, 16, 128), bf16),
        ((n, 16, 256), bf16),
        ((2048, 1), f32),
        ((2048, 1), f32),
        ((n, 1, 128), jnp.int32),
        ((n // 2, 1, 128), jnp.int32),
        ((n, 56, 128), f32),
        ((2, 1, 896), jnp.int32),
        None,
        ((planes, n, 16, 128), bf16),
        ((planes, n, 16, 256), bf16),
        ((2, planes * 8 * n, 128), bf16),
        ((2, planes * 8 * n, 256), bf16),
        ((n, 16, 7 * 128), bf16),
        ((n, 16, 7 * 128), bf16),
        ((8, 7, 256, 64), bf16),
        ((n, 16, 7 * 256), bf16),
        ((n, 16, 7 * 256), bf16),
        ((8, block, block), f32),
        ((pairs, block), f32),
        ((pairs, block), f32),
        ((pairs + 8, block), f32),
        ((n, 2, block), f32),
        ((n, 2, block), f32),
        ((held, block), f32),
        ((held + 8, block), f32),
        ((held, block), f32),
        ((2, planes, held, block), f32),
        ((2, held + 8, block), f32),
        ((n, 4, block), f32),
        ((n, 4, block), f32),
        ((8, 7, 256, 128), bf16),
        ((7, 16 * n, 128), f32),
        ((2048, 128), f32),
        ((4, n // 2, 16, 896), bf16),
        ((4, n // 2, 16, 896), bf16),
        ((896, 256), bf16),
        ((planes * 8 * n, 256), f32),
        ((2, planes, 8 * n, 256), bf16),
        ((4, planes, 8 * n, 256), bf16),
        ((4, n, 16, 128), bf16),
        ((4, n, 16, 128), bf16),
    ]
    dma = pltpu.SemaphoreType.DMA
    return pl.pallas_call(
        whole_kernel,
        out_shape=(
            jax.ShapeDtypeStruct((2048, 128), bf16),
            jax.ShapeDtypeStruct((2048, 128), bf16),
        ),
        in_specs=[smem, smem, vmem, hbm, hbm, vmem, vmem, hbm, hbm],
        out_specs=(vmem,) * 2,
        scratch_shapes=[
            pltpu.SMEM((n, 1, 128), jnp.int32) if item is None else pltpu.VMEM(*item)
            for item in scratch
        ]
        + [dma((4,))]
        + [dma] * 14
        + [dma] * 4
        + [dma((2,))] * 2
        + [dma((4,)), dma((4, 2))]
        + [dma((4,))] * 4,
        compiler_params=params(cid, 62),
    )(inv, posn, msg, x, ownp, logw, logwt, srcf, tfeats)


def shards(
    source_points, target_points, source_logw, target_logw,
    source_feats, target_feats, pair_owner, pair_slot,
):
    n = lax.axis_size("blk")
    owners = pair_owner.T.reshape(56)
    slots = pair_slot.T.reshape(56)
    ids = (slots // 8) * (8 * n) + owners * 8 + slots % 8
    earlier = jnp.tril(jnp.ones((56, 56), bool), -1) & (owners[:, None] == owners[None, :])
    posn = owners * 2 + jnp.sum(earlier.astype(jnp.int32), axis=1)
    order = jnp.arange(56, dtype=jnp.int32)
    row_of = (order % 8) * 8 + order // 8 + 1
    at = posn[None, :] == jnp.arange(2 * n, dtype=jnp.int32)[:, None]
    inv = jnp.min(jnp.where(at, row_of[None, :], 64), axis=1)
    asked = jnp.min(jnp.where(at, slots[None, :], 32), axis=1).reshape(n, 2)
    msg = jnp.concatenate(
        [jnp.broadcast_to(ids[None], (n, 56)), asked, jnp.zeros((n, 70), jnp.int32)], axis=1
    ).reshape(n, 1, 128)
    return whole(
        inv, posn, msg, source_points.T, target_points.T, source_logw.reshape(16, 128),
        target_logw.reshape(64, 128), source_feats, target_feats, 0,
    )


def solution(mesh):
    return jax.shard_map(
        shards,
        mesh=mesh,
        in_specs=(
            P(("blk", "grp"), None),
            P("blk", None),
            P(("blk", "grp")),
            P("blk"),
            P(("blk", "grp"), None),
            P("blk", None),
            P(("blk", "grp"), None),
            P(("blk", "grp"), None),
        ),
        out_specs=(P(("blk", "grp"), None), P(("blk", "grp"), None)),
        check_vma=False,
    )
```

```python
import functools
import jax
import jax.numpy as jnp
from jax import lax
from jax.experimental import pallas as pl
from jax.experimental.pallas import tpu as pltpu
from jax.sharding import PartitionSpec as P

LOWEST = -1e30
CROSS = 0.3125
SQUARE = 0.15625
MESH = pl.DeviceIdType.MESH
MIB = 2**20
SCHEDULE = ((3, 10, 8), (3, 10, 8))
f32 = jnp.float32
bf16 = jnp.bfloat16


def params(cid=None, vmem=48):
    if cid is None:
        return pltpu.CompilerParams(vmem_limit_bytes=vmem * MIB)
    return pltpu.CompilerParams(
        collective_id=cid, has_side_effects=True, vmem_limit_bytes=vmem * MIB
    )


def nt(a, b):
    return lax.dot_general(a, b, (((1,), (1,)), ((), ())), preferred_element_type=f32)


def tn(a, b):
    return lax.dot_general(a, b, (((0,), (0,)), ((), ())), preferred_element_type=f32)


def nn(a, b):
    return jnp.dot(a, b, preferred_element_type=f32)


def greet_signal(axes):
    bar = pltpu.get_barrier_semaphore()
    for name in axes:
        n = lax.axis_size(name)
        me = lax.axis_index(name)

        @pl.loop(1, n)
        def _(s):
            pl.semaphore_signal(
                bar, inc=1, device_id={name: lax.rem(me + s, n)}, device_id_type=MESH
            )


def greet_wait(axes):
    total = sum(lax.axis_size(name) - 1 for name in axes)
    pl.semaphore_wait(pltpu.get_barrier_semaphore(), total)


def remote(src, dst, send, recv, axis, to):
    return pltpu.make_async_remote_copy(
        src_ref=src,
        dst_ref=dst,
        send_sem=send,
        recv_sem=recv,
        device_id={axis: to},
        device_id_type=MESH,
    )


def send_all(src, dst, send, recv, axis):
    n = lax.axis_size(axis)
    me = lax.axis_index(axis)

    @pl.loop(1, n)
    def _(s):
        to = lax.rem(me + s, n)
        remote(src(to), dst, send, recv, axis, to).start()


def messages(ref, count, send, recv, axis):
    part = ref.at[pl.ds(0, count)]
    n = lax.axis_size(axis)
    return remote(part, part, send, recv, axis, lax.rem(lax.axis_index(axis) + 1, n))


def wait_all(ref, send, recv, axis):
    every = messages(ref, lax.axis_size(axis) - 1, send, recv, axis)
    every.wait_send()
    every.wait_recv()


def away(m):
    place = lax.rem(m, 8)
    return 8 * (2 * lax.rem(place, 4) + place // 4) + m // 8


def holder(m, me):
    z, yc = me // 8, lax.rem(me, 8)
    return 8 * lax.rem(z + 8 + along(m, yc), 8) + lax.rem(yc + m // 4, 8)


def sender(m, me):
    z, yc = me // 8, lax.rem(lax.rem(me, 8) + 8 - m // 4, 8)
    return 8 * lax.rem(z + 8 - along(m, yc), 8) + yc


def along(m, yc):
    turn = lax.rem(m, 4)
    two = (turn // 2) * (1 - turn // 3)
    return turn - 4 * (turn // 3) - 4 * two * lax.rem(yc, 2)


def stripe(device):
    return 8 * lax.rem(device // 8, 4) + lax.rem(device, 8)


def message(s):
    z = s // 8
    return 8 * lax.rem(s, 8) + z // 2 + 4 * lax.rem(z, 2)


def squares_row(t):
    wide = t.astype(f32)
    square = wide * wide
    high = square.astype(bf16)
    low = (square - high.astype(f32)).astype(bf16)
    ones = jnp.ones((8, t.shape[1]), bf16)
    return SQUARE * (nt(ones, high) + nt(ones, low))[0:1]


def whole_kernel(
    inv, posn, msg_ref, x_hbm, ownp_hbm, logw_ref, logwt_ref, srcf_hbm, tfeats_hbm,
    moved_ref, out_ref,
    turned_x, turned_own, logwt, x_ref, own_ref, srcf_ref, ownf_ref, stripe_p, stripe_f, logw_col, alpha_ref,
    ids_all, ids_sel, ids_wide, ids_lane, asked, table_p, table_f, halves_p, halves_f, out_p, in_p,
    far_ref, packed_ref, got_ref, scores, beta_ref, lse_ref,
    padded, out1, in1, own, upper, outx, inx, both, out2, in2, out3, in3,
    farf, wide, diag, out_h, in_h, pieces, total, out_x, in_x, out_f, in_f,
    local, send_i, recv_i, send_p, recv_p, send_t, recv_t, send_f, recv_f,
    send1, recv1, send3, recv3, send_s, recv_s,
    sendx_p, recvx_p, sendx_f, recvx_f, send2, recv2,
    send_m, recv_m, send_x, recv_x, send_o, recv_o,
):
    n = lax.axis_size("blk")
    me = lax.axis_index("blk")
    plane = lax.axis_index("grp")
    pairs, block = beta_ref.shape
    rows = pairs // 8
    held = own.shape[0]
    planes = table_p.shape[0]
    mine = pl.ds(pl.multiple_of(plane * 2048, 2048), 2048)
    copies = [
        pltpu.make_async_copy(src, dst, local.at[i])
        for i, (src, dst) in enumerate(
            [
                (ownp_hbm.at[:, mine], turned_own),
                (tfeats_hbm.at[mine], ownf_ref),
                (x_hbm, turned_x),
                (srcf_hbm, srcf_ref),
            ]
        )
    ]
    for copy in copies:
        copy.start()
    greet_signal(["blk", "grp"])

    copies[0].wait()
    for i in range(0, 2048, 256):
        own_ref[i : i + 256, :] = jnp.transpose(turned_own[:, i : i + 256].astype(f32)).astype(bf16)
    for s in range(8):
        for h in range(2):
            at = 256 * s + 128 * h
            pair = [own_ref[at + 64 * c : at + 64 * c + 64, :].astype(f32) for c in range(2)]
            wide[0, pl.ds(h * 8 + s, n, stride=16), :] = jnp.concatenate(pair, axis=1)
    stripe_p[...] = wide[0].reshape(n, 16, 128).astype(bf16)
    copies[1].wait()
    for c in range(2):
        for s in range(8):
            for h in range(2):
                at = 256 * s + 128 * h + 64 * c
                wide[1 + c, pl.ds(h * 8 + s, n, stride=16), :] = ownf_ref[at : at + 64, :].astype(f32)
        stripe_f[:, :, 128 * c : 128 * c + 128] = wide[1 + c].reshape(n, 16, 128).astype(bf16)
    greet_wait(["blk", "grp"])

    @pl.loop(1, n)
    def _(s):
        to = lax.rem(me + s, n)
        remote(stripe_p.at[to], table_p.at[plane, me], send_p, recv_p, "blk", to).start()
        remote(msg_ref.at[to], ids_all.at[message(s)], send_i, recv_i, "blk", to).start()

    @pl.loop(1, n)
    def _(s):
        to = lax.rem(me + s, n)
        remote(stripe_f.at[to], table_f.at[plane, me], send_s, recv_s, "blk", to).start()

    ids_all[0] = msg_ref[me]
    table_p[plane, me] = stripe_p[me]
    table_f[plane, me] = stripe_f[me]
    turned = jnp.transpose(logw_ref[...])
    for i in range(16):
        logw_col[128 * i : 128 * (i + 1), :] = turned[:, i : i + 1]
    for i in range(2):
        logwt[:, 128 * i : 128 * (i + 1)] = logwt_ref[pl.ds(i, held, stride=2), :]
    padded[pl.ds(pairs, 8), :] = jnp.full((8, block), LOWEST, f32)
    copies[2].wait()
    for i in range(0, 2048, 256):
        x_ref[i : i + 256, :] = jnp.transpose(turned_x[:, i : i + 256].astype(f32)).astype(bf16)
    copies[3].wait()
    wait_all(stripe_p, send_p, recv_p, "blk")
    send_all(lambda to: table_p.at[plane], table_p.at[plane], sendx_p, recvx_p, "grp")
    wait_all(ids_all, send_i, recv_i, "blk")
    scalars = pltpu.make_async_copy(ids_all, asked, local.at[0])
    scalars.start()
    ids = ids_all[...].reshape(n, 128).astype(f32)
    turned = jnp.transpose(ids)
    for m in range(n):
        ids_wide[m] = jnp.broadcast_to(turned[0:56, m : m + 1], (56, 128))
    spot = lax.broadcasted_iota(jnp.int32, (16, 128), 1) // 8
    row = lax.broadcasted_iota(jnp.int32, (16, 128), 0)

    @pl.loop(0, n // 2)
    def _(m):
        ids_sel[m] = ids_all[message(lax.rem(me + n - sender(m, me), n))]

    for group in range(2):
        some = ids_sel[16 * group : 16 * group + 16].reshape(16, 128).astype(f32)
        for k in range(7):
            moved = pltpu.roll(some, (128 - 8 * k) % 128, 1)
            moved = pltpu.roll(moved, 0, 1, stride=8, stride_axis=0)
            ids_lane[group, :, 128 * k : 128 * k + 128] = jnp.sum(
                jnp.where(spot == row, moved, 0.0), axis=0, keepdims=True
            ).astype(jnp.int32)
    scalars.wait()
    wait_all(stripe_f, send_s, recv_s, "blk")
    send_all(lambda to: table_f.at[plane], table_f.at[plane], sendx_f, recvx_f, "grp")

    def halve(table, halves):
        width = halves.shape[2]

        @pl.loop(0, planes)
        def _(p):
            for start in range(0, n, 16):
                piece = table[p, pl.ds(start, 16)].astype(f32)
                for h in range(2):
                    at = pl.ds(p * (8 * n) + start * 8, 128)
                    halves[h, at, :] = piece[:, 8 * h : 8 * h + 8].reshape(128, width).astype(bf16)

    def pack(halves, out, then):
        width = halves.shape[2]

        @pl.loop(0, n // 4)
        def _(g):
            ids = ids_wide[pl.ds(4 * g, 4)].reshape(224, 128)[:, 0:1]
            index = lax.broadcasted_iota(jnp.int32, (224, halves.shape[1]), 1)
            hot = (index == ids.astype(jnp.int32)).astype(f32).astype(bf16)
            low = nn(hot, halves[0])
            high = nn(hot, halves[1])
            for d in range(4):
                for k in range(7):
                    at = (d * 7 + k) * 8
                    two = jnp.concatenate([low[at : at + 8], high[at : at + 8]], axis=0)
                    out[4 * g + d, :, k * width : (k + 1) * width] = two.astype(bf16)
                then(4 * g + d)

    def send_points(m):
        @pl.when(m > 0)
        def _():
            to = lax.rem(me + n - away(m), n)
            remote(out_p.at[m], in_p.at[me], send_t, recv_t, "blk", to).start()

    wait_all(table_p, sendx_p, recvx_p, "grp")
    halve(table_p, halves_p)
    pack(halves_p, out_p, send_points)
    in_p[me] = out_p[0]
    wait_all(table_f, sendx_f, recvx_f, "grp")
    halve(table_f, halves_f)
    pack(halves_f, packed_ref, lambda m: None)
    got_ref[me] = packed_ref[0]
    wait_all(in_p, send_t, recv_t, "blk")
    for k in range(7):
        wide[k] = in_p[:, :, 128 * k : 128 * (k + 1)].astype(f32).reshape(n * 16, 128)
        for r in range(8):
            for h in range(2):
                got = wide[k, pl.ds(h * 8 + r, n, stride=16), :].astype(bf16)
                far_ref[r, k, 2 * h * 64 : (2 * h + 1) * 64, :] = got[:, 0:64]
                far_ref[r, k, (2 * h + 1) * 64 : (2 * h + 2) * 64, :] = got[:, 64:128]

    def bulk(first, count):
        @pl.loop(0, count)
        def _(j):
            m = first + j

            @pl.when(m > 0)
            def _():
                to = lax.rem(me + n - away(m), n)
                remote(packed_ref.at[m], got_ref.at[me], send_f, recv_f, "blk", to).start()

    def compute(first, start, count):
        @pl.loop(0, rows)
        def _(r):
            @pl.when(lax.rem(r, 2) == 0)
            def _():
                bulk(start + (r // 2) * count, count)

            at = pl.ds(pl.multiple_of(r * block, block), block)
            x = x_ref[at, :]
            top = None
            for k in range(8):
                t = own_ref[at, :] if k == 0 else far_ref[r, k - 1]
                bias = -squares_row(t) if first else beta_ref[pl.ds(8 * r + k, 1), :]
                z = nt(x, t) * CROSS + bias
                scores[k] = z
                top = z if top is None else jnp.maximum(top, z)
            peak = jnp.max(top, axis=1, keepdims=True)
            weight = None
            for k in range(8):
                e = jnp.exp(scores[k] - peak)
                weight = e if weight is None else weight + e
            alpha = logw_col[at, :] - peak - jnp.log(jnp.sum(weight, axis=1, keepdims=True))
            alpha_ref[at, :] = alpha
            for k in range(8):
                t = own_ref[at, :] if k == 0 else far_ref[r, k - 1]
                v = nt(x, t) * CROSS + alpha
                top = jnp.max(v, axis=0, keepdims=True)
                padded[pl.ds(8 * r + k, 1), :] = top + jnp.log(
                    jnp.sum(jnp.exp(v - top), axis=0, keepdims=True)
                )

    def potentials(turn, start, counts):
        answer, answers = (out3, in3) if turn == 0 else (out2, in2)

        @pl.loop(0, n)
        def _(s):
            to = lax.rem(me + s, n)
            out1[to, 0:1, :] = padded[pl.ds(inv[2 * to], 1), :]
            out1[to, 1:2, :] = padded[pl.ds(inv[2 * to + 1], 1), :]

            @pl.when(s > 0)
            def _():
                remote(out1.at[to], in1.at[message(s)], send1, recv1, "blk", to).start()

        bulk(start, counts[0])
        in1[0] = out1[me]
        own[...] = jnp.full(own.shape, LOWEST, f32)
        for r in range(rows):
            own[pl.ds(plane * rows + r, 1), :] = padded[pl.ds(8 * r, 1), :]
        wait_all(in1, send1, recv1, "blk")
        index = lax.broadcasted_iota(jnp.int32, own.shape, 0)

        def highest(m, best):
            for c in range(2):
                value = in1[m, c : c + 1, :]
                best = jnp.maximum(best, jnp.where(index == asked[m, 0, 56 + c], value, LOWEST))
            return best

        upper[pl.ds(0, held), :] = lax.fori_loop(0, n, highest, own[...])
        upper[pl.ds(held, 8), :] = jnp.zeros((8, block), f32)

        def add(m, so_far):
            for c in range(2):
                slot = asked[m, 0, 56 + c]
                value = jnp.exp(in1[m, c : c + 1, :] - upper[pl.ds(slot, 1), :])
                so_far = so_far + jnp.where(index == slot, value, 0.0)
            return so_far

        top = upper[pl.ds(0, held), :]
        first = jnp.where(own[...] > 0.5 * LOWEST, jnp.exp(own[...] - top), 0.0)
        summed = lax.fori_loop(0, n, add, first)
        part = jnp.where(summed > 0.0, top + jnp.log(jnp.where(summed > 0.0, summed, 1.0)), LOWEST)
        outx[...] = part
        here = inx.at[turn]
        here[plane] = part
        send_all(lambda to: outx, here.at[plane], send2.at[turn], recv2.at[turn], "grp")
        wait_all(here, send2.at[turn], recv2.at[turn], "grp")
        top = inx[turn, 0]
        for p in range(1, planes):
            top = jnp.maximum(top, inx[turn, p])
        summed = jnp.exp(inx[turn, 0] - top)
        for p in range(1, planes):
            summed = summed + jnp.exp(inx[turn, p] - top)
        lse = top + jnp.log(summed)
        both[0, pl.ds(0, held), :] = logwt[...] - lse
        both[1, pl.ds(0, held), :] = lse
        both[:, pl.ds(held, 8), :] = jnp.zeros((2, 8, block), f32)

        @pl.loop(0, n)
        def _(m):
            for c in range(2):
                slot = asked[m, 0, 56 + c]
                answer[m, c : c + 1, :] = both[0, pl.ds(slot, 1), :]
                if turn == 1:
                    answer[m, c + 2 : c + 3, :] = both[1, pl.ds(slot, 1), :]

            @pl.when(m > 0)
            def _():
                to = lax.rem(me + n - away(m), n)
                remote(answer.at[m], answers.at[me], send3, recv3, "blk", to).start()

        bulk(start + counts[0], counts[1])
        answers[me] = answer[0]
        wait_all(answers, send3, recv3, "blk")
        for r in range(rows):
            beta_ref[8 * r : 8 * r + 1, :] = both[0, pl.ds(plane * rows + r, 1), :]
            lse_ref[8 * r : 8 * r + 1, :] = both[1, pl.ds(plane * rows + r, 1), :]
            for k in range(7):
                where = posn[8 * k + r]
                owner = where // 2
                rank = where % 2
                row = 8 * r + k + 1
                beta_ref[row : row + 1, :] = answers[owner, pl.ds(rank, 1), :]
                if turn == 1:
                    lse_ref[row : row + 1, :] = answers[owner, pl.ds(rank + 2, 1), :]

    sent = 0
    for turn in range(2):
        per_two, after_ask, after_answer = SCHEDULE[turn]
        compute(turn == 0, sent, per_two)
        sent += 4 * per_two
        potentials(turn, sent, (after_ask, after_answer))
        sent += after_ask + after_answer

    few = n // 2

    def parts(h):
        @pl.loop(0, rows)
        def _(r):
            at = pl.ds(pl.multiple_of(r * block, block), block)
            x = x_ref[at, :]
            alpha = alpha_ref[at, :]
            srcf = srcf_ref[at, :]
            half = pl.ds(pl.multiple_of(r * 256 + 128 * h, 128), 128)
            for k in range(8):
                t = own_ref[half, :] if k == 0 else far_ref[r, k - 1, 128 * h : 128 * h + 128, :]
                shift = lse_ref[pl.ds(8 * r + k, 1), :][:, 128 * h : 128 * h + 128]
                w = jnp.exp(nt(x, t) * CROSS + alpha - shift).astype(bf16)
                part = tn(w, srcf).astype(bf16).astype(f32)
                if k == 0:
                    diag[half, :] = part
                else:
                    for d in range(2):
                        for c in range(2):
                            at = 64 * d + 32 * c
                            to = pl.ds(512 * d + 8 * c + r, few, stride=16)
                            wide[k - 1, to, :] = part[at : at + 32]

        for k in range(7):
            for d in range(2):
                lanes = 128 * k
                value = wide[k, 512 * d : 512 * (d + 1), :].reshape(few, 16, 128)
                out_h[2 * h + d, :, :, lanes : lanes + 128] = value.astype(bf16)
        for q in (2 * h, 2 * h + 1):

            @pl.loop(1, few)
            def _(m):
                to = holder(m, me)
                remote(
                    out_h.at[q, stripe(to)],
                    in_h.at[q, m],
                    send_m.at[q],
                    recv_m.at[q, m // 16],
                    "blk",
                    to,
                ).start()

            in_h[q, 0] = out_h[q, stripe(me)]

    def move_rows():
        wait_all(got_ref, send_f, recv_f, "blk")
        for k in range(7):
            for c in range(2):
                lanes = 128 * (2 * k + c)
                buffer = (2 * k + c) % 7
                wide[buffer] = got_ref[:, :, lanes : lanes + 128].astype(f32).reshape(16 * n, 128)
                for r in range(8):
                    for h in range(2):
                        got = wide[buffer, pl.ds(h * 8 + r, n, stride=16), :]
                        farf[r, k, 64 * (2 * h + c) : 64 * (2 * h + c + 1), :] = got.astype(bf16)

        @pl.loop(0, rows)
        def _(r):
            at = pl.ds(pl.multiple_of(r * block, block), block)
            x = x_ref[at, :]
            top = None
            for k in range(8):
                t = own_ref[at, :] if k == 0 else far_ref[r, k - 1]
                z = nt(x, t) * CROSS + beta_ref[pl.ds(8 * r + k, 1), :]
                scores[k] = z
                top = z if top is None else jnp.maximum(top, z)
            peak = jnp.max(top, axis=1, keepdims=True)
            weight = None
            mixed = None
            for k in range(8):
                e = jnp.exp(scores[k] - peak)
                weight = e if weight is None else weight + e
                feats = ownf_ref[at, :] if k == 0 else farf[r, k - 1]
                term = nn(e.astype(bf16), feats)
                mixed = term if mixed is None else mixed + term
            moved_ref[at, :] = (mixed / jnp.sum(weight, axis=1, keepdims=True)).astype(bf16)

    def collect(q):
        for group in range(2):
            count = 16 - (1 if group == 0 else 0)
            messages(in_h.at[q], count, send_m.at[q], recv_m.at[q, group], "blk").wait_recv()

            @pl.loop(0, 8)
            def _(pair):
                one = in_h[q, 16 * group + 2 * pair].astype(f32)
                two = in_h[q, 16 * group + 2 * pair + 1].astype(f32)
                for k in range(7):
                    for c in range(2):
                        lanes = slice(128 * k, 128 * (k + 1))
                        joined = jnp.concatenate(
                            [one[8 * c : 8 * c + 8, lanes], two[8 * c : 8 * c + 8, lanes]], axis=0
                        )
                        at = pl.ds(pl.multiple_of(128 * k + 16 * pair, 16), 16)
                        pieces[at, 128 * c : 128 * (c + 1)] = joined.astype(bf16)

            @pl.loop(0, 8)
            def _(i):
                at = pl.ds(pl.multiple_of(256 * i, 256), 256)
                index = lax.broadcasted_iota(jnp.int32, (256, 896), 0) + 256 * i
                hot = (index == ids_lane[group]).astype(f32).astype(bf16)
                term = nn(hot, pieces[...])
                if group == 0:
                    total[at, :] = term
                else:
                    total[at, :] += term

    def spread(q):
        out = out_x.at[q % 2]
        for p in range(planes):
            out[p] = total[512 * p : 512 * (p + 1), :].astype(bf16)
        in_x[q, plane] = out[plane]
        send_all(lambda to: out.at[to], in_x.at[q, plane], send_x.at[q], recv_x.at[q], "grp")

    def finish(q):
        wait_all(in_x.at[q], send_x.at[q], recv_x.at[q], "grp")
        added = in_x[q, 0].astype(f32)
        for p in range(1, planes):
            added = added + in_x[q, p].astype(f32)
        joined = jnp.concatenate(
            [added[:, 128 * c : 128 * (c + 1)].reshape(n, 8, 128) for c in range(2)], axis=1
        )
        out_f[q] = joined.astype(bf16)
        send_all(lambda to: out_f.at[q, to], in_f.at[q, me], send_o.at[q], recv_o.at[q], "blk")
        in_f[q, me] = out_f[q, me]

    def deliver(q):
        wait_all(in_f.at[q], send_o.at[q], recv_o.at[q], "blk")
        added = in_f[q, 0:few].astype(f32) + in_f[q, few:n].astype(f32)
        wide[q, 0:512, :] = added.reshape(16 * few, 128)
        for s in range(8):
            for c in range(2):
                at = 256 * s + 64 * q + 32 * c
                got = wide[q, pl.ds(8 * c + s, few, stride=16), :]
                out_ref[at : at + 32, :] = (got + diag[at : at + 32, :]).astype(bf16)

    parts(0)
    parts(1)
    bulk(sent, n - sent)
    collect(0)
    spread(0)
    collect(1)
    spread(1)
    finish(0)
    collect(2)
    spread(2)
    finish(1)
    collect(3)
    spread(3)
    move_rows()
    finish(2)
    finish(3)
    for q in range(4):
        deliver(q)
    for q in range(4):
        messages(out_h.at[q], few - 1, send_m.at[q], recv_m.at[q, 0], "blk").wait_send()


def whole(inv, posn, msg, x, ownp, logw, logwt, srcf, tfeats, cid):
    n = lax.axis_size("blk")
    planes = lax.axis_size("grp")
    pairs, block = 64, 256
    held = 32
    smem = pl.BlockSpec(memory_space=pltpu.SMEM)
    vmem = pl.BlockSpec(memory_space=pltpu.VMEM)
    hbm = pl.BlockSpec(memory_space=pl.ANY)
    scratch = [
        ((64, 2048), bf16),
        ((64, 2048), bf16),
        ((held, block), f32),
        ((2048, 64), bf16),
        ((2048, 64), bf16),
        ((2048, 128), bf16),
        ((2048, 128), bf16),
        ((n, 16, 128), bf16),
        ((n, 16, 256), bf16),
        ((2048, 1), f32),
        ((2048, 1), f32),
        ((n, 1, 128), jnp.int32),
        ((n // 2, 1, 128), jnp.int32),
        ((n, 56, 128), f32),
        ((2, 1, 896), jnp.int32),
        None,
        ((planes, n, 16, 128), bf16),
        ((planes, n, 16, 256), bf16),
        ((2, planes * 8 * n, 128), bf16),
        ((2, planes * 8 * n, 256), bf16),
        ((n, 16, 7 * 128), bf16),
        ((n, 16, 7 * 128), bf16),
        ((8, 7, 256, 64), bf16),
        ((n, 16, 7 * 256), bf16),
        ((n, 16, 7 * 256), bf16),
        ((8, block, block), f32),
        ((pairs, block), f32),
        ((pairs, block), f32),
        ((pairs + 8, block), f32),
        ((n, 2, block), f32),
        ((n, 2, block), f32),
        ((held, block), f32),
        ((held + 8, block), f32),
        ((held, block), f32),
        ((2, planes, held, block), f32),
        ((2, held + 8, block), f32),
        ((n, 4, block), f32),
        ((n, 4, block), f32),
        ((n, 2, block), f32),
        ((n, 2, block), f32),
        ((8, 7, 256, 128), bf16),
        ((7, 16 * n, 128), f32),
        ((2048, 128), f32),
        ((4, n // 2, 16, 896), bf16),
        ((4, n // 2, 16, 896), bf16),
        ((896, 256), bf16),
        ((planes * 8 * n, 256), f32),
        ((2, planes, 8 * n, 256), bf16),
        ((4, planes, 8 * n, 256), bf16),
        ((4, n, 16, 128), bf16),
        ((4, n, 16, 128), bf16),
    ]
    dma = pltpu.SemaphoreType.DMA
    return pl.pallas_call(
        whole_kernel,
        out_shape=(
            jax.ShapeDtypeStruct((2048, 128), bf16),
            jax.ShapeDtypeStruct((2048, 128), bf16),
        ),
        in_specs=[smem, smem, vmem, hbm, hbm, vmem, vmem, hbm, hbm],
        out_specs=(vmem,) * 2,
        scratch_shapes=[
            pltpu.SMEM((n, 1, 128), jnp.int32) if item is None else pltpu.VMEM(*item)
            for item in scratch
        ]
        + [dma((4,))]
        + [dma] * 14
        + [dma] * 4
        + [dma((2,))] * 2
        + [dma((4,)), dma((4, 2))]
        + [dma((4,))] * 4,
        compiler_params=params(cid, 62),
    )(inv, posn, msg, x, ownp, logw, logwt, srcf, tfeats)


def shards(
    source_points, target_points, source_logw, target_logw,
    source_feats, target_feats, pair_owner, pair_slot,
):
    n = lax.axis_size("blk")
    owners = pair_owner.T.reshape(56)
    slots = pair_slot.T.reshape(56)
    ids = (slots // 8) * (8 * n) + owners * 8 + slots % 8
    earlier = jnp.tril(jnp.ones((56, 56), bool), -1) & (owners[:, None] == owners[None, :])
    posn = owners * 2 + jnp.sum(earlier.astype(jnp.int32), axis=1)
    order = jnp.arange(56, dtype=jnp.int32)
    row_of = (order % 8) * 8 + order // 8 + 1
    at = posn[None, :] == jnp.arange(2 * n, dtype=jnp.int32)[:, None]
    inv = jnp.min(jnp.where(at, row_of[None, :], 64), axis=1)
    asked = jnp.min(jnp.where(at, slots[None, :], 32), axis=1).reshape(n, 2)
    msg = jnp.concatenate(
        [jnp.broadcast_to(ids[None], (n, 56)), asked, jnp.zeros((n, 70), jnp.int32)], axis=1
    ).reshape(n, 1, 128)
    return whole(
        inv, posn, msg, source_points.T, target_points.T, source_logw.reshape(16, 128),
        target_logw.reshape(64, 128), source_feats, target_feats, 0,
    )


def solution(mesh):
    return jax.shard_map(
        shards,
        mesh=mesh,
        in_specs=(
            P(("blk", "grp"), None),
            P("blk", None),
            P(("blk", "grp")),
            P("blk"),
            P(("blk", "grp"), None),
            P("blk", None),
            P(("blk", "grp"), None),
            P(("blk", "grp"), None),
        ),
        out_specs=(P(("blk", "grp"), None), P(("blk", "grp"), None)),
        check_vma=False,
    )
```
